128 devices in a mesh: gx: 8 (over z, core), gy: 16 (over x, y).
Axes of the slice: x: 4, y: 4, z: 4, core: 2. Of those that a mesh axis runs over, the one named last changes fastest.
Arguments:
- right_side: float32 [64, 64, 2048], P(None, 'gx', 'gy'), may hold values from -4 to 10
- terrain: int32 [64, 64, 2048], P(None, 'gx', 'gy'), may hold values from 0 to 1, as said below
Outputs:
- pressure: float32 [64, 64, 2048], P(None, 'gx', 'gy')
The draws below stay inside these ranges and needn't reach their ends.
Inputs may be any that keep to these rules, and one draw needn't show every extreme that they name: 1 marks a terrain cell; in every vertical column the terrain cells are the lowest ones, from none up to 32 of them.
All inputs are finite; a program needn't handle non-finite values.
Results may differ from the reference program's by a relative error of at most 0.0001.
Values sent between devices are 32-bit elements; how exact they have to be, the bound alone decides.
No kernel may reach another device: no remote copies, remote signals or barrier semaphores. Data moves between devices by JAX's collectives and lax.ppermute only.
A program may use at most 128 MiB of HBM per device.

```python
import math
import jax
import jax.numpy as jnp
from jax import lax

LAYERS = 64
SWEEPS = 4
LEVELS = 3
COARSE_SWEEPS = 8
CYCLES = 2
GRID_X = 64
GRID_Y = 2048


def smooth_field(key, amplitude):
    phase_key = jax.random.fold_in(key, 0)
    phases = jax.random.uniform(phase_key, (2,), jnp.float32, 0.0, 2.0 * math.pi)
    row_pos = jnp.arange(GRID_X, dtype=jnp.float32) / GRID_X
    col_pos = jnp.arange(GRID_Y, dtype=jnp.float32) / GRID_Y
    layer_pos = (jnp.arange(LAYERS, dtype=jnp.float32) + 0.5) / LAYERS
    row_part = 1.0 + 0.5 * jnp.sin(2.0 * math.pi * row_pos + phases[0])
    col_part = 1.0 + 0.5 * jnp.sin(4.0 * math.pi * col_pos + phases[1])
    layer_part = 0.6 + 0.4 * jnp.sin(math.pi * layer_pos)
    return amplitude * layer_part[:, None, None] * row_part[None, :, None] * col_part[None, None, :]


def draw_right_side(key, part):
    key = jax.random.fold_in(key, 11)
    smooth_key, noise_key = jax.random.split(key)
    noise = jnp.clip(jax.random.normal(noise_key, (LAYERS, GRID_X, GRID_Y), jnp.float32), -3.5, 3.5)
    values = smooth_field(smooth_key, 1.5) + noise
    return values.astype(jnp.float32)


def draw_terrain(key, part):
    key = jax.random.fold_in(key, 7)
    first_key, second_key = jax.random.split(key)
    ridge = jax.random.randint(first_key, (1, GRID_X, GRID_Y), 0, LAYERS // 4 + 1)
    ripple = jax.random.randint(second_key, (1, GRID_X, GRID_Y), 0, LAYERS // 4 + 1)
    height = ridge + ripple
    layer_index = jnp.arange(LAYERS, dtype=jnp.int32)[:, None, None]
    return (layer_index < height).astype(jnp.int32)


def setup_inputs(seed: int = 0) -> dict:
    streams_of = jax.random.split(jax.random.key(seed), 3)
    right_side = draw_right_side(jax.random.fold_in(streams_of[2], 71), 0)
    terrain = draw_terrain(jax.random.fold_in(streams_of[2], 71), 0)
    return {"right_side": right_side, "terrain": terrain}


RELAX_WEIGHT = 0.8
TERRAIN_PENALTY = 0.05


def neighbors(padded):
    centre = padded[:, 1:-1, 1:-1]
    vertical = jnp.pad(centre, ((1, 1), (0, 0), (0, 0)))
    neighbor_sum = vertical[2:] + vertical[:-2]
    neighbor_sum = neighbor_sum + padded[:, 2:, 1:-1] + padded[:, :-2, 1:-1]
    neighbor_sum = neighbor_sum + padded[:, 1:-1, 2:] + padded[:, 1:-1, :-2]
    return neighbor_sum, centre


def relax_once(padded, source, shift_now):
    neighbor_sum, centre = neighbors(padded)
    diagonal = 6.0 + shift_now
    return centre + RELAX_WEIGHT * (source - diagonal * centre + neighbor_sum) / diagonal


def defect(padded, source, shift_now):
    neighbor_sum, centre = neighbors(padded)
    return source - (6.0 + shift_now) * centre + neighbor_sum


def first_sweep(source, shift_now):
    return RELAX_WEIGHT * source / (6.0 + shift_now)


def restrict(values):
    layers_here, rows_here, cols_here = values.shape
    blocks = values.reshape(layers_here // 2, 2, rows_here // 2, 2, cols_here // 2, 2)
    return 0.5 * blocks.sum(axis=(1, 3, 5))


def prolong(values):
    layers_here, rows_here, cols_here = values.shape
    spread = jnp.broadcast_to(values[:, None, :, None, :, None], (layers_here, 2, rows_here, 2, cols_here, 2))
    return spread.reshape(2 * layers_here, 2 * rows_here, 2 * cols_here)


def zero_rim(values):
    return jnp.pad(values, ((0, 0), (1, 1), (1, 1)))


def reference(right_side, terrain):
    shift_fine = TERRAIN_PENALTY * terrain.astype(jnp.float32)
    pressure = jnp.zeros_like(right_side)
    for cycle_index in range(CYCLES):
        source, shift_now = right_side, shift_fine
        stored = []
        for level_index in range(LEVELS):
            if level_index == 0 and cycle_index > 0:
                iterate = pressure
                repeats = SWEEPS
            else:
                iterate = first_sweep(source, shift_now)
                repeats = SWEEPS - 1
            for repeat in range(repeats):
                iterate = relax_once(zero_rim(iterate), source, shift_now)
            residual = defect(zero_rim(iterate), source, shift_now)
            stored.append((iterate, source, shift_now))
            source = restrict(residual)
            shift_now = restrict(shift_now)
        coarse_source, coarse_shift = source, shift_now
        correction = first_sweep(coarse_source, coarse_shift)
        correction = lax.fori_loop(0, COARSE_SWEEPS - 1, lambda counter, current: relax_once(zero_rim(current), coarse_source, coarse_shift), correction)
        for level_index in reversed(range(LEVELS)):
            iterate, source, shift_now = stored[level_index]
            iterate = iterate + prolong(correction)
            for repeat in range(SWEEPS):
                iterate = relax_once(zero_rim(iterate), source, shift_now)
            correction = iterate
        pressure = correction
    return pressure
```

```python
import jax
import jax.numpy as jnp
from jax import lax
from jax.experimental import pallas as pl
from jax.experimental.pallas import tpu as pltpu
from jax.sharding import PartitionSpec as P

SWEEPS = 4
COARSE_SWEEPS = 8
RELAX_WEIGHT = 0.8
TERRAIN_PENALTY = 0.05

F32 = jnp.float32
LANES = 128
LAYERS = 64
TILE_ROWS = 8
PAD = 8
WINDOW = 16
VMEM_LIMIT = 56 * 1024 * 1024


D_AIR = 6.0
D_TERRAIN = 6.0 + TERRAIN_PENALTY


def lanes_iota(shape):
    return lax.broadcasted_iota(jnp.int32, shape, len(shape) - 1)


def edge_mask(level, has_left, has_right):
    lane = lanes_iota((1, LANES))
    zero = jnp.zeros((1, LANES), F32)
    left = zero + has_left.astype(F32)
    right = zero + has_right.astype(F32)
    if level == 0:
        return jnp.where(lane < 64, right, left)
    if level == 1:
        return jnp.where(lane < 64, 1.0, jnp.where(lane < 96, right, left))
    if level == 2:
        return jnp.where(
            lane < 32, 1.0, jnp.where(lane < 64, right, jnp.where(lane < 96, 0.0, left))
        )
    return jnp.where(
        lane < 16, 1.0, jnp.where(lane < 32, right, jnp.where(lane < 112, 0.0, left))
    )


def dot(values, matrix):
    return lax.dot_general(
        values, matrix, (((1,), (0,)), ((), ())),
        precision=lax.Precision.HIGHEST, preferred_element_type=F32,
    )


def matrix_of(rule):
    row = lax.broadcasted_iota(jnp.int32, (LANES, LANES), 0)
    col = lax.broadcasted_iota(jnp.int32, (LANES, LANES), 1)
    return rule(row, col)


def half(flag):
    return jnp.where(flag, 0.5, 0.0).astype(F32)


def one(flag):
    return jnp.where(flag, 1.0, 0.0).astype(F32)


def side_sum(parts):
    ahead = [pltpu.roll(x, LANES - 1, axis=x.ndim - 1) for x in parts]
    behind = [pltpu.roll(x, 1, axis=x.ndim - 1) for x in parts]
    if len(parts) == 1:
        return [ahead[0] + behind[0]]
    lane = lanes_iota(parts[0].shape)
    first, last = lane == 0, lane == LANES - 1
    return [
        jnp.where(last, ahead[1 - h], ahead[h]) + jnp.where(first, behind[1 - h], behind[h])
        for h in range(2)
    ]


def at(ref, h, halves, row, layers):
    if halves == 2:
        return ref[h, row, layers, :]
    return ref[row, layers, :]


def put(ref, h, halves, row, layers, value):
    if halves == 2:
        ref[h, row, layers, :] = value
    else:
        ref[row, layers, :] = value


def stencil_pass(src, halves, first_row, rows, base, depth, shift, emit, group, unrolled):
    def layers(offset):
        return pl.ds(shift + (base + offset), depth)

    aligned = pl.ds(PAD + base, depth)

    def rows_at(row):
        return [at(src, h, halves, row, aligned) for h in range(halves)]

    def step(row, before, centre):
        after = rows_at(row + 2)
        sides = side_sum(centre)
        for h in range(halves):
            total = before[h] + after[h]
            total = total + at(src, h, halves, row + 1, layers(-1))
            total = total + at(src, h, halves, row + 1, layers(1))
            emit(row, h, centre[h], total + sides[h])
        return centre, after

    before, centre = rows_at(first_row), rows_at(first_row + 1)
    if unrolled:
        for i in range(rows):
            before, centre = step(first_row + i, before, centre)
        return

    def body(i, carry):
        before, centre = carry
        for k in range(group):
            before, centre = step(first_row + i * group + k, before, centre)
        return before, centre

    lax.fori_loop(0, rows // group, body, (before, centre))


class Fine:
    def __init__(self, source, height, edge, shift):
        self.source, self.height, self.shift = source, height, shift
        self.edge = [jnp.ones((1, LANES), F32), edge]
        self.layer = lax.broadcasted_iota(jnp.int32, (32, LANES), 0).astype(F32)

    def terrain(self, row, h):
        height = self.height[h, row]
        return self.layer < jnp.concatenate([height] * 4, axis=0)

    def weight(self, row, h, chunk):
        air = (RELAX_WEIGHT / D_AIR) * self.edge[h]
        if chunk == 1:
            return air
        ground = (RELAX_WEIGHT / D_TERRAIN) * self.edge[h]
        return jnp.where(self.terrain(row, h), ground, air)

    def first(self, dst, rows):
        def body(row, carry):
            for h in range(2):
                for chunk in range(2):
                    value = self.weight(row, h, chunk) * self.source[h, row, pl.ds(32 * chunk, 32), :]
                    dst[h, row + 1, pl.ds(PAD + 32 * chunk, 32), :] = value
            return carry

        lax.fori_loop(0, rows, body, 0)

    def relax(self, src, dst, first_row, rows):
        for chunk in range(2):
            def emit(row, h, centre, total, chunk=chunk):
                total = total + self.source[h, row, pl.ds(32 * chunk, 32), :]
                value = (1.0 - RELAX_WEIGHT) * centre + self.weight(row, h, chunk) * total
                dst[h, row + 1, pl.ds(PAD + 32 * chunk, 32), :] = value

            stencil_pass(src, 2, first_row, rows, 32 * chunk, 32, self.shift, emit, 2, False)

    def restricted_defect(self, src, spare, rows, out):
        for chunk in range(2):
            held = {}

            def emit(row, h, centre, total, chunk=chunk):
                total = total + self.source[h, row, pl.ds(32 * chunk, 32), :]
                diagonal = D_AIR
                if chunk == 0:
                    diagonal = jnp.where(self.terrain(row, h), D_TERRAIN, D_AIR)
                value = total - diagonal * centre
                if h not in held:
                    held[h] = value
                else:
                    target = lax.div(row, 2) + 1
                    spare[h, target, pl.ds(PAD + 32 * chunk, 32), :] = held.pop(h) + value

            stencil_pass(src, 2, 0, rows, 32 * chunk, 32, self.shift, emit, 2, False)
        pair_layers_and_lanes(spare, rows // 2, out)

    def coarse_shift(self, rows, spare, out):
        base = 2.0 * lax.broadcasted_iota(jnp.int32, (32, LANES), 0).astype(F32)

        def body(row, carry):
            for h in range(2):
                count = jnp.zeros((32, LANES), F32)
                for k in range(2):
                    height = jnp.concatenate([self.height[h, 2 * row + k]] * 4, axis=0)
                    count = count + jnp.clip(height - base, 0.0, 2.0)
                spare[h, row + 1, pl.ds(PAD, 32), :] = TERRAIN_PENALTY * count
            return carry

        lax.fori_loop(0, rows // 2, body, 0)
        lanes_to_level_1(
            lambda h, row: spare[h, row + 1, pl.ds(PAD, 32), :], rows // 2, out
        )


def lanes_to_level_1(part, rows, out):
    into = [
        matrix_of(lambda a, b: half(b == lax.div(a, 2))),
        matrix_of(lambda a, b: half(b == lax.div(a, 2) + 64)),
    ]
    group = 8

    def body(i, carry):
        total = 0.0
        for h in range(2):
            stacked = jnp.concatenate([part(h, i * group + k) for k in range(group)], axis=0)
            total = total + dot(stacked, into[h])
        for k in range(group):
            out[i * group + k] = total[32 * k:32 * (k + 1)]
        return carry

    lax.fori_loop(0, rows // group, body, 0)


def pair_layers_and_lanes(spare, rows, out):
    def part(h, row):
        return (
            spare[h, row + 1, pl.ds(PAD, 32, stride=2), :]
            + spare[h, row + 1, pl.ds(PAD + 1, 32, stride=2), :]
        )

    lanes_to_level_1(part, rows, out)


class Coarse:
    def __init__(self, source, weight, shift_now, rows, layers, shift, unrolled):
        self.source, self.weight, self.shift_now = source, weight, shift_now
        self.rows, self.layers, self.shift = rows, layers, shift
        self.unrolled = unrolled

    def set_weight(self, edge):
        for row in range(self.rows):
            self.weight[row] = edge * (RELAX_WEIGHT / (6.0 + self.shift_now[row]))

    def first(self, dst):
        for row in range(self.rows):
            dst[row + 1, pl.ds(PAD, self.layers), :] = self.weight[row] * self.source[row]

    def relax(self, src, dst):
        def emit(row, h, centre, total):
            value = (1.0 - RELAX_WEIGHT) * centre + self.weight[row] * (total + self.source[row])
            dst[row + 1, pl.ds(PAD, self.layers), :] = value

        stencil_pass(src, 1, 0, self.rows, 0, self.layers, self.shift, emit, 4, self.unrolled)

    def defect_pairs(self, src, spare):
        held = []

        def emit(row, h, centre, total):
            value = self.source[row] + total - (6.0 + self.shift_now[row]) * centre
            if not held:
                held.append(value)
            else:
                spare[lax.div(row, 2) + 1 if not isinstance(row, int) else row // 2 + 1,
                      pl.ds(PAD, self.layers), :] = held.pop() + value

        stencil_pass(src, 1, 0, self.rows, 0, self.layers, self.shift, emit, 4, self.unrolled)

    def pairs_of(self, spare, row):
        count = self.layers // 2
        return (
            spare[row + 1, pl.ds(PAD, count, stride=2), :]
            + spare[row + 1, pl.ds(PAD + 1, count, stride=2), :]
        )

    def shift_pairs(self, spare):
        for row in range(self.rows // 2):
            spare[row + 1, pl.ds(PAD, self.layers), :] = (
                self.shift_now[2 * row] + self.shift_now[2 * row + 1]
            )


def pack_level_2(level, spare, out, offset):
    each = level.rows // 8
    for_out = 0.0
    for g in range(4):
        into = matrix_of(lambda a, b: half((a < 64) & (b == lax.div(a, 2) + 32 * g)))
        stacked = jnp.concatenate(
            [level.pairs_of(spare, g * each + k) for k in range(each)], axis=0
        )
        for_out = for_out + dot(stacked, into)
    for k in range(each):
        out[offset + k] = for_out[16 * k:16 * (k + 1)]


def unpack_level_2(own, right, left, offset, each, out):
    lane = lanes_iota((16, LANES))
    for g in range(4):
        for k in range(each):
            parts = []
            for ref, place in ((own, 0), (right, 32), (left, 96)):
                value = ref[offset + k]
                amount = (place - 32 * g) % LANES
                parts.append(pltpu.roll(value, amount, axis=1) if amount else value)
            out[g * each + k] = jnp.where(
                lane < 32, parts[0],
                jnp.where(lane < 64, parts[1], jnp.where(lane < 96, 0.0, parts[2])),
            )


def coarsest(source, diagonal, edge, rows):
    weight = edge * (RELAX_WEIGHT / diagonal)
    layer = lax.broadcasted_iota(jnp.int32, (8, LANES), 0)
    weights = [weight[r] for r in range(rows)]
    sources = [source[r] for r in range(rows)]
    values = tuple(w * b for w, b in zip(weights, sources))

    def body(i, values):
        zero = jnp.zeros((8, LANES), F32)
        new = []
        for r in range(rows):
            v = values[r]
            total = (values[r - 1] if r > 0 else zero) + (values[r + 1] if r < rows - 1 else zero)
            total = total + jnp.where(layer == 0, 0.0, pltpu.roll(v, 1, axis=0))
            total = total + jnp.where(layer == 7, 0.0, pltpu.roll(v, 7, axis=0))
            total = total + side_sum([v])[0]
            new.append((1.0 - RELAX_WEIGHT) * v + weights[r] * (total + sources[r]))
        return tuple(new)

    return lax.fori_loop(0, COARSE_SWEEPS - 1, body, values)


def zero_rim(ref, rows, layers, halves):
    for h in range(halves):
        def body(row, carry):
            zero = jnp.zeros((PAD, LANES), F32)
            put(ref, h, halves, row, pl.ds(0, PAD), zero)
            put(ref, h, halves, row, pl.ds(PAD + layers, PAD), zero)
            return carry

        lax.fori_loop(0, rows + 2, body, 0)
        zero = jnp.zeros((layers, LANES), F32)
        put(ref, h, halves, 0, pl.ds(PAD, layers), zero)
        put(ref, h, halves, rows + 1, pl.ds(PAD, layers), zero)


def add_prolonged(target, source_rows, layers, dup):
    for row, value in source_rows:
        dup[row % 2, pl.ds(0, layers, stride=2), :] = value
        dup[row % 2, pl.ds(1, layers, stride=2), :] = value
        both = dup[row % 2, pl.ds(0, 2 * layers), :]
        for k in range(2):
            place = (2 * row + k + 1, pl.ds(PAD, 2 * layers), slice(None))
            target[place] = target[place] + both


def level_1_down(level, va, vb, spare):
    level.first(va)
    level.relax(va, vb)
    level.relax(vb, va)
    level.relax(va, vb)
    level.defect_pairs(vb, spare)


def coarse_part(own, right, left, own_s, right_s, left_s, s_ref, rows2, refs):
    va, vb, b2, sh2, w2, dup2 = refs
    shift, has_left, has_right = s_ref[0], s_ref[2], s_ref[3]
    each = rows2 // 4
    unpack_level_2(own, right, left, 0, each, b2)
    unpack_level_2(own_s, right_s, left_s, each, each, sh2)
    level = Coarse(b2, w2, sh2, rows2, 16, shift, True)
    level.set_weight(edge_mask(2, has_left, has_right))
    level.first(va)
    level.relax(va, vb)
    level.relax(vb, va)
    level.relax(va, vb)

    into = matrix_of(
        lambda a, b: half(b == jnp.where(a < 64, lax.div(a, 2), 64 + lax.div(a, 2)))
    )
    rows3 = rows2 // 2

    def to_level_3(spare):
        stacked = jnp.concatenate([level.pairs_of(spare, r) for r in range(rows3)], axis=0)
        return dot(stacked, into).reshape(rows3, 8, LANES)

    level.shift_pairs(va)
    shift_3 = to_level_3(va)
    level.defect_pairs(vb, va)
    source_3 = to_level_3(va)
    values = coarsest(source_3, 6.0 + shift_3, edge_mask(3, has_left, has_right), rows3)
    out_of = matrix_of(
        lambda a, b: one(a == jnp.where(b < 64, lax.div(b, 2), 64 + lax.div(b, 2)))
    )
    spread = dot(jnp.concatenate(values, axis=0), out_of)
    add_prolonged(vb, [(r, spread[8 * r:8 * (r + 1)]) for r in range(rows3)], 8, dup2)
    level.relax(vb, va)
    level.relax(va, vb)
    level.relax(vb, va)
    level.relax(va, vb)
    return vb


def level_1_up(level, e2, rows2, va, vb, dup):
    out_of = matrix_of(
        lambda a, b: one(a == jnp.where(b < 96, lax.div(b, 2), 64 + lax.div(b, 2)))
    )
    stacked = jnp.concatenate([e2[r + 1, pl.ds(PAD, 16), :] for r in range(rows2)], axis=0)
    spread = dot(stacked, out_of)
    add_prolonged(va, [(r, spread[16 * r:16 * (r + 1)]) for r in range(rows2)], 16, dup)
    level.relax(va, vb)
    level.relax(vb, va)
    level.relax(va, vb)
    level.relax(vb, va)


def add_to_fine(e1, target, first_pair, pairs, dup):
    out_of = [
        matrix_of(lambda a, b: one(a == lax.div(b, 2))),
        matrix_of(lambda a, b: one(a == lax.div(b, 2) + 64)),
    ]
    group = 4

    def body(i, carry):
        start = first_pair + i * group
        stacked = jnp.concatenate(
            [e1[start + k + 1, pl.ds(PAD, 32), :] for k in range(group)], axis=0
        )
        for h in range(2):
            spread = dot(stacked, out_of[h])
            for k in range(group):
                part = spread[32 * k:32 * (k + 1)]
                dup[h * group + k, pl.ds(0, 32, stride=2), :] = part
                dup[h * group + k, pl.ds(1, 32, stride=2), :] = part
        for h in range(2):
            for k in range(group):
                both = dup[h * group + k]
                for m in range(2):
                    row = 2 * (start + k) + m + 1
                    place = (h, row, pl.ds(PAD, 64), slice(None))
                    target[place] = target[place] + both
        return carry

    lax.fori_loop(0, pairs // group, body, 0)


def interior(ref, rows):
    return ref.at[:, pl.ds(1, rows), pl.ds(PAD, LAYERS), :]


def load_source(gathered, source, height, sems):
    copies = []
    for h in range(2):
        copies.append(pltpu.make_async_copy(
            gathered.at[:, h, pl.ds(0, LAYERS), :], source.at[h], sems.at[h]))
        copies.append(pltpu.make_async_copy(
            gathered.at[:, h, pl.ds(LAYERS, 8), :], height.at[h], sems.at[2 + h]))
    for copy in copies:
        copy.start()
    return copies


def pack_kernel(right_side, terrain, own, to_left, to_right):
    lane = lanes_iota((32, LANES))
    heights = terrain[pl.ds(0, TILE_ROWS), :]
    for z in range(1, 32):
        heights = heights + terrain[pl.ds(TILE_ROWS * z, TILE_ROWS), :]
    heights = heights.astype(F32)
    for r in range(TILE_ROWS):
        low = right_side[pl.ds(r, 32, stride=TILE_ROWS), :]
        high = right_side[pl.ds(32 * TILE_ROWS + r, 32, stride=TILE_ROWS), :]
        own[r, pl.ds(0, 32), :] = low
        own[r, pl.ds(32, 32), :] = high
        height = jnp.broadcast_to(heights[r:r + 1], (8, LANES))
        own[r, pl.ds(64, 8), :] = height
        to_left[r, pl.ds(0, 32), :] = jnp.where(lane < 64, low, pltpu.roll(high, 64, axis=1))
        to_right[r, pl.ds(0, 32), :] = jnp.where(lane < 64, pltpu.roll(low, 64, axis=1), high)
        to_left[r, pl.ds(32, 8), :] = height
        to_right[r, pl.ds(32, 8), :] = height


def merge_kernel(own, from_right, from_left, out):
    lane = lanes_iota((32, LANES))
    for r in range(TILE_ROWS):
        out[r, 0] = own[r]
        right, left = from_right[r, pl.ds(0, 32), :], from_left[r, pl.ds(0, 32), :]
        out[r, 1, pl.ds(0, 32), :] = jnp.where(lane < 64, right, pltpu.roll(left, 64, axis=1))
        out[r, 1, pl.ds(32, 32), :] = jnp.where(lane < 64, pltpu.roll(right, 64, axis=1), left)
        out[r, 1, pl.ds(64, 8), :] = jnp.where(
            lane[0:8] < 64, from_right[r, pl.ds(32, 8), :], from_left[r, pl.ds(32, 8), :]
        )


def down_kernel(rows, s_ref, gathered, u0, u1, b1, sh1, packed,
                source, height, va0, vb0, va1, vb1, w1, sems):
    copies = load_source(gathered, source, height, sems)
    shift, has_left, has_right = s_ref[0], s_ref[2], s_ref[3]
    for ref in (va0, vb0):
        zero_rim(ref, rows, LAYERS, 2)
    for ref in (va1, vb1):
        zero_rim(ref, rows // 2, 32, 1)
    for copy in copies:
        copy.wait()
    fine = Fine(source, height, edge_mask(0, has_left, has_right), shift)
    fine.coarse_shift(rows, va0, sh1)
    fine.first(va0, rows)
    fine.relax(va0, vb0, 0, rows)
    fine.relax(vb0, va0, 0, rows)
    fine.relax(va0, vb0, 0, rows)
    save = pltpu.make_async_copy(interior(vb0, rows), u0, sems.at[0])
    save.start()
    fine.restricted_defect(vb0, va0, rows, b1)
    level = Coarse(b1, w1, sh1, rows // 2, 32, shift, False)
    level.set_weight(edge_mask(1, has_left, has_right))
    level_1_down(level, va1, vb1, va1)
    pack_level_2(level, va1, packed, 0)
    level.shift_pairs(va1)
    pack_level_2(level, va1, packed, rows // 16)
    for row in range(rows // 2):
        u1[row] = vb1[row + 1, pl.ds(PAD, 32), :]
    save.wait()


def middle_kernel(rows, s_ref, gathered, u0, u1, b1, sh1, own, right, left,
                  u0_out, u1_out, b1_out, packed,
                  source, height, va0, vb0, va1, vb1, w1, va2, vb2, b2, sh2, w2,
                  dup0, dup1, dup2, sems):
    shift, has_left, has_right = s_ref[0], s_ref[2], s_ref[3]
    copies = load_source(gathered, source, height, sems)
    fetch = pltpu.make_async_copy(u0, interior(va0, rows), sems.at[4])
    fetch.start()
    for ref in (va2, vb2):
        zero_rim(ref, rows // 4, 16, 1)
    for ref in (va1, vb1):
        zero_rim(ref, rows // 2, 32, 1)
    e2 = coarse_part(own, right, left, own, right, left, s_ref, rows // 4,
                     (va2, vb2, b2, sh2, w2, dup2))
    level = Coarse(b1, w1, sh1, rows // 2, 32, shift, False)
    level.set_weight(edge_mask(1, has_left, has_right))
    for row in range(rows // 2):
        va1[row + 1, pl.ds(PAD, 32), :] = u1[row]
    level_1_up(level, e2, rows // 4, va1, vb1, dup1)
    fetch.wait()
    for copy in copies:
        copy.wait()
    for ref in (va0, vb0):
        zero_rim(ref, rows, LAYERS, 2)
    fine = Fine(source, height, edge_mask(0, has_left, has_right), shift)
    add_to_fine(va1, va0, 0, rows // 2, dup0)
    for _ in range(SWEEPS):
        fine.relax(va0, vb0, 0, rows)
        fine.relax(vb0, va0, 0, rows)
    save = pltpu.make_async_copy(interior(va0, rows), u0_out, sems.at[0])
    save.start()
    fine.restricted_defect(va0, vb0, rows, b1_out)
    level = Coarse(b1_out, w1, sh1, rows // 2, 32, shift, False)
    level_1_down(level, va1, vb1, va1)
    pack_level_2(level, va1, packed, 0)
    for row in range(rows // 2):
        u1_out[row] = vb1[row + 1, pl.ds(PAD, 32), :]
    save.wait()


def last_kernel(rows, s_ref, gathered, u0, u1, b1, sh1, own, right, left, own_s, right_s, left_s,
                out, source, height, va0, vb0, va1, vb1, w1, va2, vb2, b2, sh2, w2,
                dup0, dup1, dup2, sems):
    shift, has_left, has_right = s_ref[0], s_ref[2], s_ref[3]
    start, mine = s_ref[1], s_ref[4]
    window = pl.ds(start, WINDOW)
    copies = []
    for h in range(2):
        copies.append(pltpu.make_async_copy(
            gathered.at[window, h, pl.ds(0, LAYERS), :], source.at[h], sems.at[h]))
        copies.append(pltpu.make_async_copy(
            gathered.at[window, h, pl.ds(LAYERS, 8), :], height.at[h], sems.at[2 + h]))
    copies.append(pltpu.make_async_copy(
        u0.at[:, window], interior(va0, WINDOW), sems.at[4]))
    for copy in copies:
        copy.start()
    for ref in (va2, vb2):
        zero_rim(ref, rows // 4, 16, 1)
    for ref in (va1, vb1):
        zero_rim(ref, rows // 2, 32, 1)
    e2 = coarse_part(own, right, left, own_s, right_s, left_s, s_ref, rows // 4,
                     (va2, vb2, b2, sh2, w2, dup2))
    level = Coarse(b1, w1, sh1, rows // 2, 32, shift, False)
    level.set_weight(edge_mask(1, has_left, has_right))
    for row in range(rows // 2):
        va1[row + 1, pl.ds(PAD, 32), :] = u1[row]
    level_1_up(level, e2, rows // 4, va1, vb1, dup1)
    for copy in copies:
        copy.wait()
    for ref in (va0, vb0):
        zero_rim(ref, WINDOW, LAYERS, 2)
    fine = Fine(source, height, edge_mask(0, has_left, has_right), shift)

    class Shifted:
        def __getitem__(self, index):
            row, layers, lanes = index
            return va1[row + lax.div(start, 2), layers, lanes]

    add_to_fine(Shifted(), va0, 0, WINDOW // 2, dup0)
    for _ in range(SWEEPS // 2):
        fine.relax(va0, vb0, 0, WINDOW)
        fine.relax(vb0, va0, 0, WINDOW)
    for r in range(TILE_ROWS):
        out[pl.ds(r, LAYERS, stride=TILE_ROWS), :] = va0[0, mine - start + r + 1, pl.ds(PAD, LAYERS), :]


def spec(space=pltpu.VMEM):
    return pl.BlockSpec(memory_space=space)


def params():
    return pltpu.CompilerParams(vmem_limit_bytes=VMEM_LIMIT)


def shape(*dims):
    return jax.ShapeDtypeStruct(dims, F32)


def vmem(*dims):
    return pltpu.VMEM(dims, F32)


def level_0_scratch(rows):
    return [
        vmem(2, rows, LAYERS, LANES),
        vmem(2, rows, 8, LANES),
        vmem(2, rows + 2, LAYERS + 2 * PAD, LANES),
        vmem(2, rows + 2, LAYERS + 2 * PAD, LANES),
    ]


def level_1_scratch(rows):
    return [
        vmem(rows // 2 + 2, 32 + 2 * PAD, LANES),
        vmem(rows // 2 + 2, 32 + 2 * PAD, LANES),
        vmem(rows // 2, 32, LANES),
    ]


def level_2_scratch(rows):
    return [
        vmem(rows // 4 + 2, 16 + 2 * PAD, LANES),
        vmem(rows // 4 + 2, 16 + 2 * PAD, LANES),
        vmem(rows // 4, 16, LANES),
        vmem(rows // 4, 16, LANES),
        vmem(rows // 4, 16, LANES),
        vmem(8, 64, LANES),
        vmem(2, 32, LANES),
        vmem(2, 16, LANES),
    ]


def per_device(right_side, terrain):
    gx, gy = lax.axis_size("gx"), lax.axis_size("gy")
    rows = TILE_ROWS * gx
    i, j = lax.axis_index("gx"), lax.axis_index("gy")
    mine = TILE_ROWS * i
    start = jnp.clip(mine - 4, 0, rows - WINDOW)
    scalars = jnp.stack([
        jnp.int32(PAD), start, (j > 0).astype(jnp.int32), (j < gy - 1).astype(jnp.int32), mine
    ])
    rightward = [(k, k + 1) for k in range(gy - 1)]
    leftward = [(k + 1, k) for k in range(gy - 1)]

    def exchange(to_left, to_right):
        from_right = lax.ppermute(to_left, "gy", leftward)
        from_left = lax.ppermute(to_right, "gy", rightward)
        return from_right, from_left

    flat = LAYERS * TILE_ROWS
    own, to_left, to_right = pl.pallas_call(
        pack_kernel,
        out_shape=(shape(TILE_ROWS, 72, LANES), shape(TILE_ROWS, 40, LANES),
                   shape(TILE_ROWS, 40, LANES)),
        in_specs=[spec()] * 2, out_specs=(spec(),) * 3, name="pack",
    )(right_side.reshape(flat, LANES), terrain.reshape(flat, LANES))
    from_right, from_left = exchange(to_left, to_right)
    merged = pl.pallas_call(
        merge_kernel, out_shape=shape(TILE_ROWS, 2, 72, LANES),
        in_specs=[spec()] * 3, out_specs=spec(), name="merge",
    )(own, from_right, from_left)
    gathered = lax.all_gather(merged, "gx", axis=0, tiled=True)

    smem, hbm = spec(pltpu.SMEM), spec(pl.ANY)
    each = rows // 16
    level_1 = shape(rows // 2, 32, LANES)
    u0, u1, b1, sh1, packed = pl.pallas_call(
        lambda *refs: down_kernel(rows, *refs),
        out_shape=(shape(2, rows, LAYERS, LANES), level_1, level_1, level_1,
                   shape(2 * each, 16, LANES)),
        in_specs=[smem, hbm], out_specs=(hbm,) + (spec(),) * 4,
        scratch_shapes=level_0_scratch(rows) + level_1_scratch(rows)
        + [pltpu.SemaphoreType.DMA((5,))],
        compiler_params=params(), name="down",
    )(scalars, gathered)

    right, left = exchange(packed, packed)
    u0, u1, b1, packed_2 = pl.pallas_call(
        lambda *refs: middle_kernel(rows, *refs),
        out_shape=(shape(2, rows, LAYERS, LANES), level_1, level_1, shape(each, 16, LANES)),
        in_specs=[smem, hbm, hbm] + [spec()] * 6, out_specs=(hbm,) + (spec(),) * 3,
        scratch_shapes=level_0_scratch(rows) + level_1_scratch(rows) + level_2_scratch(rows)
        + [pltpu.SemaphoreType.DMA((5,))],
        compiler_params=params(), name="middle",
    )(scalars, gathered, u0, u1, b1, sh1, packed, right, left)

    right_2, left_2 = exchange(packed_2, packed_2)
    out = pl.pallas_call(
        lambda *refs: last_kernel(rows, *refs),
        out_shape=shape(flat, LANES),
        in_specs=[smem, hbm, hbm] + [spec()] * 9, out_specs=spec(),
        scratch_shapes=level_0_scratch(WINDOW) + level_1_scratch(rows) + level_2_scratch(rows)
        + [pltpu.SemaphoreType.DMA((5,))],
        compiler_params=params(), name="last",
    )(scalars, gathered, u0, u1, b1, sh1, packed_2, right_2, left_2, packed, right, left)
    return out.reshape(LAYERS, TILE_ROWS, LANES)


def solution(mesh):
    in_specs = (P(None, "gx", "gy"), P(None, "gx", "gy"))
    out_specs = P(None, "gx", "gy")
    return jax.shard_map(
        per_device, mesh=mesh, in_specs=in_specs, out_specs=out_specs, check_vma=False
    )
```

```python
import jax
import jax.numpy as jnp
from jax import lax
from jax.experimental import pallas as pl
from jax.experimental.pallas import tpu as pltpu
from jax.sharding import PartitionSpec as P

SWEEPS = 4
COARSE_SWEEPS = 8
RELAX_WEIGHT = 0.8
TERRAIN_PENALTY = 0.05

F32 = jnp.float32
LANES = 128
SUB = 8
LAYERS = 64
TILE_ROWS = 8
WINDOW = 16
VMEM_LIMIT = 56 * 1024 * 1024

D_AIR = 6.0
D_TERRAIN = 6.0 + TERRAIN_PENALTY


def lanes_iota(shape):
    return lax.broadcasted_iota(jnp.int32, shape, len(shape) - 1)


def edge_mask(level, has_left, has_right):
    lane = lanes_iota((1, LANES))
    zero = jnp.zeros((1, LANES), F32)
    left = zero + has_left.astype(F32)
    right = zero + has_right.astype(F32)
    if level < 2:
        return jnp.where(lane < 64, 1.0, jnp.where(lane < 96, right, left))
    if level == 2:
        return jnp.where(
            lane < 32, 1.0, jnp.where(lane < 64, right, jnp.where(lane < 96, 0.0, left))
        )
    return jnp.where(
        lane < 16, 1.0, jnp.where(lane < 32, right, jnp.where(lane < 112, 0.0, left))
    )


def dot(values, matrix):
    return lax.dot_general(
        values, matrix, (((1,), (0,)), ((), ())),
        precision=lax.Precision.HIGHEST, preferred_element_type=F32,
    )


def matrix_of(rule, value=1.0):
    row = lax.broadcasted_iota(jnp.int32, (LANES, LANES), 0)
    col = lax.broadcasted_iota(jnp.int32, (LANES, LANES), 1)
    return jnp.where(rule(row, col), value, 0.0).astype(F32)


def layer_sum(v):
    count = v.shape[0]
    sub = lax.broadcasted_iota(jnp.int32, (1, SUB, LANES), 1)
    below = jnp.where(sub == 0, 0.0, pltpu.roll(v[count - 1:], 1, axis=1))
    above = jnp.where(sub == SUB - 1, 0.0, pltpu.roll(v[:1], SUB - 1, axis=1))
    if count == 1:
        return below + above
    return jnp.concatenate([below, v[:-1]], axis=0) + jnp.concatenate([v[1:], above], axis=0)


def column_sum(parts):
    if len(parts) == 1:
        v = parts[0]
        return [pltpu.roll(v, 1, axis=2) + pltpu.roll(v, LANES - 1, axis=2)]
    even, odd = parts
    return [odd + pltpu.roll(odd, 1, axis=2), even + pltpu.roll(even, LANES - 1, axis=2)]


def stencil_group(load, first, count, emit):
    held = [load(first + k - 1) for k in range(count + 2)]
    stores = []
    for k in range(count):
        centre = held[k + 1]
        sides = column_sum(centre)
        pairs = []
        for h, v in enumerate(centre):
            total = held[k][h] + held[k + 2][h]
            pairs.append((v, total + layer_sum(v) + sides[h]))
        stores.append(emit(first + k, pairs))
    for store in stores:
        store()


def over_rows(start, rows, group, body):
    if isinstance(rows, int) and rows <= group:
        body(start, rows)
        return

    def step(i, carry):
        body(start + i * group, group)
        return carry

    lax.fori_loop(0, rows // group, step, 0)


class Fine:
    def __init__(self, source, weight, height):
        self.source, self.weight, self.height = source, weight, height

    @staticmethod
    def loader(src):
        return lambda row: [src[h, row + 1] for h in range(2)]

    def ground(self, row, h):
        layer = (
            8 * lax.broadcasted_iota(jnp.int32, (8, SUB, LANES), 1)
            + lax.broadcasted_iota(jnp.int32, (8, SUB, LANES), 0)
        ).astype(F32)
        return layer < self.height[h, row][None]

    def relax(self, src, dst, start, rows, group):
        def emit(row, pairs):
            new = [
                (1.0 - RELAX_WEIGHT) * v + self.weight[h, row] * (total + self.source[h, row])
                for h, (v, total) in enumerate(pairs)
            ]

            def store():
                for h in range(2):
                    dst[h, row + 1] = new[h]

            return store

        over_rows(start, rows, group,
                  lambda first, count: stencil_group(self.loader(src), first, count, emit))

    def restricted_defect(self, src, rows, out):
        load = self.loader(src)

        def body(first, count):
            sums = []

            def emit(row, pairs):
                total = 0.0
                for h, (v, near) in enumerate(pairs):
                    diagonal = jnp.where(self.ground(row, h), D_TERRAIN, D_AIR)
                    total = total + (self.source[h, row] + near - diagonal * v)
                sums.append(total)
                return lambda: None

            stencil_group(load, first, count, emit)
            for k in range(count // 2):
                both = sums[2 * k] + sums[2 * k + 1]
                for z in range(4):
                    out[lax.div(first, 2) + k, z] = 0.5 * (both[2 * z] + both[2 * z + 1])

        over_rows(0, rows, 8, body)

    def coarse_shift(self, rows, out):
        base = (
            8 * lax.broadcasted_iota(jnp.int32, (4, SUB, LANES), 1)
            + 2 * lax.broadcasted_iota(jnp.int32, (4, SUB, LANES), 0)
        ).astype(F32)

        def body(first, count):
            for k in range(count):
                total = 0.0
                for h in range(2):
                    for m in range(2):
                        height = self.height[h, 2 * (first + k) + m][None]
                        total = total + jnp.clip(height - base, 0.0, 2.0)
                out[first + k] = (0.5 * TERRAIN_PENALTY) * total

        over_rows(0, rows // 2, 4, body)


class Coarse:
    def __init__(self, source, weight, shift_now, rows, group):
        self.source, self.weight, self.shift_now = source, weight, shift_now
        self.rows, self.group = rows, group

    def set_weight(self, edge):
        def body(first, count):
            for k in range(count):
                self.weight[first + k] = edge * (RELAX_WEIGHT / (6.0 + self.shift_now[first + k]))

        over_rows(0, self.rows, self.group, body)

    def first(self, dst):
        def body(first, count):
            for k in range(count):
                dst[first + k + 1] = self.weight[first + k] * self.source[first + k]

        over_rows(0, self.rows, self.group, body)

    def relax(self, src, dst):
        def emit(row, pairs):
            v, total = pairs[0]
            new = (1.0 - RELAX_WEIGHT) * v + self.weight[row] * (total + self.source[row])

            def store():
                dst[row + 1] = new

            return store

        load = lambda row: [src[row + 1]]
        over_rows(0, self.rows, self.group,
                  lambda first, count: stencil_group(load, first, count, emit))

    def defect_pairs(self, src):
        sums = []

        def emit(row, pairs):
            v, total = pairs[0]
            sums.append(self.source[row] + total - (6.0 + self.shift_now[row]) * v)
            return lambda: None

        stencil_group(lambda row: [src[row + 1]], 0, self.rows, emit)
        return pair_up(sums)

    def shift_pairs(self):
        return pair_up([self.shift_now[row] for row in range(self.rows)])


def pair_up(rows):
    out = []
    for k in range(len(rows) // 2):
        both = rows[2 * k] + rows[2 * k + 1]
        out.append(jnp.stack([both[2 * z] + both[2 * z + 1] for z in range(both.shape[0] // 2)]))
    return out


def pack_level_2(pairs, out, offset):
    into = matrix_of(lambda a, b: (a < 64) & (b == lax.div(a, 2)), 0.5)
    count = len(pairs) // 4
    flat = jnp.stack(pairs).reshape(len(pairs) * 2 * SUB, LANES)
    lanes = dot(flat, into).reshape(4, count, 2, SUB, LANES)
    total = lanes[0]
    for g in range(1, 4):
        total = total + pltpu.roll(lanes[g], 32 * g, axis=3)
    out[pl.ds(offset, count)] = total


def unpack_level_2(own, right, left, offset, each, out):
    lane = lanes_iota((each, 2, SUB, LANES))
    for g in range(4):
        parts = []
        for ref, place in ((own, 0), (right, 32), (left, 96)):
            value = ref[pl.ds(offset, each)]
            amount = (place - 32 * g) % LANES
            parts.append(pltpu.roll(value, amount, axis=3) if amount else value)
        out[pl.ds(g * each, each)] = jnp.where(
            lane < 32, parts[0],
            jnp.where(lane < 64, parts[1], jnp.where(lane < 96, 0.0, parts[2])),
        )


def coarsest(source, diagonal, edge, rows):
    weight = edge * (RELAX_WEIGHT / diagonal)
    zero = jnp.zeros((1, SUB, LANES), F32)

    def body(i, v):
        total = jnp.concatenate([zero, v[:-1]], axis=0) + jnp.concatenate([v[1:], zero], axis=0)
        sub = lax.broadcasted_iota(jnp.int32, (rows, SUB, LANES), 1)
        total = total + jnp.where(sub == 0, 0.0, pltpu.roll(v, 1, axis=1))
        total = total + jnp.where(sub == SUB - 1, 0.0, pltpu.roll(v, SUB - 1, axis=1))
        total = total + column_sum([v])[0]
        return (1.0 - RELAX_WEIGHT) * v + weight * (total + source)

    v = weight * source
    for i in range(COARSE_SWEEPS - 1):
        v = body(i, v)
    return v


def zero_rim(ref, rows, halves):
    if halves == 2:
        zero = jnp.zeros((2,) + ref.shape[2:], F32)
        ref[:, 0] = zero
        ref[:, rows + 1] = zero
    else:
        zero = jnp.zeros(ref.shape[1:], F32)
        ref[0] = zero
        ref[rows + 1] = zero


def level_1_down(level, va, vb, packed):
    level.first(va)
    level.relax(va, vb)
    level.relax(vb, va)
    level.relax(va, vb)
    pack_level_2(level.defect_pairs(vb), packed, 0)


def coarse_part(own, right, left, own_s, right_s, left_s, has_left, has_right, rows2, refs):
    va, vb, b2, sh2, w2 = refs
    each = rows2 // 4
    unpack_level_2(own, right, left, 0, each, b2)
    unpack_level_2(own_s, right_s, left_s, each, each, sh2)
    for ref in (va, vb):
        zero_rim(ref, rows2, 1)
    level = Coarse(b2, w2, sh2, rows2, rows2)
    level.set_weight(edge_mask(2, has_left, has_right))
    level.first(va)
    level.relax(va, vb)
    level.relax(vb, va)
    level.relax(va, vb)

    into = matrix_of(
        lambda a, b: b == jnp.where(a < 64, lax.div(a, 2), 64 + lax.div(a, 2)), 0.5
    )
    rows3 = rows2 // 2

    def to_level_3(pairs):
        flat = jnp.stack(pairs).reshape(rows3 * SUB, LANES)
        return dot(flat, into).reshape(rows3, SUB, LANES)

    shift_3 = to_level_3(level.shift_pairs())
    source_3 = to_level_3(level.defect_pairs(vb))
    e3 = coarsest(source_3, 6.0 + shift_3, edge_mask(3, has_left, has_right), rows3)
    out_of = matrix_of(
        lambda a, b: a == jnp.where(b < 64, lax.div(b, 2), 64 + lax.div(b, 2))
    )
    spread = dot(e3.reshape(rows3 * SUB, LANES), out_of).reshape(rows3, SUB, LANES)
    for row in range(rows2):
        vb[row + 1] = vb[row + 1] + spread[row // 2][None]
    for _ in range(SWEEPS // 2):
        level.relax(vb, va)
        level.relax(va, vb)
    return vb


def level_1_up(level, e2, rows2, u1, va, vb):
    out_of = matrix_of(
        lambda a, b: a == jnp.where(b < 96, lax.div(b, 2), 64 + lax.div(b, 2))
    )
    flat = e2[pl.ds(1, rows2)].reshape(rows2 * 2 * SUB, LANES)
    spread = dot(flat, out_of).reshape(rows2, 2, SUB, LANES)
    for row in range(2 * rows2):
        e = spread[row // 2]
        for z in range(4):
            va[row + 1, z] = u1[row, z] + e[z // 2]
    for _ in range(SWEEPS // 2):
        level.relax(va, vb)
        level.relax(vb, va)


def add_to_fine(e1, target, first_pair, pairs):
    def body(first, count):
        for k in range(count):
            e = e1[first_pair + first + k + 1]
            twice = jnp.stack([e[z // 2] for z in range(8)])
            for h in range(2):
                for m in range(2):
                    row = 2 * (first + k) + m + 1
                    target[h, row] = target[h, row] + twice

    over_rows(0, pairs, 4, body)


def interior(ref, rows):
    return ref.at[:, pl.ds(1, rows)]


def first_columns(shape):
    return lax.rem(lax.div(lanes_iota(shape), 32), 2) == 0


def pack_kernel(right_side, terrain, own, to_left, to_right):
    apart = matrix_of(lambda a, b: b == lax.div(a, 2) + 64 * lax.rem(a, 2))
    heights = terrain[pl.ds(0, TILE_ROWS), :]
    for z in range(1, 32):
        heights = heights + terrain[pl.ds(TILE_ROWS * z, TILE_ROWS), :]
    heights = dot(heights.astype(F32), apart)
    own[64] = heights
    heights = pltpu.roll(heights, 64, axis=1)
    to_left[32] = heights
    to_right[32] = heights
    first = first_columns((4, SUB, LANES))
    for r in range(TILE_ROWS):
        layers = [
            right_side[pl.ds(zz * TILE_ROWS + r, SUB, stride=8 * TILE_ROWS), :] for zz in range(8)
        ]
        value = dot(jnp.concatenate(layers, axis=0), apart).reshape(8, SUB, LANES)
        own[pl.ds(8 * r, 8)] = value
        value = pltpu.roll(value, 64, axis=2)
        low, high = value[:4], value[4:]
        to_left[pl.ds(4 * r, 4)] = jnp.where(first, low, pltpu.roll(high, 32, axis=2))
        to_right[pl.ds(4 * r, 4)] = jnp.where(first, pltpu.roll(high, 96, axis=2), low)


def merge_kernel(own, from_right, from_left, out):
    first = first_columns((4, SUB, LANES))
    for r in range(TILE_ROWS):
        part, place = r // 4, 8 * (r % 4)
        out[part, pl.ds(place, 8)] = own[pl.ds(8 * r, 8)]
        right, left = from_right[pl.ds(4 * r, 4)], from_left[pl.ds(4 * r, 4)]
        out[part, pl.ds(32 + place, 4)] = jnp.where(first, right, left)
        out[part, pl.ds(32 + place + 4, 4)] = jnp.where(
            first, pltpu.roll(right, 96, axis=2), pltpu.roll(left, 32, axis=2)
        )
    out[0, 64] = own[64]
    out[1, 64] = jnp.where(first[0], from_right[32], from_left[32])


def down_kernel(rows, s_ref, *refs):
    tiles, refs = refs[:10], refs[10:]
    (u0, source_out, weight_out, height_out, u1, b1, sh1, packed,
     source, weight, height, own, beside, heights, va0, vb0, va1, vb1, w1, sems) = refs
    has_left, has_right = s_ref[2], s_ref[3]
    chips = rows // (2 * TILE_ROWS)
    me = lax.div(s_ref[4], TILE_ROWS)
    z, core = lax.div(me, 2), lax.rem(me, 2)

    def device(step, other):
        return 2 * lax.rem(z + step + chips, chips) + (1 - core if other else core)

    pieces = []
    for other, (w, a, b, c0, c1) in ((False, tiles[:5]), (True, tiles[5:])):
        for ref, step in ((w, 0), (a, -1), (b, 1)):
            for part in range(2):
                pieces.append((ref.at[part], device(step, other), part))
        pieces.append((c0, device(2, other), 0))
        pieces.append((c1, device(2, other), 1))
    copies = []
    for n, (ref, dev, part) in enumerate(pieces):
        row = TILE_ROWS * dev + 4 * part
        copies += [
            pltpu.make_async_copy(ref.at[pl.ds(0, 32)], own.at[pl.ds(8 * row, 32)], sems.at[3 * n]),
            pltpu.make_async_copy(
                ref.at[pl.ds(32, 32)], beside.at[pl.ds(8 * row, 32)], sems.at[3 * n + 1]),
            pltpu.make_async_copy(ref.at[64], heights.at[part, dev], sems.at[3 * n + 2]),
        ]
    for copy in copies:
        copy.start()
    for ref in (va0, vb0):
        zero_rim(ref, rows, 2)
    for ref in (va1, vb1):
        zero_rim(ref, rows // 2, 1)
    for copy in copies:
        copy.wait()

    edge = edge_mask(0, has_left, has_right)
    fine = Fine(source, weight, height)
    lane = lanes_iota((8, SUB, LANES))
    low = lane < 64

    def halves(own_value, beside_value, low):
        even = jnp.where(low, own_value, beside_value)
        odd = jnp.where(low, beside_value, own_value)
        return even, pltpu.roll(odd, 64, axis=odd.ndim - 1)

    def assemble(dev, carry):
        tall = halves(heights[0, dev], heights[1, dev], low[0])
        for r in range(TILE_ROWS):
            row = TILE_ROWS * dev + r
            place = pl.ds(8 * row, 8)
            both = halves(own[place], beside[place], low)
            for h in range(2):
                source[h, row] = both[h]
                height[h, row] = jnp.broadcast_to(tall[h][r:r + 1], (SUB, LANES))
                now = edge * jnp.where(
                    fine.ground(row, h), RELAX_WEIGHT / D_TERRAIN, RELAX_WEIGHT / D_AIR
                )
                weight[h, row] = now
                va0[h, row + 1] = now * both[h]
        return carry

    lax.fori_loop(0, rows // TILE_ROWS, assemble, 0)
    saves = [
        pltpu.make_async_copy(source, source_out, sems.at[1]),
        pltpu.make_async_copy(weight, weight_out, sems.at[2]),
        pltpu.make_async_copy(height, height_out, sems.at[3]),
    ]
    for save in saves:
        save.start()
    fine.coarse_shift(rows, sh1)
    fine.relax(va0, vb0, 0, rows, 8)
    fine.relax(vb0, va0, 0, rows, 8)
    fine.relax(va0, vb0, 0, rows, 8)
    saves.append(pltpu.make_async_copy(interior(vb0, rows), u0, sems.at[0]))
    saves[-1].start()
    fine.restricted_defect(vb0, rows, b1)
    level = Coarse(b1, w1, sh1, rows // 2, 16)
    level.set_weight(edge_mask(1, has_left, has_right))
    level_1_down(level, va1, vb1, packed)
    pack_level_2(level.shift_pairs(), packed, rows // 16)
    u1[...] = vb1[pl.ds(1, rows // 2)]
    for save in saves:
        save.wait()


def middle_kernel(rows, s_ref, source_in, weight_in, height_in, u0, u1, b1, sh1, own, right, left,
                  u0_out, u1_out, b1_out, packed,
                  source, weight, height, va0, vb0, va1, vb1, w1, va2, vb2, b2, sh2, w2, sems):
    has_left, has_right = s_ref[2], s_ref[3]
    copies = [
        pltpu.make_async_copy(u0, interior(va0, rows), sems.at[0]),
        pltpu.make_async_copy(source_in, source, sems.at[1]),
        pltpu.make_async_copy(weight_in, weight, sems.at[2]),
        pltpu.make_async_copy(height_in, height, sems.at[3]),
    ]
    for copy in copies:
        copy.start()
    for ref in (va1, vb1):
        zero_rim(ref, rows // 2, 1)
    e2 = coarse_part(own, right, left, own, right, left, has_left, has_right, rows // 4,
                     (va2, vb2, b2, sh2, w2))
    level = Coarse(b1, w1, sh1, rows // 2, 16)
    level.set_weight(edge_mask(1, has_left, has_right))
    level_1_up(level, e2, rows // 4, u1, va1, vb1)
    for ref in (va0, vb0):
        zero_rim(ref, rows, 2)
    for copy in copies:
        copy.wait()
    fine = Fine(source, weight, height)
    add_to_fine(va1, va0, 0, rows // 2)
    for _ in range(SWEEPS):
        fine.relax(va0, vb0, 0, rows, 8)
        fine.relax(vb0, va0, 0, rows, 8)
    save = pltpu.make_async_copy(interior(va0, rows), u0_out, sems.at[0])
    save.start()
    fine.restricted_defect(va0, rows, b1_out)
    level = Coarse(b1_out, w1, sh1, rows // 2, 16)
    level_1_down(level, va1, vb1, packed)
    u1_out[...] = vb1[pl.ds(1, rows // 2)]
    save.wait()


def last_kernel(rows, s_ref, source_in, weight_in, u0, u1, b1, sh1,
                own, right, left, own_s, right_s, left_s,
                out, source, weight, va0, vb0, va1, vb1, w1, va2, vb2, b2, sh2, w2, sems):
    start, has_left, has_right, mine = s_ref[1], s_ref[2], s_ref[3], s_ref[4]
    window = pl.ds(start, WINDOW)
    copies = [
        pltpu.make_async_copy(u0.at[:, window], interior(va0, WINDOW), sems.at[0]),
        pltpu.make_async_copy(source_in.at[:, window], source, sems.at[1]),
        pltpu.make_async_copy(weight_in.at[:, window], weight, sems.at[2]),
    ]
    for copy in copies:
        copy.start()
    for ref in (va1, vb1):
        zero_rim(ref, rows // 2, 1)
    e2 = coarse_part(own, right, left, own_s, right_s, left_s, has_left, has_right, rows // 4,
                     (va2, vb2, b2, sh2, w2))
    level = Coarse(b1, w1, sh1, rows // 2, 16)
    level.set_weight(edge_mask(1, has_left, has_right))
    level_1_up(level, e2, rows // 4, u1, va1, vb1)
    for ref in (va0, vb0):
        zero_rim(ref, WINDOW, 2)
    for copy in copies:
        copy.wait()
    fine = Fine(source, weight, None)
    add_to_fine(va1, va0, lax.div(start, 2), WINDOW // 2)
    src, dst = va0, vb0
    for k in range(SWEEPS):
        reach = SWEEPS - 1 - k
        count = TILE_ROWS + 2 * reach
        first = jnp.clip(mine - start - reach, 0, WINDOW - count)
        fine.relax(src, dst, first, count, count)
        src, dst = dst, src
    together = [
        matrix_of(lambda a, b, h=h: (a < 64) & (b == 2 * a + h)) for h in range(2)
    ]
    for r in range(TILE_ROWS):
        row = mine - start + r + 1
        value = 0.0
        for h in range(2):
            value = value + dot(src[h, row].reshape(8 * SUB, LANES), together[h])
        for zz in range(8):
            out[pl.ds(zz * TILE_ROWS + r, SUB, stride=8 * TILE_ROWS), :] = (
                value[SUB * zz:SUB * (zz + 1)]
            )


def spec(space=pltpu.VMEM):
    return pl.BlockSpec(memory_space=space)


def params():
    return pltpu.CompilerParams(vmem_limit_bytes=VMEM_LIMIT)


def shape(*dims):
    return jax.ShapeDtypeStruct(dims + (SUB, LANES), F32)


def vmem(*dims):
    return pltpu.VMEM(dims + (SUB, LANES), F32)


def level_1_scratch(rows):
    return [vmem(rows // 2 + 2, 4), vmem(rows // 2 + 2, 4), vmem(rows // 2, 4)]


def level_2_scratch(rows):
    return [vmem(rows // 4 + 2, 2)] * 2 + [vmem(rows // 4, 2)] * 3


def per_device(right_side, terrain):
    gx, gy = lax.axis_size("gx"), lax.axis_size("gy")
    rows = TILE_ROWS * gx
    i, j = lax.axis_index("gx"), lax.axis_index("gy")
    mine = TILE_ROWS * i
    start = jnp.clip(mine - 4, 0, rows - WINDOW)
    scalars = jnp.stack([
        jnp.int32(0), start, (j > 0).astype(jnp.int32), (j < gy - 1).astype(jnp.int32), mine
    ])
    rightward = [(k, k + 1) for k in range(gy - 1)]
    leftward = [(k + 1, k) for k in range(gy - 1)]

    def exchange(to_left, to_right):
        from_right = lax.ppermute(to_left, "gy", leftward)
        from_left = lax.ppermute(to_right, "gy", rightward)
        return from_right, from_left

    flat = LAYERS * TILE_ROWS
    blocks = TILE_ROWS * 8
    own, to_left, to_right = pl.pallas_call(
        pack_kernel,
        out_shape=(shape(blocks + 1), shape(blocks // 2 + 1), shape(blocks // 2 + 1)),
        in_specs=[spec()] * 2, out_specs=(spec(),) * 3, name="pack",
    )(right_side.reshape(flat, LANES), terrain.reshape(flat, LANES))
    from_right, from_left = exchange(to_left, to_right)
    tile = pl.pallas_call(
        merge_kernel, out_shape=shape(2, blocks + 1),
        in_specs=[spec()] * 3, out_specs=spec(), name="merge",
    )(own, from_right, from_left)

    up = [(k, (k + 2) % gx) for k in range(gx)]
    down = [(k, (k - 2) % gx) for k in range(gx)]
    swap = [(k, k ^ 1) for k in range(gx)]
    below = lax.ppermute(tile, "gx", up)
    above = lax.ppermute(tile, "gx", down)
    tile_s = lax.ppermute(tile, "gx", swap)
    far_0 = lax.ppermute(below[0], "gx", up)
    far_1 = lax.ppermute(above[1], "gx", down)
    below_s = lax.ppermute(below, "gx", swap)
    above_s = lax.ppermute(above, "gx", swap)
    far_0_s = lax.ppermute(far_0, "gx", swap)
    far_1_s = lax.ppermute(far_1, "gx", swap)
    tiles = (tile, below, above, far_0, far_1, tile_s, below_s, above_s, far_0_s, far_1_s)

    smem, hbm = spec(pltpu.SMEM), spec(pl.ANY)
    each = rows // 16
    level_0, level_1 = shape(2, rows, 8), shape(rows // 2, 4)
    fine_rows = [vmem(2, rows + 2, 8)] * 2
    u0, source, weight, height, u1, b1, sh1, packed = pl.pallas_call(
        lambda *refs: down_kernel(rows, *refs),
        out_shape=(level_0, level_0, level_0, shape(2, rows), level_1, level_1, level_1,
                   shape(2 * each, 2)),
        in_specs=[smem] + [hbm] * 10, out_specs=(hbm,) * 4 + (spec(),) * 4,
        scratch_shapes=[vmem(2, rows, 8), vmem(2, rows, 8), vmem(2, rows),
                        vmem(rows * 8), vmem(rows * 8), vmem(2, gx)]
        + fine_rows + level_1_scratch(rows) + [pltpu.SemaphoreType.DMA((48,))],
        compiler_params=params(), name="down",
    )(scalars, *tiles)

    right, left = exchange(packed, packed)
    u0, u1, b1, packed_2 = pl.pallas_call(
        lambda *refs: middle_kernel(rows, *refs),
        out_shape=(level_0, level_1, level_1, shape(each, 2)),
        in_specs=[smem] + [hbm] * 4 + [spec()] * 6, out_specs=(hbm,) + (spec(),) * 3,
        scratch_shapes=[vmem(2, rows, 8), vmem(2, rows, 8), vmem(2, rows)]
        + fine_rows + level_1_scratch(rows) + level_2_scratch(rows)
        + [pltpu.SemaphoreType.DMA((4,))],
        compiler_params=params(), name="middle",
    )(scalars, source, weight, height, u0, u1, b1, sh1, packed, right, left)

    right_2, left_2 = exchange(packed_2, packed_2)
    out = pl.pallas_call(
        lambda *refs: last_kernel(rows, *refs),
        out_shape=jax.ShapeDtypeStruct((flat, LANES), F32),
        in_specs=[smem] + [hbm] * 3 + [spec()] * 9, out_specs=spec(),
        scratch_shapes=[vmem(2, WINDOW, 8), vmem(2, WINDOW, 8)]
        + [vmem(2, WINDOW + 2, 8)] * 2 + level_1_scratch(rows) + level_2_scratch(rows)
        + [pltpu.SemaphoreType.DMA((3,))],
        compiler_params=params(), name="last",
    )(scalars, source, weight, u0, u1, b1, sh1,
      packed_2, right_2, left_2, packed, right, left)
    return out.reshape(LAYERS, TILE_ROWS, LANES)


def solution(mesh):
    in_specs = (P(None, "gx", "gy"), P(None, "gx", "gy"))
    out_specs = P(None, "gx", "gy")
    return jax.shard_map(
        per_device, mesh=mesh, in_specs=in_specs, out_specs=out_specs, check_vma=False
    )
```

```python
import jax
import jax.numpy as jnp
from jax import lax
from jax.experimental import pallas as pl
from jax.experimental.pallas import tpu as pltpu
from jax.sharding import PartitionSpec as P

SWEEPS = 4
COARSE_SWEEPS = 8
RELAX_WEIGHT = 0.8
TERRAIN_PENALTY = 0.05

F32 = jnp.float32
LANES = 128
SUB = 8
LAYERS = 64
TILE_ROWS = 8
WINDOW = 16
VMEM_LIMIT = 56 * 1024 * 1024

D_AIR = 6.0
D_TERRAIN = 6.0 + TERRAIN_PENALTY


def lanes_iota(shape):
    return lax.broadcasted_iota(jnp.int32, shape, len(shape) - 1)


def edge_mask(level, has_left, has_right):
    lane = lanes_iota((1, LANES))
    zero = jnp.zeros((1, LANES), F32)
    left = zero + has_left.astype(F32)
    right = zero + has_right.astype(F32)
    if level < 2:
        return jnp.where(lane < 64, 1.0, jnp.where(lane < 96, right, left))
    if level == 2:
        return jnp.where(
            lane < 32, 1.0, jnp.where(lane < 64, right, jnp.where(lane < 96, 0.0, left))
        )
    return jnp.where(
        lane < 16, 1.0, jnp.where(lane < 32, right, jnp.where(lane < 112, 0.0, left))
    )


def dot(values, matrix):
    return lax.dot_general(
        values, matrix, (((1,), (0,)), ((), ())),
        precision=lax.Precision.HIGHEST, preferred_element_type=F32,
    )


def matrix_of(rule, value=1.0):
    row = lax.broadcasted_iota(jnp.int32, (LANES, LANES), 0)
    col = lax.broadcasted_iota(jnp.int32, (LANES, LANES), 1)
    return jnp.where(rule(row, col), value, 0.0).astype(F32)


def layer_sum(v):
    count = v.shape[0]
    sub = lax.broadcasted_iota(jnp.int32, (1, SUB, LANES), 1)
    below = jnp.where(sub == 0, 0.0, pltpu.roll(v[count - 1:], 1, axis=1))
    above = jnp.where(sub == SUB - 1, 0.0, pltpu.roll(v[:1], SUB - 1, axis=1))
    if count == 1:
        return below + above
    return jnp.concatenate([below, v[:-1]], axis=0) + jnp.concatenate([v[1:], above], axis=0)


def column_sum(parts):
    if len(parts) == 1:
        v = parts[0]
        return [pltpu.roll(v, 1, axis=2) + pltpu.roll(v, LANES - 1, axis=2)]
    even, odd = parts
    return [odd + pltpu.roll(odd, 1, axis=2), even + pltpu.roll(even, LANES - 1, axis=2)]


def stencil_group(load, first, count, emit):
    before, centre = load(first - 1), load(first)
    for k in range(count):
        after = load(first + k + 1)
        sides = column_sum(centre)
        pairs = []
        for h, v in enumerate(centre):
            total = before[h] + after[h]
            pairs.append((v, total + layer_sum(v) + sides[h]))
        emit(first + k, pairs)
        before, centre = centre, after


def over_rows(start, rows, group, body):
    if isinstance(rows, int) and rows <= group:
        body(start, rows)
        return

    def step(i, carry):
        body(start + i * group, group)
        return carry

    lax.fori_loop(0, rows // group, step, 0)


class Fine:
    def __init__(self, source, weight, height):
        self.source, self.weight, self.height = source, weight, height

    @staticmethod
    def loader(src):
        return lambda row: [src[h, row + 1] for h in range(2)]

    def ground(self, row, h):
        layer = (
            8 * lax.broadcasted_iota(jnp.int32, (8, SUB, LANES), 1)
            + lax.broadcasted_iota(jnp.int32, (8, SUB, LANES), 0)
        ).astype(F32)
        return layer < self.height[h, row][None]

    def relax(self, src, dst, start, rows, group):
        def emit(row, pairs):
            for h, (v, total) in enumerate(pairs):
                total = total + self.source[h, row]
                dst[h, row + 1] = (1.0 - RELAX_WEIGHT) * v + self.weight[h, row] * total

        over_rows(start, rows, group,
                  lambda first, count: stencil_group(self.loader(src), first, count, emit))

    def restricted_defect(self, src, rows, out):
        load = self.loader(src)

        def body(first, count):
            sums = []

            def emit(row, pairs):
                total = 0.0
                for h, (v, near) in enumerate(pairs):
                    diagonal = jnp.where(self.ground(row, h), D_TERRAIN, D_AIR)
                    total = total + (self.source[h, row] + near - diagonal * v)
                sums.append(total)

            stencil_group(load, first, count, emit)
            for k in range(count // 2):
                both = sums[2 * k] + sums[2 * k + 1]
                for z in range(4):
                    out[lax.div(first, 2) + k, z] = 0.5 * (both[2 * z] + both[2 * z + 1])

        over_rows(0, rows, 8, body)

    def coarse_shift(self, rows, out):
        base = (
            8 * lax.broadcasted_iota(jnp.int32, (4, SUB, LANES), 1)
            + 2 * lax.broadcasted_iota(jnp.int32, (4, SUB, LANES), 0)
        ).astype(F32)

        def body(first, count):
            for k in range(count):
                total = 0.0
                for h in range(2):
                    for m in range(2):
                        height = self.height[h, 2 * (first + k) + m][None]
                        total = total + jnp.clip(height - base, 0.0, 2.0)
                out[first + k] = (0.5 * TERRAIN_PENALTY) * total

        over_rows(0, rows // 2, 4, body)


class Coarse:
    def __init__(self, source, weight, shift_now, rows, group):
        self.source, self.weight, self.shift_now = source, weight, shift_now
        self.rows, self.group = rows, group

    def set_weight(self, edge):
        def body(first, count):
            for k in range(count):
                self.weight[first + k] = edge * (RELAX_WEIGHT / (6.0 + self.shift_now[first + k]))

        over_rows(0, self.rows, self.group, body)

    def first(self, dst):
        def body(first, count):
            for k in range(count):
                dst[first + k + 1] = self.weight[first + k] * self.source[first + k]

        over_rows(0, self.rows, self.group, body)

    def relax(self, src, dst):
        def emit(row, pairs):
            v, total = pairs[0]
            total = total + self.source[row]
            dst[row + 1] = (1.0 - RELAX_WEIGHT) * v + self.weight[row] * total

        load = lambda row: [src[row + 1]]
        over_rows(0, self.rows, self.group,
                  lambda first, count: stencil_group(load, first, count, emit))

    def defect_pairs(self, src):
        sums = []

        def emit(row, pairs):
            v, total = pairs[0]
            sums.append(self.source[row] + total - (6.0 + self.shift_now[row]) * v)

        stencil_group(lambda row: [src[row + 1]], 0, self.rows, emit)
        return pair_up(sums)

    def shift_pairs(self):
        return pair_up([self.shift_now[row] for row in range(self.rows)])


def pair_up(rows):
    out = []
    for k in range(len(rows) // 2):
        both = rows[2 * k] + rows[2 * k + 1]
        out.append(jnp.stack([both[2 * z] + both[2 * z + 1] for z in range(both.shape[0] // 2)]))
    return out


def pack_level_2(pairs, out, offset):
    into = matrix_of(lambda a, b: (a < 64) & (b == lax.div(a, 2)), 0.5)
    count = len(pairs) // 4
    flat = jnp.stack(pairs).reshape(len(pairs) * 2 * SUB, LANES)
    lanes = dot(flat, into).reshape(4, count, 2, SUB, LANES)
    total = lanes[0]
    for g in range(1, 4):
        total = total + pltpu.roll(lanes[g], 32 * g, axis=3)
    out[pl.ds(offset, count)] = total


def unpack_level_2(own, first, second, even, offset, each, out):
    lane = lanes_iota((each, 2, SUB, LANES))
    held = [ref[pl.ds(offset, each)] for ref in (own, first, second)]
    left = jnp.where(even, held[1], held[2])
    right = jnp.where(even, held[2], held[1])
    for g in range(4):
        parts = []
        for value, place in ((held[0], 0), (right, 32), (left, 96)):
            amount = (place - 32 * g) % LANES
            parts.append(pltpu.roll(value, amount, axis=3) if amount else value)
        out[pl.ds(g * each, each)] = jnp.where(
            lane < 32, parts[0],
            jnp.where(lane < 64, parts[1], jnp.where(lane < 96, 0.0, parts[2])),
        )


def coarsest(source, diagonal, edge, rows):
    weight = edge * (RELAX_WEIGHT / diagonal)
    zero = jnp.zeros((1, SUB, LANES), F32)

    def body(i, v):
        total = jnp.concatenate([zero, v[:-1]], axis=0) + jnp.concatenate([v[1:], zero], axis=0)
        sub = lax.broadcasted_iota(jnp.int32, (rows, SUB, LANES), 1)
        total = total + jnp.where(sub == 0, 0.0, pltpu.roll(v, 1, axis=1))
        total = total + jnp.where(sub == SUB - 1, 0.0, pltpu.roll(v, SUB - 1, axis=1))
        total = total + column_sum([v])[0]
        return (1.0 - RELAX_WEIGHT) * v + weight * (total + source)

    v = weight * source
    for i in range(COARSE_SWEEPS - 1):
        v = body(i, v)
    return v


def zero_rim(ref, rows, halves):
    if halves == 2:
        zero = jnp.zeros((2,) + ref.shape[2:], F32)
        ref[:, 0] = zero
        ref[:, rows + 1] = zero
    else:
        zero = jnp.zeros(ref.shape[1:], F32)
        ref[0] = zero
        ref[rows + 1] = zero


def level_1_down(level, va, vb, packed):
    level.first(va)
    level.relax(va, vb)
    level.relax(vb, va)
    level.relax(va, vb)
    pack_level_2(level.defect_pairs(vb), packed, 0)


def coarse_part(tiles, shift_tiles, s_ref, rows2, refs):
    va, vb, b2, sh2, w2 = refs
    has_left, has_right, even = s_ref[2], s_ref[3], s_ref[5] == 1
    each = rows2 // 4
    unpack_level_2(*tiles, even, 0, each, b2)
    unpack_level_2(*shift_tiles, even, each, each, sh2)
    for ref in (va, vb):
        zero_rim(ref, rows2, 1)
    level = Coarse(b2, w2, sh2, rows2, rows2)
    level.set_weight(edge_mask(2, has_left, has_right))
    level.first(va)
    level.relax(va, vb)
    level.relax(vb, va)
    level.relax(va, vb)

    into = matrix_of(
        lambda a, b: b == jnp.where(a < 64, lax.div(a, 2), 64 + lax.div(a, 2)), 0.5
    )
    rows3 = rows2 // 2

    def to_level_3(pairs):
        flat = jnp.stack(pairs).reshape(rows3 * SUB, LANES)
        return dot(flat, into).reshape(rows3, SUB, LANES)

    shift_3 = to_level_3(level.shift_pairs())
    source_3 = to_level_3(level.defect_pairs(vb))
    e3 = coarsest(source_3, 6.0 + shift_3, edge_mask(3, has_left, has_right), rows3)
    out_of = matrix_of(
        lambda a, b: a == jnp.where(b < 64, lax.div(b, 2), 64 + lax.div(b, 2))
    )
    spread = dot(e3.reshape(rows3 * SUB, LANES), out_of).reshape(rows3, SUB, LANES)
    for row in range(rows2):
        vb[row + 1] = vb[row + 1] + spread[row // 2][None]
    for _ in range(SWEEPS // 2):
        level.relax(vb, va)
        level.relax(va, vb)
    return vb


def level_1_up(level, e2, rows2, u1, va, vb):
    out_of = matrix_of(
        lambda a, b: a == jnp.where(b < 96, lax.div(b, 2), 64 + lax.div(b, 2))
    )
    flat = e2[pl.ds(1, rows2)].reshape(rows2 * 2 * SUB, LANES)
    spread = dot(flat, out_of).reshape(rows2, 2, SUB, LANES)
    for row in range(2 * rows2):
        e = spread[row // 2]
        for z in range(4):
            va[row + 1, z] = u1[row, z] + e[z // 2]
    for _ in range(SWEEPS // 2):
        level.relax(va, vb)
        level.relax(vb, va)


def add_to_fine(e1, target, first_pair, pairs):
    def body(first, count):
        for k in range(count):
            e = e1[first_pair + first + k + 1]
            twice = jnp.stack([e[z // 2] for z in range(8)])
            for h in range(2):
                for m in range(2):
                    row = 2 * (first + k) + m + 1
                    target[h, row] = target[h, row] + twice

    over_rows(0, pairs, 4, body)


def interior(ref, rows):
    return ref.at[:, pl.ds(1, rows)]


def first_columns(shape):
    return lax.rem(lax.div(lanes_iota(shape), 32), 2) == 0


def pack_kernel(s_ref, right_side, terrain, own, first_out, second_out):
    even = s_ref[5] == 1
    apart = matrix_of(lambda a, b: b == lax.div(a, 2) + 64 * lax.rem(a, 2))
    heights = terrain[pl.ds(0, TILE_ROWS), :]
    for z in range(1, 32):
        heights = heights + terrain[pl.ds(TILE_ROWS * z, TILE_ROWS), :]
    heights = dot(heights.astype(F32), apart)
    own[0, 32] = heights
    own[1, 32] = heights
    heights = pltpu.roll(heights, 64, axis=1)
    first_out[32] = heights
    second_out[32] = heights
    first = first_columns((4, SUB, LANES))
    for r in range(TILE_ROWS):
        layers = [
            right_side[pl.ds(zz * TILE_ROWS + r, SUB, stride=8 * TILE_ROWS), :] for zz in range(8)
        ]
        value = dot(jnp.concatenate(layers, axis=0), apart).reshape(8, SUB, LANES)
        own[r // 4, pl.ds(8 * (r % 4), 8)] = value
        value = pltpu.roll(value, 64, axis=2)
        low, high = value[:4], value[4:]
        to_left = jnp.where(first, low, pltpu.roll(high, 32, axis=2))
        to_right = jnp.where(first, pltpu.roll(high, 96, axis=2), low)
        first_out[pl.ds(4 * r, 4)] = jnp.where(even, to_left, to_right)
        second_out[pl.ds(4 * r, 4)] = jnp.where(even, to_right, to_left)


def down_kernel(rows, s_ref, *refs):
    tiles, refs = refs[:20], refs[20:]
    (u0, source_out, weight_out, height_out, u1, b1, sh1, packed,
     source, weight, height, own, beside, heights, va0, vb0, va1, vb1, w1, sems) = refs
    has_left, has_right = s_ref[2], s_ref[3]
    chips = rows // (2 * TILE_ROWS)
    me = lax.div(s_ref[4], TILE_ROWS)
    z, core = lax.div(me, 2), lax.rem(me, 2)

    def device(step, other):
        return 2 * lax.rem(z + step + chips, chips) + (1 - core if other else core)

    copies = []

    def start_copy(source_ref, target_ref):
        copies.append(pltpu.make_async_copy(source_ref, target_ref, sems.at[len(copies)]))

    for kind in range(2):
        for other in range(2):
            w, a, b, c0, c1 = tiles[10 * kind + 5 * other:10 * kind + 5 * other + 5]
            pieces = [(ref.at[part], device(step, other), part)
                      for ref, step in ((w, 0), (a, -1), (b, 1)) for part in range(2)]
            pieces += [(c0, device(2, other), 0), (c1, device(2, other), 1)]
            for ref, dev, part in pieces:
                target = own.at[2 * dev + part] if kind == 0 else beside.at[part, dev]
                start_copy(ref.at[pl.ds(0, 32)], target)
                if part == 0:
                    start_copy(ref.at[32], heights.at[kind, dev])
    for copy in copies:
        copy.start()
    for ref in (va0, vb0):
        zero_rim(ref, rows, 2)
    for ref in (va1, vb1):
        zero_rim(ref, rows // 2, 1)
    for copy in copies:
        copy.wait()

    edge = edge_mask(0, has_left, has_right)
    fine = Fine(source, weight, height)
    lane = lanes_iota((8, SUB, LANES))
    low = lane < 64

    def halves(own_value, beside_value, low):
        even = jnp.where(low, own_value, beside_value)
        odd = jnp.where(low, beside_value, own_value)
        return even, pltpu.roll(odd, 64, axis=odd.ndim - 1)

    first = first_columns((4, SUB, LANES))

    def assemble(dev, carry):
        tall = halves(heights[0, dev], heights[1, dev], low[0])
        for r in range(TILE_ROWS):
            row = TILE_ROWS * dev + r
            upper = beside[1, dev, pl.ds(4 * r, 4)]
            upper = jnp.where(first, pltpu.roll(upper, 96, axis=2), pltpu.roll(upper, 32, axis=2))
            side = jnp.concatenate([beside[0, dev, pl.ds(4 * r, 4)], upper], axis=0)
            both = halves(own[2 * dev + r // 4, pl.ds(8 * (r % 4), 8)], side, low)
            for h in range(2):
                source[h, row] = both[h]
                height[h, row] = jnp.broadcast_to(tall[h][r:r + 1], (SUB, LANES))
                now = edge * jnp.where(
                    fine.ground(row, h), RELAX_WEIGHT / D_TERRAIN, RELAX_WEIGHT / D_AIR
                )
                weight[h, row] = now
                va0[h, row + 1] = now * both[h]
        return carry

    lax.fori_loop(0, rows // TILE_ROWS, assemble, 0)
    saves = [
        pltpu.make_async_copy(source, source_out, sems.at[1]),
        pltpu.make_async_copy(weight, weight_out, sems.at[2]),
        pltpu.make_async_copy(height, height_out, sems.at[3]),
    ]
    for save in saves:
        save.start()
    fine.coarse_shift(rows, sh1)
    fine.relax(va0, vb0, 0, rows, 16)
    fine.relax(vb0, va0, 0, rows, 16)
    fine.relax(va0, vb0, 0, rows, 16)
    saves.append(pltpu.make_async_copy(interior(vb0, rows), u0, sems.at[0]))
    saves[-1].start()
    fine.restricted_defect(vb0, rows, b1)
    level = Coarse(b1, w1, sh1, rows // 2, 16)
    level.set_weight(edge_mask(1, has_left, has_right))
    level_1_down(level, va1, vb1, packed)
    pack_level_2(level.shift_pairs(), packed, rows // 16)
    u1[...] = vb1[pl.ds(1, rows // 2)]
    for save in saves:
        save.wait()


def middle_kernel(rows, s_ref, source_in, weight_in, height_in, u0, u1, b1, sh1, own, second, first,
                  u0_out, u1_out, b1_out, packed,
                  source, weight, height, va0, vb0, va1, vb1, w1, va2, vb2, b2, sh2, w2, sems):
    has_left, has_right = s_ref[2], s_ref[3]
    copies = [
        pltpu.make_async_copy(u0, interior(va0, rows), sems.at[0]),
        pltpu.make_async_copy(source_in, source, sems.at[1]),
        pltpu.make_async_copy(weight_in, weight, sems.at[2]),
        pltpu.make_async_copy(height_in, height, sems.at[3]),
    ]
    for copy in copies:
        copy.start()
    for ref in (va1, vb1):
        zero_rim(ref, rows // 2, 1)
    e2 = coarse_part((own, first, second), (own, first, second), s_ref, rows // 4,
                     (va2, vb2, b2, sh2, w2))
    level = Coarse(b1, w1, sh1, rows // 2, 16)
    level.set_weight(edge_mask(1, has_left, has_right))
    level_1_up(level, e2, rows // 4, u1, va1, vb1)
    for ref in (va0, vb0):
        zero_rim(ref, rows, 2)
    for copy in copies:
        copy.wait()
    fine = Fine(source, weight, height)
    add_to_fine(va1, va0, 0, rows // 2)
    for _ in range(SWEEPS):
        fine.relax(va0, vb0, 0, rows, 8)
        fine.relax(vb0, va0, 0, rows, 8)
    save = pltpu.make_async_copy(interior(va0, rows), u0_out, sems.at[0])
    save.start()
    fine.restricted_defect(va0, rows, b1_out)
    level = Coarse(b1_out, w1, sh1, rows // 2, 16)
    level_1_down(level, va1, vb1, packed)
    u1_out[...] = vb1[pl.ds(1, rows // 2)]
    save.wait()


def last_kernel(rows, s_ref, source_in, weight_in, u0, u1, b1, sh1,
                own, second, first, own_s, second_s, first_s,
                out, source, weight, va0, vb0, va1, vb1, w1, va2, vb2, b2, sh2, w2, sems):
    start, has_left, has_right, mine = s_ref[1], s_ref[2], s_ref[3], s_ref[4]
    window = pl.ds(start, WINDOW)
    copies = [
        pltpu.make_async_copy(u0.at[:, window], interior(va0, WINDOW), sems.at[0]),
        pltpu.make_async_copy(source_in.at[:, window], source, sems.at[1]),
        pltpu.make_async_copy(weight_in.at[:, window], weight, sems.at[2]),
    ]
    for copy in copies:
        copy.start()
    for ref in (va1, vb1):
        zero_rim(ref, rows // 2, 1)
    e2 = coarse_part((own, first, second), (own_s, first_s, second_s), s_ref, rows // 4,
                     (va2, vb2, b2, sh2, w2))
    level = Coarse(b1, w1, sh1, rows // 2, 16)
    level.set_weight(edge_mask(1, has_left, has_right))
    level_1_up(level, e2, rows // 4, u1, va1, vb1)
    for ref in (va0, vb0):
        zero_rim(ref, WINDOW, 2)
    for copy in copies:
        copy.wait()
    fine = Fine(source, weight, None)
    add_to_fine(va1, va0, lax.div(start, 2), WINDOW // 2)
    src, dst = va0, vb0
    for k in range(SWEEPS):
        reach = SWEEPS - 1 - k
        count = TILE_ROWS + 2 * reach
        first = jnp.clip(mine - start - reach, 0, WINDOW - count)
        fine.relax(src, dst, first, count, count)
        src, dst = dst, src
    together = [
        matrix_of(lambda a, b, h=h: (a < 64) & (b == 2 * a + h)) for h in range(2)
    ]
    for r in range(TILE_ROWS):
        row = mine - start + r + 1
        value = 0.0
        for h in range(2):
            value = value + dot(src[h, row].reshape(8 * SUB, LANES), together[h])
        for zz in range(8):
            out[pl.ds(zz * TILE_ROWS + r, SUB, stride=8 * TILE_ROWS), :] = (
                value[SUB * zz:SUB * (zz + 1)]
            )


def spec(space=pltpu.VMEM):
    return pl.BlockSpec(memory_space=space)


def params():
    return pltpu.CompilerParams(vmem_limit_bytes=VMEM_LIMIT)


def shape(*dims):
    return jax.ShapeDtypeStruct(dims + (SUB, LANES), F32)


def vmem(*dims):
    return pltpu.VMEM(dims + (SUB, LANES), F32)


def level_1_scratch(rows):
    return [vmem(rows // 2 + 2, 4), vmem(rows // 2 + 2, 4), vmem(rows // 2, 4)]


def level_2_scratch(rows):
    return [vmem(rows // 4 + 2, 2)] * 2 + [vmem(rows // 4, 2)] * 3


def per_device(right_side, terrain):
    gx, gy = lax.axis_size("gx"), lax.axis_size("gy")
    rows = TILE_ROWS * gx
    i, j = lax.axis_index("gx"), lax.axis_index("gy")
    mine = TILE_ROWS * i
    start = jnp.clip(mine - 4, 0, rows - WINDOW)
    even = 1 - lax.rem(j, 2)
    scalars = jnp.stack([
        jnp.int32(0), start, (j > 0).astype(jnp.int32), (j < gy - 1).astype(jnp.int32), mine, even
    ])

    def swaps(begin):
        pairs = [(k, k + 1) for k in range(begin, gy - 1, 2)]
        return pairs + [(b, a) for a, b in pairs]

    def exchange(first_out, second_out):
        first = lax.ppermute(first_out, "gy", swaps(1))
        second = lax.ppermute(second_out, "gy", swaps(0))
        return first, second

    smem, hbm = spec(pltpu.SMEM), spec(pl.ANY)
    flat = LAYERS * TILE_ROWS
    own, first_out, second_out = pl.pallas_call(
        pack_kernel,
        out_shape=(shape(2, 33), shape(33), shape(33)),
        in_specs=[smem] + [spec()] * 2, out_specs=(spec(),) * 3, name="pack",
    )(scalars, right_side.reshape(flat, LANES), terrain.reshape(flat, LANES))
    first, second = exchange(first_out, second_out)

    up = [(k, (k + 2) % gx) for k in range(gx)]
    down = [(k, (k - 2) % gx) for k in range(gx)]
    swap = [(k, k ^ 1) for k in range(gx)]

    def gather_rows(tile):
        below = lax.ppermute(tile, "gx", up)
        above = lax.ppermute(tile, "gx", down)
        tile_s = lax.ppermute(tile, "gx", swap)
        far_0 = lax.ppermute(below[0], "gx", up)
        far_1 = lax.ppermute(above[1], "gx", down)
        below_s = lax.ppermute(below, "gx", swap)
        above_s = lax.ppermute(above, "gx", swap)
        far_0_s = lax.ppermute(far_0, "gx", swap)
        far_1_s = lax.ppermute(far_1, "gx", swap)
        return (tile, below, above, far_0, far_1, tile_s, below_s, above_s, far_0_s, far_1_s)

    is_last = first_columns((1, 1, LANES)) != (even == 1)
    halo = jnp.stack([jnp.where(is_last, first, second), jnp.where(is_last, second, first)])
    tiles = gather_rows(own) + gather_rows(halo)

    each = rows // 16
    level_0, level_1 = shape(2, rows, 8), shape(rows // 2, 4)
    fine_rows = [vmem(2, rows + 2, 8)] * 2
    u0, source, weight, height, u1, b1, sh1, packed = pl.pallas_call(
        lambda *refs: down_kernel(rows, *refs),
        out_shape=(level_0, level_0, level_0, shape(2, rows), level_1, level_1, level_1,
                   shape(2 * each, 2)),
        in_specs=[smem] + [hbm] * 20, out_specs=(hbm,) * 4 + (spec(),) * 4,
        scratch_shapes=[vmem(2, rows, 8), vmem(2, rows, 8), vmem(2, rows),
                        vmem(2 * gx, 32), vmem(2, gx, 32), vmem(2, gx)]
        + fine_rows + level_1_scratch(rows) + [pltpu.SemaphoreType.DMA((48,))],
        compiler_params=params(), name="down",
    )(scalars, *tiles)

    first, second = exchange(packed, packed)
    u0, u1, b1, packed_2 = pl.pallas_call(
        lambda *refs: middle_kernel(rows, *refs),
        out_shape=(level_0, level_1, level_1, shape(each, 2)),
        in_specs=[smem] + [hbm] * 4 + [spec()] * 6, out_specs=(hbm,) + (spec(),) * 3,
        scratch_shapes=[vmem(2, rows, 8), vmem(2, rows, 8), vmem(2, rows)]
        + fine_rows + level_1_scratch(rows) + level_2_scratch(rows)
        + [pltpu.SemaphoreType.DMA((4,))],
        compiler_params=params(), name="middle",
    )(scalars, source, weight, height, u0, u1, b1, sh1, packed, second, first)

    first_2, second_2 = exchange(packed_2, packed_2)
    out = pl.pallas_call(
        lambda *refs: last_kernel(rows, *refs),
        out_shape=jax.ShapeDtypeStruct((flat, LANES), F32),
        in_specs=[smem] + [hbm] * 3 + [spec()] * 9, out_specs=spec(),
        scratch_shapes=[vmem(2, WINDOW, 8), vmem(2, WINDOW, 8)]
        + [vmem(2, WINDOW + 2, 8)] * 2 + level_1_scratch(rows) + level_2_scratch(rows)
        + [pltpu.SemaphoreType.DMA((3,))],
        compiler_params=params(), name="last",
    )(scalars, source, weight, u0, u1, b1, sh1,
      packed_2, second_2, first_2, packed, second, first)
    return out.reshape(LAYERS, TILE_ROWS, LANES)


def solution(mesh):
    in_specs = (P(None, "gx", "gy"), P(None, "gx", "gy"))
    out_specs = P(None, "gx", "gy")
    return jax.shard_map(
        per_device, mesh=mesh, in_specs=in_specs, out_specs=out_specs, check_vma=False
    )
```

```python
import jax
import jax.numpy as jnp
from jax import lax
from jax.experimental import pallas as pl
from jax.experimental.pallas import tpu as pltpu
from jax.sharding import PartitionSpec as P

SWEEPS = 4
COARSE_SWEEPS = 8
RELAX_WEIGHT = 0.8
TERRAIN_PENALTY = 0.05

F32 = jnp.float32
LANES = 128
SUB = 8
LAYERS = 64
TILE_ROWS = 8
WINDOW = 16
VMEM_LIMIT = 56 * 1024 * 1024

D_AIR = 6.0
D_TERRAIN = 6.0 + TERRAIN_PENALTY


def lanes_iota(shape):
    return lax.broadcasted_iota(jnp.int32, shape, len(shape) - 1)


def edge_mask(level, has_left, has_right):
    lane = lanes_iota((1, LANES))
    zero = jnp.zeros((1, LANES), F32)
    left = zero + has_left.astype(F32)
    right = zero + has_right.astype(F32)
    if level < 2:
        return jnp.where(lane < 64, 1.0, jnp.where(lane < 96, right, left))
    if level == 2:
        return jnp.where(
            lane < 32, 1.0, jnp.where(lane < 64, right, jnp.where(lane < 96, 0.0, left))
        )
    return jnp.where(
        lane < 16, 1.0, jnp.where(lane < 32, right, jnp.where(lane < 112, 0.0, left))
    )


def dot(values, matrix):
    return lax.dot_general(
        values, matrix, (((1,), (0,)), ((), ())),
        precision=lax.Precision.HIGHEST, preferred_element_type=F32,
    )


def matrix_of(rule, value=1.0):
    row = lax.broadcasted_iota(jnp.int32, (LANES, LANES), 0)
    col = lax.broadcasted_iota(jnp.int32, (LANES, LANES), 1)
    return jnp.where(rule(row, col), value, 0.0).astype(F32)


def layer_sum(v):
    count = v.shape[0]
    sub = lax.broadcasted_iota(jnp.int32, (1, SUB, LANES), 1)
    below = jnp.where(sub == 0, 0.0, pltpu.roll(v[count - 1:], 1, axis=1))
    above = jnp.where(sub == SUB - 1, 0.0, pltpu.roll(v[:1], SUB - 1, axis=1))
    if count == 1:
        return below + above
    return jnp.concatenate([below, v[:-1]], axis=0) + jnp.concatenate([v[1:], above], axis=0)


def column_sum(parts):
    if len(parts) == 1:
        v = parts[0]
        return [pltpu.roll(v, 1, axis=2) + pltpu.roll(v, LANES - 1, axis=2)]
    even, odd = parts
    return [odd + pltpu.roll(odd, 1, axis=2), even + pltpu.roll(even, LANES - 1, axis=2)]


def stencil_group(load, first, count, emit):
    before, centre = load(first - 1), load(first)
    for k in range(count):
        after = load(first + k + 1)
        sides = column_sum(centre)
        pairs = []
        for h, v in enumerate(centre):
            total = before[h] + after[h]
            pairs.append((v, total + layer_sum(v) + sides[h]))
        emit(first + k, pairs)
        before, centre = centre, after


def over_rows(start, rows, group, body):
    if isinstance(rows, int) and rows <= group:
        body(start, rows)
        return

    def step(i, carry):
        body(start + i * group, group)
        return carry

    lax.fori_loop(0, rows // group, step, 0)


class Fine:
    def __init__(self, source, weight, height):
        self.source, self.weight, self.height = source, weight, height

    @staticmethod
    def loader(src):
        return lambda row: [src[h, row + 1] for h in range(2)]

    def ground(self, row, h):
        layer = (
            8 * lax.broadcasted_iota(jnp.int32, (8, SUB, LANES), 1)
            + lax.broadcasted_iota(jnp.int32, (8, SUB, LANES), 0)
        ).astype(F32)
        return layer < self.height[h, row][None]

    def relax(self, src, dst, start, rows, group, together=1):
        sub = lax.broadcasted_iota(jnp.int32, (1, SUB, LANES), 1)

        def body(first, count):
            for z in (0, 4):
                chunk = pl.ds(z, 4)

                def load(row):
                    return [src[h, row + 1, chunk] for h in range(2)]

                before, centre = load(first - 1), load(first)
                pending = []
                for k in range(count):
                    row = first + k
                    after = load(row + 1)
                    sides = column_sum(centre)
                    for h, v in enumerate(centre):
                        if z == 0:
                            below = pltpu.roll(src[h, row + 1, pl.ds(7, 1)], 1, axis=1)
                            below = jnp.where(sub == 0, 0.0, below)
                            above = src[h, row + 1, pl.ds(4, 1)]
                        else:
                            below = src[h, row + 1, pl.ds(3, 1)]
                            above = pltpu.roll(src[h, row + 1, pl.ds(0, 1)], SUB - 1, axis=1)
                            above = jnp.where(sub == SUB - 1, 0.0, above)
                        total = before[h] + after[h] + sides[h]
                        total = total + (
                            jnp.concatenate([below, v[:-1]], axis=0)
                            + jnp.concatenate([v[1:], above], axis=0)
                        )
                        total = total + self.source[h, row, chunk]
                        new = (1.0 - RELAX_WEIGHT) * v + self.weight[h, row, chunk] * total
                        pending.append((h, row, new))
                    before, centre = centre, after
                    if (k + 1) % together == 0 or k == count - 1:
                        for h, row, new in pending:
                            dst[h, row + 1, chunk] = new
                        pending = []

        over_rows(start, rows, group, body)

    def restricted_defect(self, src, rows, out):
        load = self.loader(src)

        def body(first, count):
            sums = []

            def emit(row, pairs):
                total = 0.0
                for h, (v, near) in enumerate(pairs):
                    diagonal = jnp.where(self.ground(row, h), D_TERRAIN, D_AIR)
                    total = total + (self.source[h, row] + near - diagonal * v)
                sums.append(total)

            stencil_group(load, first, count, emit)
            for k in range(count // 2):
                both = sums[2 * k] + sums[2 * k + 1]
                for z in range(4):
                    out[lax.div(first, 2) + k, z] = 0.5 * (both[2 * z] + both[2 * z + 1])

        over_rows(0, rows, 8, body)

    def coarse_shift(self, rows, out):
        base = (
            8 * lax.broadcasted_iota(jnp.int32, (4, SUB, LANES), 1)
            + 2 * lax.broadcasted_iota(jnp.int32, (4, SUB, LANES), 0)
        ).astype(F32)

        def body(first, count):
            for k in range(count):
                total = 0.0
                for h in range(2):
                    for m in range(2):
                        height = self.height[h, 2 * (first + k) + m][None]
                        total = total + jnp.clip(height - base, 0.0, 2.0)
                out[first + k] = (0.5 * TERRAIN_PENALTY) * total

        over_rows(0, rows // 2, 4, body)


class Coarse:
    def __init__(self, source, weight, shift_now, rows, group):
        self.source, self.weight, self.shift_now = source, weight, shift_now
        self.rows, self.group = rows, group

    def set_weight(self, edge):
        def body(first, count):
            for k in range(count):
                self.weight[first + k] = edge * (RELAX_WEIGHT / (6.0 + self.shift_now[first + k]))

        over_rows(0, self.rows, self.group, body)

    def first(self, dst):
        def body(first, count):
            for k in range(count):
                dst[first + k + 1] = self.weight[first + k] * self.source[first + k]

        over_rows(0, self.rows, self.group, body)

    def relax(self, src, dst):
        def emit(row, pairs):
            v, total = pairs[0]
            total = total + self.source[row]
            dst[row + 1] = (1.0 - RELAX_WEIGHT) * v + self.weight[row] * total

        load = lambda row: [src[row + 1]]
        over_rows(0, self.rows, self.group,
                  lambda first, count: stencil_group(load, first, count, emit))

    def defect_pairs(self, src):
        sums = []

        def emit(row, pairs):
            v, total = pairs[0]
            sums.append(self.source[row] + total - (6.0 + self.shift_now[row]) * v)

        stencil_group(lambda row: [src[row + 1]], 0, self.rows, emit)
        return pair_up(sums)

    def shift_pairs(self):
        return pair_up([self.shift_now[row] for row in range(self.rows)])


def pair_up(rows):
    out = []
    for k in range(len(rows) // 2):
        both = rows[2 * k] + rows[2 * k + 1]
        out.append(jnp.stack([both[2 * z] + both[2 * z + 1] for z in range(both.shape[0] // 2)]))
    return out


def pack_level_2(pairs, out, offset):
    into = matrix_of(lambda a, b: (a < 64) & (b == lax.div(a, 2)), 0.5)
    count = len(pairs) // 4
    flat = jnp.stack(pairs).reshape(len(pairs) * 2 * SUB, LANES)
    lanes = dot(flat, into).reshape(4, count, 2, SUB, LANES)
    total = lanes[0]
    for g in range(1, 4):
        total = total + pltpu.roll(lanes[g], 32 * g, axis=3)
    out[pl.ds(offset, count)] = total


def unpack_level_2(own, first, second, even, offset, each, out):
    lane = lanes_iota((each, 2, SUB, LANES))
    held = [ref[pl.ds(offset, each)] for ref in (own, first, second)]
    left = jnp.where(even, held[1], held[2])
    right = jnp.where(even, held[2], held[1])
    for g in range(4):
        parts = []
        for value, place in ((held[0], 0), (right, 32), (left, 96)):
            amount = (place - 32 * g) % LANES
            parts.append(pltpu.roll(value, amount, axis=3) if amount else value)
        out[pl.ds(g * each, each)] = jnp.where(
            lane < 32, parts[0],
            jnp.where(lane < 64, parts[1], jnp.where(lane < 96, 0.0, parts[2])),
        )


def coarsest(source, diagonal, edge, rows):
    weight = edge * (RELAX_WEIGHT / diagonal)
    zero = jnp.zeros((1, SUB, LANES), F32)

    def body(i, v):
        total = jnp.concatenate([zero, v[:-1]], axis=0) + jnp.concatenate([v[1:], zero], axis=0)
        sub = lax.broadcasted_iota(jnp.int32, (rows, SUB, LANES), 1)
        total = total + jnp.where(sub == 0, 0.0, pltpu.roll(v, 1, axis=1))
        total = total + jnp.where(sub == SUB - 1, 0.0, pltpu.roll(v, SUB - 1, axis=1))
        total = total + column_sum([v])[0]
        return (1.0 - RELAX_WEIGHT) * v + weight * (total + source)

    v = weight * source
    for i in range(COARSE_SWEEPS - 1):
        v = body(i, v)
    return v


def zero_rim(ref, rows, halves):
    if halves == 2:
        zero = jnp.zeros((2,) + ref.shape[2:], F32)
        ref[:, 0] = zero
        ref[:, rows + 1] = zero
    else:
        zero = jnp.zeros(ref.shape[1:], F32)
        ref[0] = zero
        ref[rows + 1] = zero


def level_1_down(level, va, vb, packed):
    level.first(va)
    level.relax(va, vb)
    level.relax(vb, va)
    level.relax(va, vb)
    pack_level_2(level.defect_pairs(vb), packed, 0)


def coarse_part(tiles, shift_tiles, at, rows2, refs):
    va, vb, b2, sh2, w2 = refs
    has_left, has_right, even = at.has_left, at.has_right, at.even
    each = rows2 // 4
    unpack_level_2(*tiles, even, 0, each, b2)
    unpack_level_2(*shift_tiles, even, each, each, sh2)
    for ref in (va, vb):
        zero_rim(ref, rows2, 1)
    level = Coarse(b2, w2, sh2, rows2, rows2)
    level.set_weight(edge_mask(2, has_left, has_right))
    level.first(va)
    level.relax(va, vb)
    level.relax(vb, va)
    level.relax(va, vb)

    into = matrix_of(
        lambda a, b: b == jnp.where(a < 64, lax.div(a, 2), 64 + lax.div(a, 2)), 0.5
    )
    rows3 = rows2 // 2

    def to_level_3(pairs):
        flat = jnp.stack(pairs).reshape(rows3 * SUB, LANES)
        return dot(flat, into).reshape(rows3, SUB, LANES)

    shift_3 = to_level_3(level.shift_pairs())
    source_3 = to_level_3(level.defect_pairs(vb))
    e3 = coarsest(source_3, 6.0 + shift_3, edge_mask(3, has_left, has_right), rows3)
    out_of = matrix_of(
        lambda a, b: a == jnp.where(b < 64, lax.div(b, 2), 64 + lax.div(b, 2))
    )
    spread = dot(e3.reshape(rows3 * SUB, LANES), out_of).reshape(rows3, SUB, LANES)
    for row in range(rows2):
        vb[row + 1] = vb[row + 1] + spread[row // 2][None]
    for _ in range(SWEEPS // 2):
        level.relax(vb, va)
        level.relax(va, vb)
    return vb


def level_1_up(level, e2, rows2, u1, va, vb):
    out_of = matrix_of(
        lambda a, b: a == jnp.where(b < 96, lax.div(b, 2), 64 + lax.div(b, 2))
    )
    flat = e2[pl.ds(1, rows2)].reshape(rows2 * 2 * SUB, LANES)
    spread = dot(flat, out_of).reshape(rows2, 2, SUB, LANES)
    for row in range(2 * rows2):
        e = spread[row // 2]
        for z in range(4):
            va[row + 1, z] = u1[row, z] + e[z // 2]
    for _ in range(SWEEPS // 2):
        level.relax(va, vb)
        level.relax(vb, va)


def add_to_fine(e1, target, first_pair, pairs):
    def body(first, count):
        for k in range(count):
            e = e1[first_pair + first + k + 1]
            twice = jnp.stack([e[z // 2] for z in range(8)])
            for h in range(2):
                for m in range(2):
                    row = 2 * (first + k) + m + 1
                    target[h, row] = target[h, row] + twice

    over_rows(0, pairs, 4, body)


def interior(ref, rows):
    return ref.at[:, pl.ds(1, rows)]


def first_columns(shape):
    return lax.rem(lax.div(lanes_iota(shape), 32), 2) == 0


def pack_kernel(s_ref, right_side, terrain, own, first_out, second_out):
    even = Place(s_ref).even
    apart = matrix_of(lambda a, b: b == lax.div(a, 2) + 64 * lax.rem(a, 2))
    heights = terrain[pl.ds(0, TILE_ROWS), :]
    for z in range(1, 32):
        heights = heights + terrain[pl.ds(TILE_ROWS * z, TILE_ROWS), :]
    heights = dot(heights.astype(F32), apart)
    own[0, 32] = heights
    own[1, 32] = heights
    heights = pltpu.roll(heights, 64, axis=1)
    first_out[32] = heights
    second_out[32] = heights
    first = first_columns((4, SUB, LANES))
    for r in range(TILE_ROWS):
        layers = [
            right_side[pl.ds(zz * TILE_ROWS + r, SUB, stride=8 * TILE_ROWS), :] for zz in range(8)
        ]
        value = dot(jnp.concatenate(layers, axis=0), apart).reshape(8, SUB, LANES)
        own[r // 4, pl.ds(8 * (r % 4), 8)] = value
        value = pltpu.roll(value, 64, axis=2)
        low, high = value[:4], value[4:]
        to_left = jnp.where(first, low, pltpu.roll(high, 32, axis=2))
        to_right = jnp.where(first, pltpu.roll(high, 96, axis=2), low)
        first_out[pl.ds(4 * r, 4)] = jnp.where(even, to_left, to_right)
        second_out[pl.ds(4 * r, 4)] = jnp.where(even, to_right, to_left)


def down_kernel(rows, s_ref, *refs):
    at = Place(s_ref)
    tiles, refs = refs[:16], refs[16:]
    (u0, source_out, weight_out, height_out, u1, b1, sh1, packed,
     source, weight, height, own, beside, heights, va0, vb0, va1, vb1, w1, sems) = refs
    has_left, has_right = at.has_left, at.has_right
    chips = rows // (2 * TILE_ROWS)
    z, core = at.chip, at.core

    def device(step, other):
        return 2 * lax.rem(z + step + chips, chips) + (1 - core if other else core)

    copies = []

    def start_copy(source_ref, target_ref):
        copies.append(pltpu.make_async_copy(source_ref, target_ref, sems.at[len(copies)]))

    for other in range(2):
        group = tiles[8 * other:8 * other + 8]
        for kind in range(2):
            pieces = [
                (group[3 * kind + n].at[part], device(step, other), part)
                for n, step in enumerate((0, -1, 1)) for part in range(2)
            ]
            pieces += [(group[6 + part].at[kind], device(2, other), part) for part in range(2)]
            for ref, dev, part in pieces:
                target = own.at[2 * dev + part] if kind == 0 else beside.at[part, dev]
                start_copy(ref.at[pl.ds(0, 32)], target)
                if part == 0:
                    start_copy(ref.at[32], heights.at[kind, dev])
    for copy in copies:
        copy.start()
    for ref in (va0, vb0):
        zero_rim(ref, rows, 2)
    for ref in (va1, vb1):
        zero_rim(ref, rows // 2, 1)
    for copy in copies:
        copy.wait()

    edge = edge_mask(0, has_left, has_right)
    fine = Fine(source, weight, height)
    lane = lanes_iota((8, SUB, LANES))
    low = lane < 64

    def halves(own_value, beside_value, low):
        even = jnp.where(low, own_value, beside_value)
        odd = jnp.where(low, beside_value, own_value)
        return even, pltpu.roll(odd, 64, axis=odd.ndim - 1)

    first = first_columns((4, SUB, LANES))

    def assemble(dev, carry):
        tall = halves(heights[0, dev], heights[1, dev], low[0])
        for r in range(TILE_ROWS):
            row = TILE_ROWS * dev + r
            upper = beside[1, dev, pl.ds(4 * r, 4)]
            upper = jnp.where(first, pltpu.roll(upper, 96, axis=2), pltpu.roll(upper, 32, axis=2))
            side = jnp.concatenate([beside[0, dev, pl.ds(4 * r, 4)], upper], axis=0)
            both = halves(own[2 * dev + r // 4, pl.ds(8 * (r % 4), 8)], side, low)
            for h in range(2):
                source[h, row] = both[h]
                height[h, row] = jnp.broadcast_to(tall[h][r:r + 1], (SUB, LANES))
                now = edge * jnp.where(
                    fine.ground(row, h), RELAX_WEIGHT / D_TERRAIN, RELAX_WEIGHT / D_AIR
                )
                weight[h, row] = now
                va0[h, row + 1] = now * both[h]
        return carry

    lax.fori_loop(0, rows // TILE_ROWS, assemble, 0)
    saves = [
        pltpu.make_async_copy(source, source_out, sems.at[1]),
        pltpu.make_async_copy(weight, weight_out, sems.at[2]),
        pltpu.make_async_copy(height, height_out, sems.at[3]),
    ]
    for save in saves:
        save.start()
    fine.coarse_shift(rows, sh1)
    fine.relax(va0, vb0, 0, rows, 8, 4)
    fine.relax(vb0, va0, 0, rows, 8, 4)
    fine.relax(va0, vb0, 0, rows, 8, 4)
    saves.append(pltpu.make_async_copy(interior(vb0, rows), u0, sems.at[0]))
    saves[-1].start()
    fine.restricted_defect(vb0, rows, b1)
    level = Coarse(b1, w1, sh1, rows // 2, 16)
    level.set_weight(edge_mask(1, has_left, has_right))
    level_1_down(level, va1, vb1, packed)
    pack_level_2(level.shift_pairs(), packed, rows // 16)
    u1[...] = vb1[pl.ds(1, rows // 2)]
    for save in saves:
        save.wait()


def middle_kernel(rows, s_ref, source_in, weight_in, height_in, u0, u1, b1, sh1, own, second, first,
                  u0_out, u1_out, b1_out, packed,
                  source, weight, height, va0, vb0, va1, vb1, w1, va2, vb2, b2, sh2, w2, sems):
    at = Place(s_ref)
    has_left, has_right = at.has_left, at.has_right
    copies = [
        pltpu.make_async_copy(u0, interior(va0, rows), sems.at[0]),
        pltpu.make_async_copy(source_in, source, sems.at[1]),
        pltpu.make_async_copy(weight_in, weight, sems.at[2]),
        pltpu.make_async_copy(height_in, height, sems.at[3]),
    ]
    for copy in copies:
        copy.start()
    for ref in (va1, vb1):
        zero_rim(ref, rows // 2, 1)
    e2 = coarse_part((own, first, second), (own, first, second), at, rows // 4,
                     (va2, vb2, b2, sh2, w2))
    level = Coarse(b1, w1, sh1, rows // 2, 16)
    level.set_weight(edge_mask(1, has_left, has_right))
    level_1_up(level, e2, rows // 4, u1, va1, vb1)
    for ref in (va0, vb0):
        zero_rim(ref, rows, 2)
    for copy in copies:
        copy.wait()
    fine = Fine(source, weight, height)
    add_to_fine(va1, va0, 0, rows // 2)
    for _ in range(SWEEPS):
        fine.relax(va0, vb0, 0, rows, 8)
        fine.relax(vb0, va0, 0, rows, 8)
    save = pltpu.make_async_copy(interior(va0, rows), u0_out, sems.at[0])
    save.start()
    fine.restricted_defect(va0, rows, b1_out)
    level = Coarse(b1_out, w1, sh1, rows // 2, 16)
    level_1_down(level, va1, vb1, packed)
    u1_out[...] = vb1[pl.ds(1, rows // 2)]
    save.wait()


def last_kernel(rows, s_ref, source_in, weight_in, u0, u1, b1, sh1,
                own, second, first, own_s, second_s, first_s,
                out, source, weight, va0, vb0, va1, vb1, w1, va2, vb2, b2, sh2, w2, sems):
    at = Place(s_ref)
    start, has_left, has_right, mine = at.start, at.has_left, at.has_right, at.mine
    window = pl.ds(start, WINDOW)
    copies = [
        pltpu.make_async_copy(u0.at[:, window], interior(va0, WINDOW), sems.at[0]),
        pltpu.make_async_copy(source_in.at[:, window], source, sems.at[1]),
        pltpu.make_async_copy(weight_in.at[:, window], weight, sems.at[2]),
    ]
    for copy in copies:
        copy.start()
    for ref in (va1, vb1):
        zero_rim(ref, rows // 2, 1)
    e2 = coarse_part((own, first, second), (own_s, first_s, second_s), at, rows // 4,
                     (va2, vb2, b2, sh2, w2))
    level = Coarse(b1, w1, sh1, rows // 2, 16)
    level.set_weight(edge_mask(1, has_left, has_right))
    level_1_up(level, e2, rows // 4, u1, va1, vb1)
    for ref in (va0, vb0):
        zero_rim(ref, WINDOW, 2)
    for copy in copies:
        copy.wait()
    fine = Fine(source, weight, None)
    add_to_fine(va1, va0, lax.div(start, 2), WINDOW // 2)
    src, dst = va0, vb0
    for k in range(SWEEPS):
        reach = SWEEPS - 1 - k
        count = TILE_ROWS + 2 * reach
        first = jnp.clip(mine - start - reach, 0, WINDOW - count)
        fine.relax(src, dst, first, count, count)
        src, dst = dst, src
    together = [
        matrix_of(lambda a, b, h=h: (a < 64) & (b == 2 * a + h)) for h in range(2)
    ]
    for r in range(TILE_ROWS):
        row = mine - start + r + 1
        value = 0.0
        for h in range(2):
            value = value + dot(src[h, row].reshape(8 * SUB, LANES), together[h])
        for zz in range(8):
            out[pl.ds(zz * TILE_ROWS + r, SUB, stride=8 * TILE_ROWS), :] = (
                value[SUB * zz:SUB * (zz + 1)]
            )


class Place:
    def __init__(self, s_ref):
        self.start, self.mine, self.chip, self.core = s_ref[0], s_ref[1], s_ref[2], s_ref[3]
        self.has_left, self.has_right, self.even = s_ref[4], s_ref[5], s_ref[6] == 1


def spec(space=pltpu.VMEM):
    return pl.BlockSpec(memory_space=space)


def params():
    return pltpu.CompilerParams(vmem_limit_bytes=VMEM_LIMIT)


def shape(*dims):
    return jax.ShapeDtypeStruct(dims + (SUB, LANES), F32)


def vmem(*dims):
    return pltpu.VMEM(dims + (SUB, LANES), F32)


def level_1_scratch(rows):
    return [vmem(rows // 2 + 2, 4), vmem(rows // 2 + 2, 4), vmem(rows // 2, 4)]


def level_2_scratch(rows):
    return [vmem(rows // 4 + 2, 2)] * 2 + [vmem(rows // 4, 2)] * 3


def per_device(right_side, terrain):
    gx, gy = lax.axis_size("gx"), lax.axis_size("gy")
    rows = TILE_ROWS * gx
    i, j = lax.axis_index("gx"), lax.axis_index("gy")
    mine, even = TILE_ROWS * i, 1 - lax.rem(j, 2)
    scalars = jnp.stack([
        jnp.clip(mine - 4, 0, rows - WINDOW), mine, lax.div(i, 2), lax.rem(i, 2),
        (j > 0).astype(jnp.int32), (j < gy - 1).astype(jnp.int32), even,
    ])

    def swaps(begin):
        pairs = [(k, k + 1) for k in range(begin, gy - 1, 2)]
        return pairs + [(b, a) for a, b in pairs]

    def exchange(first_out, second_out):
        first = lax.ppermute(first_out, "gy", swaps(1))
        second = lax.ppermute(second_out, "gy", swaps(0))
        return first, second

    smem, hbm = spec(pltpu.SMEM), spec(pl.ANY)
    flat = LAYERS * TILE_ROWS
    own, first_out, second_out = pl.pallas_call(
        pack_kernel,
        out_shape=(shape(2, 33), shape(33), shape(33)),
        in_specs=[smem] + [spec()] * 2, out_specs=(spec(),) * 3, name="pack",
    )(scalars, right_side.reshape(flat, LANES), terrain.reshape(flat, LANES))
    first, second = exchange(first_out, second_out)

    up = [(k, (k + 2) % gx) for k in range(gx)]
    down = [(k, (k - 2) % gx) for k in range(gx)]
    swap = [(k, k ^ 1) for k in range(gx)]

    def gather_near(tile):
        below = lax.ppermute(tile, "gx", up)
        above = lax.ppermute(tile, "gx", down)
        return below, above

    def swapped(*arrays):
        return tuple(lax.ppermute(x, "gx", swap) for x in arrays)

    own_near = gather_near(own)

    is_last = first_columns((1, 1, LANES)) != (even == 1)
    halo = jnp.stack([jnp.where(is_last, first, second), jnp.where(is_last, second, first)])
    halo_near = gather_near(halo)
    far = (
        lax.ppermute(jnp.stack([own_near[0][0], halo_near[0][0]]), "gx", up),
        lax.ppermute(jnp.stack([own_near[1][1], halo_near[1][1]]), "gx", down),
    )
    arrays = (own,) + own_near + (halo,) + halo_near + far
    tiles = arrays + swapped(*arrays)

    each = rows // 16
    level_0, level_1 = shape(2, rows, 8), shape(rows // 2, 4)
    fine_rows = [vmem(2, rows + 2, 8)] * 2
    u0, source, weight, height, u1, b1, sh1, packed = pl.pallas_call(
        lambda *refs: down_kernel(rows, *refs),
        out_shape=(level_0, level_0, level_0, shape(2, rows), level_1, level_1, level_1,
                   shape(2 * each, 2)),
        in_specs=[smem] + [hbm] * 16, out_specs=(hbm,) * 4 + (spec(),) * 4,
        scratch_shapes=[vmem(2, rows, 8), vmem(2, rows, 8), vmem(2, rows),
                        vmem(2 * gx, 32), vmem(2, gx, 32), vmem(2, gx)]
        + fine_rows + level_1_scratch(rows) + [pltpu.SemaphoreType.DMA((48,))],
        compiler_params=params(), name="down",
    )(scalars, *tiles)

    first, second = exchange(packed, packed)
    u0, u1, b1, packed_2 = pl.pallas_call(
        lambda *refs: middle_kernel(rows, *refs),
        out_shape=(level_0, level_1, level_1, shape(each, 2)),
        in_specs=[smem] + [hbm] * 4 + [spec()] * 6, out_specs=(hbm,) + (spec(),) * 3,
        scratch_shapes=[vmem(2, rows, 8), vmem(2, rows, 8), vmem(2, rows)]
        + fine_rows + level_1_scratch(rows) + level_2_scratch(rows)
        + [pltpu.SemaphoreType.DMA((4,))],
        compiler_params=params(), name="middle",
    )(scalars, source, weight, height, u0, u1, b1, sh1, packed, second, first)

    first_2, second_2 = exchange(packed_2, packed_2)
    out = pl.pallas_call(
        lambda *refs: last_kernel(rows, *refs),
        out_shape=jax.ShapeDtypeStruct((flat, LANES), F32),
        in_specs=[smem] + [hbm] * 3 + [spec()] * 9, out_specs=spec(),
        scratch_shapes=[vmem(2, WINDOW, 8), vmem(2, WINDOW, 8)]
        + [vmem(2, WINDOW + 2, 8)] * 2 + level_1_scratch(rows) + level_2_scratch(rows)
        + [pltpu.SemaphoreType.DMA((3,))],
        compiler_params=params(), name="last",
    )(scalars, source, weight, u0, u1, b1, sh1,
      packed_2, second_2, first_2, packed, second, first)
    return out.reshape(LAYERS, TILE_ROWS, LANES)


def solution(mesh):
    in_specs = (P(None, "gx", "gy"), P(None, "gx", "gy"))
    out_specs = P(None, "gx", "gy")
    return jax.shard_map(
        per_device, mesh=mesh, in_specs=in_specs, out_specs=out_specs, check_vma=False
    )
```

```python
import jax
import jax.numpy as jnp
from jax import lax
from jax.experimental import pallas as pl
from jax.experimental.pallas import tpu as pltpu
from jax.sharding import PartitionSpec as P

SWEEPS = 4
COARSE_SWEEPS = 8
RELAX_WEIGHT = 0.8
TERRAIN_PENALTY = 0.05

F32 = jnp.float32
LANES = 128
SUB = 8
LAYERS = 64
TILE_ROWS = 8
WINDOW = 16
VMEM_LIMIT = 40 * 1024 * 1024

D_AIR = 6.0
D_TERRAIN = 6.0 + TERRAIN_PENALTY


def lanes_iota(shape):
    return lax.broadcasted_iota(jnp.int32, shape, len(shape) - 1)


def edge_mask(level, has_left, has_right):
    lane = lanes_iota((1, LANES))
    zero = jnp.zeros((1, LANES), F32)
    left = zero + has_left.astype(F32)
    right = zero + has_right.astype(F32)
    if level < 2:
        return jnp.where(lane < 64, 1.0, jnp.where(lane < 96, right, left))
    if level == 2:
        return jnp.where(
            lane < 32, 1.0, jnp.where(lane < 64, right, jnp.where(lane < 96, 0.0, left))
        )
    return jnp.where(
        lane < 16, 1.0, jnp.where(lane < 32, right, jnp.where(lane < 112, 0.0, left))
    )


def dot(values, matrix):
    return lax.dot_general(
        values, matrix, (((1,), (0,)), ((), ())),
        precision=lax.Precision.HIGHEST, preferred_element_type=F32,
    )


def matrix_of(rule, value=1.0):
    row = lax.broadcasted_iota(jnp.int32, (LANES, LANES), 0)
    col = lax.broadcasted_iota(jnp.int32, (LANES, LANES), 1)
    return jnp.where(rule(row, col), value, 0.0).astype(F32)


def layer_sum(v):
    count = v.shape[0]
    sub = lax.broadcasted_iota(jnp.int32, (1, SUB, LANES), 1)
    below = jnp.where(sub == 0, 0.0, pltpu.roll(v[count - 1:], 1, axis=1))
    above = jnp.where(sub == SUB - 1, 0.0, pltpu.roll(v[:1], SUB - 1, axis=1))
    if count == 1:
        return below + above
    return jnp.concatenate([below, v[:-1]], axis=0) + jnp.concatenate([v[1:], above], axis=0)


def column_sum(parts):
    if len(parts) == 1:
        v = parts[0]
        return [pltpu.roll(v, 1, axis=2) + pltpu.roll(v, LANES - 1, axis=2)]
    even, odd = parts
    return [odd + pltpu.roll(odd, 1, axis=2), even + pltpu.roll(even, LANES - 1, axis=2)]


def stencil_group(load, first, count, emit):
    before, centre = load(first - 1), load(first)
    for k in range(count):
        after = load(first + k + 1)
        sides = column_sum(centre)
        pairs = []
        for h, v in enumerate(centre):
            total = before[h] + after[h]
            pairs.append((v, total + layer_sum(v) + sides[h]))
        emit(first + k, pairs)
        before, centre = centre, after


def over_rows(start, rows, group, body):
    if isinstance(rows, int) and rows <= group:
        body(start, rows)
        return

    def step(i, carry):
        body(start + i * group, group)
        return carry

    lax.fori_loop(0, rows // group, step, 0)


class Fine:
    def __init__(self, source, weight, height):
        self.source, self.weight, self.height = source, weight, height

    @staticmethod
    def loader(src):
        return lambda row: [src[h, row + 1] for h in range(2)]

    def ground(self, row, h):
        layer = (
            8 * lax.broadcasted_iota(jnp.int32, (8, SUB, LANES), 1)
            + lax.broadcasted_iota(jnp.int32, (8, SUB, LANES), 0)
        ).astype(F32)
        return layer < self.height[h, row][None]

    def relax(self, src, dst, start, rows, group):
        def emit(row, pairs):
            for h, (v, total) in enumerate(pairs):
                total = total + self.source[h, row]
                dst[h, row + 1] = (1.0 - RELAX_WEIGHT) * v + self.weight[h, row] * total

        over_rows(start, rows, group,
                  lambda first, count: stencil_group(self.loader(src), first, count, emit))

    def restricted_defect(self, src, rows, out):
        load = self.loader(src)

        def body(first, count):
            sums = []

            def emit(row, pairs):
                total = 0.0
                for h, (v, near) in enumerate(pairs):
                    diagonal = jnp.where(self.ground(row, h), D_TERRAIN, D_AIR)
                    total = total + (self.source[h, row] + near - diagonal * v)
                sums.append(total)

            stencil_group(load, first, count, emit)
            for k in range(count // 2):
                both = sums[2 * k] + sums[2 * k + 1]
                for z in range(4):
                    out[lax.div(first, 2) + k, z] = 0.5 * (both[2 * z] + both[2 * z + 1])

        over_rows(0, rows, 8, body)

    def coarse_shift(self, rows, out):
        base = (
            8 * lax.broadcasted_iota(jnp.int32, (4, SUB, LANES), 1)
            + 2 * lax.broadcasted_iota(jnp.int32, (4, SUB, LANES), 0)
        ).astype(F32)

        def body(first, count):
            for k in range(count):
                total = 0.0
                for h in range(2):
                    for m in range(2):
                        height = self.height[h, 2 * (first + k) + m][None]
                        total = total + jnp.clip(height - base, 0.0, 2.0)
                out[first + k] = (0.5 * TERRAIN_PENALTY) * total

        over_rows(0, rows // 2, 4, body)


class Coarse:
    def __init__(self, source, weight, shift_now, rows, group):
        self.source, self.weight, self.shift_now = source, weight, shift_now
        self.rows, self.group = rows, group

    def set_weight(self, edge):
        def body(first, count):
            for k in range(count):
                self.weight[first + k] = edge * (RELAX_WEIGHT / (6.0 + self.shift_now[first + k]))

        over_rows(0, self.rows, self.group, body)

    def first(self, dst):
        def body(first, count):
            for k in range(count):
                dst[first + k + 1] = self.weight[first + k] * self.source[first + k]

        over_rows(0, self.rows, self.group, body)

    def relax(self, src, dst):
        def emit(row, pairs):
            v, total = pairs[0]
            total = total + self.source[row]
            dst[row + 1] = (1.0 - RELAX_WEIGHT) * v + self.weight[row] * total

        load = lambda row: [src[row + 1]]
        over_rows(0, self.rows, self.group,
                  lambda first, count: stencil_group(load, first, count, emit))

    def defect_pairs(self, src):
        sums = []

        def emit(row, pairs):
            v, total = pairs[0]
            sums.append(self.source[row] + total - (6.0 + self.shift_now[row]) * v)

        stencil_group(lambda row: [src[row + 1]], 0, self.rows, emit)
        return pair_up(sums)

    def shift_pairs(self):
        return pair_up([self.shift_now[row] for row in range(self.rows)])


def pair_up(rows):
    out = []
    for k in range(len(rows) // 2):
        both = rows[2 * k] + rows[2 * k + 1]
        out.append(jnp.stack([both[2 * z] + both[2 * z + 1] for z in range(both.shape[0] // 2)]))
    return out


def pack_level_2(pairs, out, offset):
    into = matrix_of(lambda a, b: (a < 64) & (b == lax.div(a, 2)), 0.5)
    count = len(pairs) // 4
    flat = jnp.stack(pairs).reshape(len(pairs) * 2 * SUB, LANES)
    lanes = dot(flat, into).reshape(4, count, 2, SUB, LANES)
    total = lanes[0]
    for g in range(1, 4):
        total = total + pltpu.roll(lanes[g], 32 * g, axis=3)
    out[pl.ds(offset, count)] = total


def unpack_level_2(own, first, second, even, offset, each, out):
    lane = lanes_iota((each, 2, SUB, LANES))
    held = [ref[pl.ds(offset, each)] for ref in (own, first, second)]
    left = jnp.where(even, held[1], held[2])
    right = jnp.where(even, held[2], held[1])
    for g in range(4):
        parts = []
        for value, place in ((held[0], 0), (right, 32), (left, 96)):
            amount = (place - 32 * g) % LANES
            parts.append(pltpu.roll(value, amount, axis=3) if amount else value)
        out[pl.ds(g * each, each)] = jnp.where(
            lane < 32, parts[0],
            jnp.where(lane < 64, parts[1], jnp.where(lane < 96, 0.0, parts[2])),
        )


def coarsest(source, diagonal, edge, rows):
    weight = edge * (RELAX_WEIGHT / diagonal)
    zero = jnp.zeros((1, SUB, LANES), F32)

    def body(i, v):
        total = jnp.concatenate([zero, v[:-1]], axis=0) + jnp.concatenate([v[1:], zero], axis=0)
        sub = lax.broadcasted_iota(jnp.int32, (rows, SUB, LANES), 1)
        total = total + jnp.where(sub == 0, 0.0, pltpu.roll(v, 1, axis=1))
        total = total + jnp.where(sub == SUB - 1, 0.0, pltpu.roll(v, SUB - 1, axis=1))
        total = total + column_sum([v])[0]
        return (1.0 - RELAX_WEIGHT) * v + weight * (total + source)

    v = weight * source
    for i in range(COARSE_SWEEPS - 1):
        v = body(i, v)
    return v


def zero_rim(ref, rows, halves):
    if halves == 2:
        zero = jnp.zeros((2,) + ref.shape[2:], F32)
        ref[:, 0] = zero
        ref[:, rows + 1] = zero
    else:
        zero = jnp.zeros(ref.shape[1:], F32)
        ref[0] = zero
        ref[rows + 1] = zero


def level_1_down(level, va, vb, packed):
    level.first(va)
    level.relax(va, vb)
    level.relax(vb, va)
    level.relax(va, vb)
    pack_level_2(level.defect_pairs(vb), packed, 0)


def coarse_part(tiles, shift_tiles, at, rows2, refs):
    va, vb, b2, sh2, w2 = refs
    has_left, has_right, even = at.has_left, at.has_right, at.even
    each = rows2 // 4
    unpack_level_2(*tiles, even, 0, each, b2)
    unpack_level_2(*shift_tiles, even, each, each, sh2)
    for ref in (va, vb):
        zero_rim(ref, rows2, 1)
    level = Coarse(b2, w2, sh2, rows2, rows2)
    level.set_weight(edge_mask(2, has_left, has_right))
    level.first(va)
    level.relax(va, vb)
    level.relax(vb, va)
    level.relax(va, vb)

    into = matrix_of(
        lambda a, b: b == jnp.where(a < 64, lax.div(a, 2), 64 + lax.div(a, 2)), 0.5
    )
    rows3 = rows2 // 2

    def to_level_3(pairs):
        flat = jnp.stack(pairs).reshape(rows3 * SUB, LANES)
        return dot(flat, into).reshape(rows3, SUB, LANES)

    shift_3 = to_level_3(level.shift_pairs())
    source_3 = to_level_3(level.defect_pairs(vb))
    e3 = coarsest(source_3, 6.0 + shift_3, edge_mask(3, has_left, has_right), rows3)
    out_of = matrix_of(
        lambda a, b: a == jnp.where(b < 64, lax.div(b, 2), 64 + lax.div(b, 2))
    )
    spread = dot(e3.reshape(rows3 * SUB, LANES), out_of).reshape(rows3, SUB, LANES)
    for row in range(rows2):
        vb[row + 1] = vb[row + 1] + spread[row // 2][None]
    for _ in range(SWEEPS // 2):
        level.relax(vb, va)
        level.relax(va, vb)
    return vb


def level_1_up(level, e2, rows2, u1, va, vb):
    out_of = matrix_of(
        lambda a, b: a == jnp.where(b < 96, lax.div(b, 2), 64 + lax.div(b, 2))
    )
    flat = e2[pl.ds(1, rows2)].reshape(rows2 * 2 * SUB, LANES)
    spread = dot(flat, out_of).reshape(rows2, 2, SUB, LANES)
    for row in range(2 * rows2):
        e = spread[row // 2]
        for z in range(4):
            va[row + 1, z] = u1[row, z] + e[z // 2]
    for _ in range(SWEEPS // 2):
        level.relax(va, vb)
        level.relax(vb, va)


def add_to_fine(e1, target, first_pair, pairs):
    def body(first, count):
        for k in range(count):
            e = e1[first_pair + first + k + 1]
            twice = jnp.stack([e[z // 2] for z in range(8)])
            for h in range(2):
                for m in range(2):
                    row = 2 * (first + k) + m + 1
                    target[h, row] = target[h, row] + twice

    over_rows(0, pairs, 4, body)


def interior(ref, rows):
    return ref.at[:, pl.ds(1, rows)]


def first_columns(shape):
    return lax.rem(lax.div(lanes_iota(shape), 32), 2) == 0


def pack_kernel(s_ref, right_side, terrain, own, first_out, second_out):
    even = Place(s_ref).even
    apart = matrix_of(lambda a, b: b == lax.div(a, 2) + 64 * lax.rem(a, 2))
    heights = terrain[pl.ds(0, TILE_ROWS), :]
    for z in range(1, 32):
        heights = heights + terrain[pl.ds(TILE_ROWS * z, TILE_ROWS), :]
    heights = dot(heights.astype(F32), apart)
    own[0, 32] = heights
    own[1, 32] = heights
    heights = pltpu.roll(heights, 64, axis=1)
    first_out[32] = heights
    second_out[32] = heights
    first = first_columns((4, SUB, LANES))
    for r in range(TILE_ROWS):
        layers = [
            right_side[pl.ds(zz * TILE_ROWS + r, SUB, stride=8 * TILE_ROWS), :] for zz in range(8)
        ]
        value = dot(jnp.concatenate(layers, axis=0), apart).reshape(8, SUB, LANES)
        own[r // 4, pl.ds(8 * (r % 4), 8)] = value
        value = pltpu.roll(value, 64, axis=2)
        low, high = value[:4], value[4:]
        to_left = jnp.where(first, low, pltpu.roll(high, 32, axis=2))
        to_right = jnp.where(first, pltpu.roll(high, 96, axis=2), low)
        first_out[pl.ds(4 * r, 4)] = jnp.where(even, to_left, to_right)
        second_out[pl.ds(4 * r, 4)] = jnp.where(even, to_right, to_left)


def down_kernel(rows, s_ref, *refs):
    at = Place(s_ref)
    tiles, refs = refs[:16], refs[16:]
    (u0, source_out, weight_out, height_out, u1, b1, sh1, packed,
     source, weight, height, va0, vb0, va1, vb1, w1, sems) = refs
    has_left, has_right = at.has_left, at.has_right
    chips = rows // (2 * TILE_ROWS)
    z, core = at.chip, at.core

    def device(step, other):
        return 2 * lax.rem(z + step + chips, chips) + (1 - core if other else core)

    for ref in (va0, vb0):
        zero_rim(ref, rows, 2)
    for ref in (va1, vb1):
        zero_rim(ref, rows // 2, 1)

    edge = edge_mask(0, has_left, has_right)
    fine = Fine(source, weight, height)
    lane = lanes_iota((8, SUB, LANES))
    low = lane < 64

    def halves(own_value, beside_value, low):
        even = jnp.where(low, own_value, beside_value)
        odd = jnp.where(low, beside_value, own_value)
        return even, pltpu.roll(odd, 64, axis=odd.ndim - 1)

    first = first_columns((4, SUB, LANES))

    def assemble(dev, mine, side):
        tall = halves(mine(0)[32], side(0)[32], low[0])
        for r in range(TILE_ROWS):
            row = TILE_ROWS * dev + r
            upper = side(1)[pl.ds(4 * r, 4)]
            upper = jnp.where(first, pltpu.roll(upper, 96, axis=2), pltpu.roll(upper, 32, axis=2))
            beside = jnp.concatenate([side(0)[pl.ds(4 * r, 4)], upper], axis=0)
            both = halves(mine(r // 4)[pl.ds(8 * (r % 4), 8)], beside, low)
            for h in range(2):
                source[h, row] = both[h]
                height[h, row] = jnp.broadcast_to(tall[h][r:r + 1], (SUB, LANES))
                now = edge * jnp.where(
                    fine.ground(row, h), RELAX_WEIGHT / D_TERRAIN, RELAX_WEIGHT / D_AIR
                )
                weight[h, row] = now
                va0[h, row + 1] = now * both[h]

    for other in range(2):
        group = tiles[8 * other:8 * other + 8]
        for n, step in enumerate((0, -1, 1)):
            assemble(device(step, other), lambda part: group[n].at[part],
                     lambda part: group[3 + n].at[part])
        assemble(device(2, other), lambda part: group[6 + part].at[0],
                 lambda part: group[6 + part].at[1])
    saves = [
        pltpu.make_async_copy(source, source_out, sems.at[1]),
        pltpu.make_async_copy(weight, weight_out, sems.at[2]),
        pltpu.make_async_copy(height, height_out, sems.at[3]),
    ]
    for save in saves:
        save.start()
    fine.coarse_shift(rows, sh1)
    fine.relax(va0, vb0, 0, rows, 8)
    fine.relax(vb0, va0, 0, rows, 8)
    fine.relax(va0, vb0, 0, rows, 8)
    saves.append(pltpu.make_async_copy(interior(vb0, rows), u0, sems.at[0]))
    saves[-1].start()
    fine.restricted_defect(vb0, rows, b1)
    level = Coarse(b1, w1, sh1, rows // 2, 16)
    level.set_weight(edge_mask(1, has_left, has_right))
    level_1_down(level, va1, vb1, packed)
    pack_level_2(level.shift_pairs(), packed, rows // 16)
    u1[...] = vb1[pl.ds(1, rows // 2)]
    for save in saves:
        save.wait()


def middle_kernel(rows, s_ref, source_in, weight_in, height_in, u0, u1, b1, sh1, own, second, first,
                  u0_out, u1_out, b1_out, packed,
                  source, weight, height, va0, vb0, va1, vb1, w1, va2, vb2, b2, sh2, w2, sems):
    at = Place(s_ref)
    has_left, has_right = at.has_left, at.has_right
    copies = [
        pltpu.make_async_copy(u0, interior(va0, rows), sems.at[0]),
        pltpu.make_async_copy(source_in, source, sems.at[1]),
        pltpu.make_async_copy(weight_in, weight, sems.at[2]),
        pltpu.make_async_copy(height_in, height, sems.at[3]),
    ]
    for copy in copies:
        copy.start()
    for ref in (va1, vb1):
        zero_rim(ref, rows // 2, 1)
    e2 = coarse_part((own, first, second), (own, first, second), at, rows // 4,
                     (va2, vb2, b2, sh2, w2))
    level = Coarse(b1, w1, sh1, rows // 2, 16)
    level.set_weight(edge_mask(1, has_left, has_right))
    level_1_up(level, e2, rows // 4, u1, va1, vb1)
    for ref in (va0, vb0):
        zero_rim(ref, rows, 2)
    for copy in copies:
        copy.wait()
    fine = Fine(source, weight, height)
    add_to_fine(va1, va0, 0, rows // 2)
    for _ in range(SWEEPS):
        fine.relax(va0, vb0, 0, rows, 8)
        fine.relax(vb0, va0, 0, rows, 8)
    save = pltpu.make_async_copy(interior(va0, rows), u0_out, sems.at[0])
    save.start()
    fine.restricted_defect(va0, rows, b1_out)
    level = Coarse(b1_out, w1, sh1, rows // 2, 16)
    level_1_down(level, va1, vb1, packed)
    u1_out[...] = vb1[pl.ds(1, rows // 2)]
    save.wait()


def last_kernel(rows, s_ref, source_in, weight_in, u0, u1, b1, sh1,
                own, second, first, own_s, second_s, first_s,
                out, source, weight, va0, vb0, va1, vb1, w1, va2, vb2, b2, sh2, w2, sems):
    at = Place(s_ref)
    start, has_left, has_right, mine = at.start, at.has_left, at.has_right, at.mine
    window = pl.ds(start, WINDOW)
    copies = [
        pltpu.make_async_copy(u0.at[:, window], interior(va0, WINDOW), sems.at[0]),
        pltpu.make_async_copy(source_in.at[:, window], source, sems.at[1]),
        pltpu.make_async_copy(weight_in.at[:, window], weight, sems.at[2]),
    ]
    for copy in copies:
        copy.start()
    for ref in (va1, vb1):
        zero_rim(ref, rows // 2, 1)
    e2 = coarse_part((own, first, second), (own_s, first_s, second_s), at, rows // 4,
                     (va2, vb2, b2, sh2, w2))
    level = Coarse(b1, w1, sh1, rows // 2, 16)
    level.set_weight(edge_mask(1, has_left, has_right))
    level_1_up(level, e2, rows // 4, u1, va1, vb1)
    for ref in (va0, vb0):
        zero_rim(ref, WINDOW, 2)
    for copy in copies:
        copy.wait()
    fine = Fine(source, weight, None)
    add_to_fine(va1, va0, lax.div(start, 2), WINDOW // 2)
    src, dst = va0, vb0
    for k in range(SWEEPS):
        reach = SWEEPS - 1 - k
        count = TILE_ROWS + 2 * reach
        first = jnp.clip(mine - start - reach, 0, WINDOW - count)
        fine.relax(src, dst, first, count, count)
        src, dst = dst, src
    together = [
        matrix_of(lambda a, b, h=h: (a < 64) & (b == 2 * a + h)) for h in range(2)
    ]
    for r in range(TILE_ROWS):
        row = mine - start + r + 1
        value = 0.0
        for h in range(2):
            value = value + dot(src[h, row].reshape(8 * SUB, LANES), together[h])
        for zz in range(8):
            out[pl.ds(zz * TILE_ROWS + r, SUB, stride=8 * TILE_ROWS), :] = (
                value[SUB * zz:SUB * (zz + 1)]
            )


class Place:
    def __init__(self, s_ref):
        self.start, self.mine, self.chip, self.core = s_ref[0], s_ref[1], s_ref[2], s_ref[3]
        self.has_left, self.has_right, self.even = s_ref[4], s_ref[5], s_ref[6] == 1


def spec(space=pltpu.VMEM):
    return pl.BlockSpec(memory_space=space)


def params():
    return pltpu.CompilerParams(vmem_limit_bytes=VMEM_LIMIT)


def shape(*dims):
    return jax.ShapeDtypeStruct(dims + (SUB, LANES), F32)


def vmem(*dims):
    return pltpu.VMEM(dims + (SUB, LANES), F32)


def level_1_scratch(rows):
    return [vmem(rows // 2 + 2, 4), vmem(rows // 2 + 2, 4), vmem(rows // 2, 4)]


def level_2_scratch(rows):
    return [vmem(rows // 4 + 2, 2)] * 2 + [vmem(rows // 4, 2)] * 3


def per_device(right_side, terrain):
    gx, gy = lax.axis_size("gx"), lax.axis_size("gy")
    rows = TILE_ROWS * gx
    i, j = lax.axis_index("gx"), lax.axis_index("gy")
    mine, even = TILE_ROWS * i, 1 - lax.rem(j, 2)
    scalars = jnp.stack([
        jnp.clip(mine - 4, 0, rows - WINDOW), mine, lax.div(i, 2), lax.rem(i, 2),
        (j > 0).astype(jnp.int32), (j < gy - 1).astype(jnp.int32), even,
    ])

    def swaps(begin):
        pairs = [(k, k + 1) for k in range(begin, gy - 1, 2)]
        return pairs + [(b, a) for a, b in pairs]

    def exchange(first_out, second_out):
        first = lax.ppermute(first_out, "gy", swaps(1))
        second = lax.ppermute(second_out, "gy", swaps(0))
        return first, second

    smem, hbm = spec(pltpu.SMEM), spec(pl.ANY)
    flat = LAYERS * TILE_ROWS
    own, first_out, second_out = pl.pallas_call(
        pack_kernel,
        out_shape=(shape(2, 33), shape(33), shape(33)),
        in_specs=[smem] + [spec()] * 2, out_specs=(spec(),) * 3, name="pack",
    )(scalars, right_side.reshape(flat, LANES), terrain.reshape(flat, LANES))
    first, second = exchange(first_out, second_out)

    up = [(k, (k + 2) % gx) for k in range(gx)]
    down = [(k, (k - 2) % gx) for k in range(gx)]
    swap = [(k, k ^ 1) for k in range(gx)]

    def gather_near(tile):
        below = lax.ppermute(tile, "gx", up)
        above = lax.ppermute(tile, "gx", down)
        return below, above

    def swapped(*arrays):
        return tuple(lax.ppermute(x, "gx", swap) for x in arrays)

    own_near = gather_near(own)

    is_last = first_columns((1, 1, LANES)) != (even == 1)
    halo = jnp.stack([jnp.where(is_last, first, second), jnp.where(is_last, second, first)])
    halo_near = gather_near(halo)
    far = (
        lax.ppermute(jnp.stack([own_near[0][0], halo_near[0][0]]), "gx", up),
        lax.ppermute(jnp.stack([own_near[1][1], halo_near[1][1]]), "gx", down),
    )
    arrays = (own,) + own_near + (halo,) + halo_near + far
    tiles = arrays + swapped(*arrays)

    each = rows // 16
    level_0, level_1 = shape(2, rows, 8), shape(rows // 2, 4)
    fine_rows = [vmem(2, rows + 2, 8)] * 2
    u0, source, weight, height, u1, b1, sh1, packed = pl.pallas_call(
        lambda *refs: down_kernel(rows, *refs),
        out_shape=(level_0, level_0, level_0, shape(2, rows), level_1, level_1, level_1,
                   shape(2 * each, 2)),
        in_specs=[smem] + [spec()] * 16, out_specs=(hbm,) * 4 + (spec(),) * 4,
        scratch_shapes=[vmem(2, rows, 8), vmem(2, rows, 8), vmem(2, rows)]
        + fine_rows + level_1_scratch(rows) + [pltpu.SemaphoreType.DMA((4,))],
        compiler_params=params(), name="down",
    )(scalars, *tiles)

    first, second = exchange(packed, packed)
    u0, u1, b1, packed_2 = pl.pallas_call(
        lambda *refs: middle_kernel(rows, *refs),
        out_shape=(level_0, level_1, level_1, shape(each, 2)),
        in_specs=[smem] + [hbm] * 4 + [spec()] * 6, out_specs=(hbm,) + (spec(),) * 3,
        scratch_shapes=[vmem(2, rows, 8), vmem(2, rows, 8), vmem(2, rows)]
        + fine_rows + level_1_scratch(rows) + level_2_scratch(rows)
        + [pltpu.SemaphoreType.DMA((4,))],
        compiler_params=params(), name="middle",
    )(scalars, source, weight, height, u0, u1, b1, sh1, packed, second, first)

    first_2, second_2 = exchange(packed_2, packed_2)
    out = pl.pallas_call(
        lambda *refs: last_kernel(rows, *refs),
        out_shape=jax.ShapeDtypeStruct((flat, LANES), F32),
        in_specs=[smem] + [hbm] * 3 + [spec()] * 9, out_specs=spec(),
        scratch_shapes=[vmem(2, WINDOW, 8), vmem(2, WINDOW, 8)]
        + [vmem(2, WINDOW + 2, 8)] * 2 + level_1_scratch(rows) + level_2_scratch(rows)
        + [pltpu.SemaphoreType.DMA((3,))],
        compiler_params=params(), name="last",
    )(scalars, source, weight, u0, u1, b1, sh1,
      packed_2, second_2, first_2, packed, second, first)
    return out.reshape(LAYERS, TILE_ROWS, LANES)


def solution(mesh):
    in_specs = (P(None, "gx", "gy"), P(None, "gx", "gy"))
    out_specs = P(None, "gx", "gy")
    return jax.shard_map(
        per_device, mesh=mesh, in_specs=in_specs, out_specs=out_specs, check_vma=False
    )
```

```python
import jax
import jax.numpy as jnp
from jax import lax
from jax.experimental import pallas as pl
from jax.experimental.pallas import tpu as pltpu
from jax.sharding import PartitionSpec as P

SWEEPS = 4
COARSE_SWEEPS = 8
RELAX_WEIGHT = 0.8
TERRAIN_PENALTY = 0.05

F32 = jnp.float32
LANES = 128
SUB = 8
LAYERS = 64
TILE_ROWS = 8
WINDOW = 16
DOWN_VMEM = 48
OTHER_VMEM = 56

D_AIR = 6.0
D_TERRAIN = 6.0 + TERRAIN_PENALTY


def lanes_iota(shape):
    return lax.broadcasted_iota(jnp.int32, shape, len(shape) - 1)


def edge_mask(level, has_left, has_right):
    lane = lanes_iota((1, LANES))
    zero = jnp.zeros((1, LANES), F32)
    left = zero + has_left.astype(F32)
    right = zero + has_right.astype(F32)
    if level < 2:
        return jnp.where(lane < 64, 1.0, jnp.where(lane < 96, right, left))
    if level == 2:
        return jnp.where(
            lane < 32, 1.0, jnp.where(lane < 64, right, jnp.where(lane < 96, 0.0, left))
        )
    return jnp.where(
        lane < 16, 1.0, jnp.where(lane < 32, right, jnp.where(lane < 112, 0.0, left))
    )


def dot(values, matrix):
    return lax.dot_general(
        values, matrix, (((1,), (0,)), ((), ())),
        precision=lax.Precision.HIGHEST, preferred_element_type=F32,
    )


def matrix_of(rule, value=1.0):
    row = lax.broadcasted_iota(jnp.int32, (LANES, LANES), 0)
    col = lax.broadcasted_iota(jnp.int32, (LANES, LANES), 1)
    return jnp.where(rule(row, col), value, 0.0).astype(F32)


def layer_sum(v):
    count = v.shape[0]
    sub = lax.broadcasted_iota(jnp.int32, (1, SUB, LANES), 1)
    below = jnp.where(sub == 0, 0.0, pltpu.roll(v[count - 1:], 1, axis=1))
    above = jnp.where(sub == SUB - 1, 0.0, pltpu.roll(v[:1], SUB - 1, axis=1))
    if count == 1:
        return below + above
    return jnp.concatenate([below, v[:-1]], axis=0) + jnp.concatenate([v[1:], above], axis=0)


def column_sum(parts):
    if len(parts) == 1:
        v = parts[0]
        return [pltpu.roll(v, 1, axis=2) + pltpu.roll(v, LANES - 1, axis=2)]
    even, odd = parts
    return [odd + pltpu.roll(odd, 1, axis=2), even + pltpu.roll(even, LANES - 1, axis=2)]


def stencil_group(load, first, count, emit):
    before, centre = load(first - 1), load(first)
    for k in range(count):
        after = load(first + k + 1)
        sides = column_sum(centre)
        pairs = []
        for h, v in enumerate(centre):
            total = before[h] + after[h]
            pairs.append((v, total + layer_sum(v) + sides[h]))
        emit(first + k, pairs)
        before, centre = centre, after


def over_rows(start, rows, group, body):
    if isinstance(rows, int) and rows <= group:
        body(start, rows)
        return

    def step(i, carry):
        body(start + i * group, group)
        return carry

    lax.fori_loop(0, rows // group, step, 0)


class Fine:
    def __init__(self, source, weight, height):
        self.source, self.weight, self.height = source, weight, height

    @staticmethod
    def loader(src):
        return lambda row: [src[h, row + 1] for h in range(2)]

    def ground(self, row, h):
        layer = (
            8 * lax.broadcasted_iota(jnp.int32, (8, SUB, LANES), 1)
            + lax.broadcasted_iota(jnp.int32, (8, SUB, LANES), 0)
        ).astype(F32)
        return layer < self.height[h, row][None]

    def relax(self, src, dst, start, rows, group):
        def emit(row, pairs):
            for h, (v, total) in enumerate(pairs):
                total = total + self.source[h, row]
                dst[h, row + 1] = (1.0 - RELAX_WEIGHT) * v + self.weight[h, row] * total

        over_rows(start, rows, group,
                  lambda first, count: stencil_group(self.loader(src), first, count, emit))

    def restricted_defect(self, src, rows, out):
        load = self.loader(src)

        def body(first, count):
            sums = []

            def emit(row, pairs):
                total = 0.0
                for h, (v, near) in enumerate(pairs):
                    diagonal = jnp.where(self.ground(row, h), D_TERRAIN, D_AIR)
                    total = total + (self.source[h, row] + near - diagonal * v)
                sums.append(total)

            stencil_group(load, first, count, emit)
            for k in range(count // 2):
                both = sums[2 * k] + sums[2 * k + 1]
                for z in range(4):
                    out[lax.div(first, 2) + k, z] = 0.5 * (both[2 * z] + both[2 * z + 1])

        over_rows(0, rows, 8, body)

    def coarse_shift(self, rows, out):
        base = (
            8 * lax.broadcasted_iota(jnp.int32, (4, SUB, LANES), 1)
            + 2 * lax.broadcasted_iota(jnp.int32, (4, SUB, LANES), 0)
        ).astype(F32)

        def body(first, count):
            for k in range(count):
                total = 0.0
                for h in range(2):
                    for m in range(2):
                        height = self.height[h, 2 * (first + k) + m][None]
                        total = total + jnp.clip(height - base, 0.0, 2.0)
                out[first + k] = (0.5 * TERRAIN_PENALTY) * total

        over_rows(0, rows // 2, 4, body)


class Coarse:
    def __init__(self, source, weight, shift_now, rows, group):
        self.source, self.weight, self.shift_now = source, weight, shift_now
        self.rows, self.group = rows, group

    def set_weight(self, edge):
        def body(first, count):
            for k in range(count):
                self.weight[first + k] = edge * (RELAX_WEIGHT / (6.0 + self.shift_now[first + k]))

        over_rows(0, self.rows, self.group, body)

    def first(self, dst):
        def body(first, count):
            for k in range(count):
                dst[first + k + 1] = self.weight[first + k] * self.source[first + k]

        over_rows(0, self.rows, self.group, body)

    def relax(self, src, dst):
        def emit(row, pairs):
            v, total = pairs[0]
            total = total + self.source[row]
            dst[row + 1] = (1.0 - RELAX_WEIGHT) * v + self.weight[row] * total

        load = lambda row: [src[row + 1]]
        over_rows(0, self.rows, self.group,
                  lambda first, count: stencil_group(load, first, count, emit))

    def defect_pairs(self, src):
        sums = []

        def emit(row, pairs):
            v, total = pairs[0]
            sums.append(self.source[row] + total - (6.0 + self.shift_now[row]) * v)

        stencil_group(lambda row: [src[row + 1]], 0, self.rows, emit)
        return pair_up(sums)

    def shift_pairs(self):
        return pair_up([self.shift_now[row] for row in range(self.rows)])


def pair_up(rows):
    out = []
    for k in range(len(rows) // 2):
        both = rows[2 * k] + rows[2 * k + 1]
        out.append(jnp.stack([both[2 * z] + both[2 * z + 1] for z in range(both.shape[0] // 2)]))
    return out


def pack_level_2(pairs, out, offset):
    into = matrix_of(lambda a, b: (a < 64) & (b == lax.div(a, 2)), 0.5)
    count = len(pairs) // 4
    flat = jnp.stack(pairs).reshape(len(pairs) * 2 * SUB, LANES)
    lanes = dot(flat, into).reshape(4, count, 2, SUB, LANES)
    total = lanes[0]
    for g in range(1, 4):
        total = total + pltpu.roll(lanes[g], 32 * g, axis=3)
    out[pl.ds(offset, count)] = total


def unpack_level_2(own, first, second, even, offset, each, out):
    lane = lanes_iota((each, 2, SUB, LANES))
    held = [ref[pl.ds(offset, each)] for ref in (own, first, second)]
    left = jnp.where(even, held[1], held[2])
    right = jnp.where(even, held[2], held[1])
    for g in range(4):
        parts = []
        for value, place in ((held[0], 0), (right, 32), (left, 96)):
            amount = (place - 32 * g) % LANES
            parts.append(pltpu.roll(value, amount, axis=3) if amount else value)
        out[pl.ds(g * each, each)] = jnp.where(
            lane < 32, parts[0],
            jnp.where(lane < 64, parts[1], jnp.where(lane < 96, 0.0, parts[2])),
        )


def coarsest(source, diagonal, edge, rows):
    weight = edge * (RELAX_WEIGHT / diagonal)
    zero = jnp.zeros((1, SUB, LANES), F32)

    def body(i, v):
        total = jnp.concatenate([zero, v[:-1]], axis=0) + jnp.concatenate([v[1:], zero], axis=0)
        sub = lax.broadcasted_iota(jnp.int32, (rows, SUB, LANES), 1)
        total = total + jnp.where(sub == 0, 0.0, pltpu.roll(v, 1, axis=1))
        total = total + jnp.where(sub == SUB - 1, 0.0, pltpu.roll(v, SUB - 1, axis=1))
        total = total + column_sum([v])[0]
        return (1.0 - RELAX_WEIGHT) * v + weight * (total + source)

    v = weight * source
    for i in range(COARSE_SWEEPS - 1):
        v = body(i, v)
    return v


def zero_rim(ref, rows, halves):
    if halves == 2:
        zero = jnp.zeros((2,) + ref.shape[2:], F32)
        ref[:, 0] = zero
        ref[:, rows + 1] = zero
    else:
        zero = jnp.zeros(ref.shape[1:], F32)
        ref[0] = zero
        ref[rows + 1] = zero


def level_1_down(level, va, vb, packed):
    level.first(va)
    level.relax(va, vb)
    level.relax(vb, va)
    level.relax(va, vb)
    pack_level_2(level.defect_pairs(vb), packed, 0)


def coarse_part(tiles, shift_tiles, at, rows2, refs):
    va, vb, b2, sh2, w2 = refs
    has_left, has_right, even = at.has_left, at.has_right, at.even
    each = rows2 // 4
    unpack_level_2(*tiles, even, 0, each, b2)
    unpack_level_2(*shift_tiles, even, each, each, sh2)
    for ref in (va, vb):
        zero_rim(ref, rows2, 1)
    level = Coarse(b2, w2, sh2, rows2, rows2)
    level.set_weight(edge_mask(2, has_left, has_right))
    level.first(va)
    level.relax(va, vb)
    level.relax(vb, va)
    level.relax(va, vb)

    into = matrix_of(
        lambda a, b: b == jnp.where(a < 64, lax.div(a, 2), 64 + lax.div(a, 2)), 0.5
    )
    rows3 = rows2 // 2

    def to_level_3(pairs):
        flat = jnp.stack(pairs).reshape(rows3 * SUB, LANES)
        return dot(flat, into).reshape(rows3, SUB, LANES)

    shift_3 = to_level_3(level.shift_pairs())
    source_3 = to_level_3(level.defect_pairs(vb))
    e3 = coarsest(source_3, 6.0 + shift_3, edge_mask(3, has_left, has_right), rows3)
    out_of = matrix_of(
        lambda a, b: a == jnp.where(b < 64, lax.div(b, 2), 64 + lax.div(b, 2))
    )
    spread = dot(e3.reshape(rows3 * SUB, LANES), out_of).reshape(rows3, SUB, LANES)
    for row in range(rows2):
        vb[row + 1] = vb[row + 1] + spread[row // 2][None]
    for _ in range(SWEEPS // 2):
        level.relax(vb, va)
        level.relax(va, vb)
    return vb


def level_1_up(level, e2, rows2, u1, va, vb):
    out_of = matrix_of(
        lambda a, b: a == jnp.where(b < 96, lax.div(b, 2), 64 + lax.div(b, 2))
    )
    flat = e2[pl.ds(1, rows2)].reshape(rows2 * 2 * SUB, LANES)
    spread = dot(flat, out_of).reshape(rows2, 2, SUB, LANES)
    for row in range(2 * rows2):
        e = spread[row // 2]
        for z in range(4):
            va[row + 1, z] = u1[row, z] + e[z // 2]
    for _ in range(SWEEPS // 2):
        level.relax(va, vb)
        level.relax(vb, va)


def add_to_fine(e1, target, first_pair, pairs):
    def body(first, count):
        for k in range(count):
            e = e1[first_pair + first + k + 1]
            twice = jnp.stack([e[z // 2] for z in range(8)])
            for h in range(2):
                for m in range(2):
                    row = 2 * (first + k) + m + 1
                    target[h, row] = target[h, row] + twice

    over_rows(0, pairs, 4, body)


def interior(ref, rows):
    return ref.at[:, pl.ds(1, rows)]


def first_columns(shape):
    return lax.rem(lax.div(lanes_iota(shape), 32), 2) == 0


def pack_kernel(s_ref, right_side, terrain, own, first_out, second_out):
    even = Place(s_ref).even
    apart = matrix_of(lambda a, b: b == lax.div(a, 2) + 64 * lax.rem(a, 2))
    heights = terrain[pl.ds(0, TILE_ROWS), :]
    for z in range(1, 32):
        heights = heights + terrain[pl.ds(TILE_ROWS * z, TILE_ROWS), :]
    heights = dot(heights.astype(F32), apart)
    own[0, 32] = heights
    own[1, 32] = heights
    heights = pltpu.roll(heights, 64, axis=1)
    first_out[32] = heights
    second_out[32] = heights
    first = first_columns((4, SUB, LANES))
    for r in range(TILE_ROWS):
        layers = [
            right_side[pl.ds(zz * TILE_ROWS + r, SUB, stride=8 * TILE_ROWS), :] for zz in range(8)
        ]
        value = dot(jnp.concatenate(layers, axis=0), apart).reshape(8, SUB, LANES)
        own[r // 4, pl.ds(8 * (r % 4), 8)] = value
        value = pltpu.roll(value, 64, axis=2)
        low, high = value[:4], value[4:]
        to_left = jnp.where(first, low, pltpu.roll(high, 32, axis=2))
        to_right = jnp.where(first, pltpu.roll(high, 96, axis=2), low)
        first_out[pl.ds(4 * r, 4)] = jnp.where(even, to_left, to_right)
        second_out[pl.ds(4 * r, 4)] = jnp.where(even, to_right, to_left)


def down_kernel(rows, s_ref, *refs):
    at = Place(s_ref)
    tiles, refs = refs[:16], refs[16:]
    (u0, source_out, weight_out, height_out, u1, b1, sh1, packed,
     source, weight, height, va0, vb0, va1, vb1, w1, sems) = refs
    has_left, has_right = at.has_left, at.has_right
    chips = rows // (2 * TILE_ROWS)
    z, core = at.chip, at.core

    def device(step, other):
        return 2 * lax.rem(z + step + chips, chips) + (1 - core if other else core)

    for ref in (va0, vb0):
        zero_rim(ref, rows, 2)
    for ref in (va1, vb1):
        zero_rim(ref, rows // 2, 1)

    edge = edge_mask(0, has_left, has_right)
    fine = Fine(source, weight, height)
    lane = lanes_iota((8, SUB, LANES))
    low = lane < 64

    def halves(own_value, beside_value, low):
        even = jnp.where(low, own_value, beside_value)
        odd = jnp.where(low, beside_value, own_value)
        return even, pltpu.roll(odd, 64, axis=odd.ndim - 1)

    first = first_columns((4, SUB, LANES))

    def assemble(dev, mine, side):
        tall = halves(mine(0)[32], side(0)[32], low[0])
        for r in range(TILE_ROWS):
            row = TILE_ROWS * dev + r
            upper = side(1)[pl.ds(4 * r, 4)]
            upper = jnp.where(first, pltpu.roll(upper, 96, axis=2), pltpu.roll(upper, 32, axis=2))
            beside = jnp.concatenate([side(0)[pl.ds(4 * r, 4)], upper], axis=0)
            both = halves(mine(r // 4)[pl.ds(8 * (r % 4), 8)], beside, low)
            for h in range(2):
                source[h, row] = both[h]
                height[h, row] = jnp.broadcast_to(tall[h][r:r + 1], (SUB, LANES))
                now = edge * jnp.where(
                    fine.ground(row, h), RELAX_WEIGHT / D_TERRAIN, RELAX_WEIGHT / D_AIR
                )
                weight[h, row] = now
                va0[h, row + 1] = now * both[h]

    for other in range(2):
        group = tiles[8 * other:8 * other + 8]
        for n, step in enumerate((0, -1, 1)):
            assemble(device(step, other), lambda part: group[n].at[part],
                     lambda part: group[3 + n].at[part])
        assemble(device(2, other), lambda part: group[6 + part].at[0],
                 lambda part: group[6 + part].at[1])
    saves = [
        pltpu.make_async_copy(source, source_out, sems.at[1]),
        pltpu.make_async_copy(weight, weight_out, sems.at[2]),
        pltpu.make_async_copy(height, height_out, sems.at[3]),
    ]
    for save in saves:
        save.start()
    fine.coarse_shift(rows, sh1)
    fine.relax(va0, vb0, 0, rows, 8)
    fine.relax(vb0, va0, 0, rows, 8)
    fine.relax(va0, vb0, 0, rows, 8)
    saves.append(pltpu.make_async_copy(interior(vb0, rows), u0, sems.at[0]))
    saves[-1].start()
    fine.restricted_defect(vb0, rows, b1)
    level = Coarse(b1, w1, sh1, rows // 2, 16)
    level.set_weight(edge_mask(1, has_left, has_right))
    level_1_down(level, va1, vb1, packed)
    pack_level_2(level.shift_pairs(), packed, rows // 16)
    u1[...] = vb1[pl.ds(1, rows // 2)]
    for save in saves:
        save.wait()


def middle_kernel(rows, s_ref, source_in, weight_in, height_in, u0, u1, b1, sh1, own, second, first,
                  u0_out, u1_out, b1_out, packed,
                  source, weight, height, va0, vb0, va1, vb1, w1, va2, vb2, b2, sh2, w2, sems):
    at = Place(s_ref)
    has_left, has_right = at.has_left, at.has_right
    copies = [
        pltpu.make_async_copy(u0, interior(va0, rows), sems.at[0]),
        pltpu.make_async_copy(source_in, source, sems.at[1]),
        pltpu.make_async_copy(weight_in, weight, sems.at[2]),
        pltpu.make_async_copy(height_in, height, sems.at[3]),
    ]
    for copy in copies:
        copy.start()
    for ref in (va1, vb1):
        zero_rim(ref, rows // 2, 1)
    e2 = coarse_part((own, first, second), (own, first, second), at, rows // 4,
                     (va2, vb2, b2, sh2, w2))
    level = Coarse(b1, w1, sh1, rows // 2, 16)
    level.set_weight(edge_mask(1, has_left, has_right))
    level_1_up(level, e2, rows // 4, u1, va1, vb1)
    for ref in (va0, vb0):
        zero_rim(ref, rows, 2)
    for copy in copies:
        copy.wait()
    fine = Fine(source, weight, height)
    add_to_fine(va1, va0, 0, rows // 2)
    for _ in range(SWEEPS):
        fine.relax(va0, vb0, 0, rows, 8)
        fine.relax(vb0, va0, 0, rows, 8)
    save = pltpu.make_async_copy(interior(va0, rows), u0_out, sems.at[0])
    save.start()
    fine.restricted_defect(va0, rows, b1_out)
    level = Coarse(b1_out, w1, sh1, rows // 2, 16)
    level_1_down(level, va1, vb1, packed)
    u1_out[...] = vb1[pl.ds(1, rows // 2)]
    save.wait()


def last_kernel(rows, s_ref, source_in, weight_in, u0, u1, b1, sh1,
                own, second, first, own_s, second_s, first_s,
                out, source, weight, va0, vb0, va1, vb1, w1, va2, vb2, b2, sh2, w2, sems):
    at = Place(s_ref)
    start, has_left, has_right, mine = at.start, at.has_left, at.has_right, at.mine
    window = pl.ds(start, WINDOW)
    copies = [
        pltpu.make_async_copy(u0.at[:, window], interior(va0, WINDOW), sems.at[0]),
        pltpu.make_async_copy(source_in.at[:, window], source, sems.at[1]),
        pltpu.make_async_copy(weight_in.at[:, window], weight, sems.at[2]),
    ]
    for copy in copies:
        copy.start()
    for ref in (va1, vb1):
        zero_rim(ref, rows // 2, 1)
    e2 = coarse_part((own, first, second), (own_s, first_s, second_s), at, rows // 4,
                     (va2, vb2, b2, sh2, w2))
    level = Coarse(b1, w1, sh1, rows // 2, 16)
    level.set_weight(edge_mask(1, has_left, has_right))
    level_1_up(level, e2, rows // 4, u1, va1, vb1)
    for ref in (va0, vb0):
        zero_rim(ref, WINDOW, 2)
    for copy in copies:
        copy.wait()
    fine = Fine(source, weight, None)
    add_to_fine(va1, va0, lax.div(start, 2), WINDOW // 2)
    src, dst = va0, vb0
    for k in range(SWEEPS):
        reach = SWEEPS - 1 - k
        count = TILE_ROWS + 2 * reach
        first = jnp.clip(mine - start - reach, 0, WINDOW - count)
        fine.relax(src, dst, first, count, count)
        src, dst = dst, src
    together = [
        matrix_of(lambda a, b, h=h: (a < 64) & (b == 2 * a + h)) for h in range(2)
    ]
    for r in range(TILE_ROWS):
        row = mine - start + r + 1
        value = 0.0
        for h in range(2):
            value = value + dot(src[h, row].reshape(8 * SUB, LANES), together[h])
        for zz in range(8):
            out[pl.ds(zz * TILE_ROWS + r, SUB, stride=8 * TILE_ROWS), :] = (
                value[SUB * zz:SUB * (zz + 1)]
            )


class Place:
    def __init__(self, s_ref):
        self.start, self.mine, self.chip, self.core = s_ref[0], s_ref[1], s_ref[2], s_ref[3]
        self.has_left, self.has_right, self.even = s_ref[4], s_ref[5], s_ref[6] == 1


def spec(space=pltpu.VMEM):
    return pl.BlockSpec(memory_space=space)


def params(mebibytes):
    return pltpu.CompilerParams(vmem_limit_bytes=mebibytes * 1024 * 1024)


def shape(*dims):
    return jax.ShapeDtypeStruct(dims + (SUB, LANES), F32)


def vmem(*dims):
    return pltpu.VMEM(dims + (SUB, LANES), F32)


def level_1_scratch(rows):
    return [vmem(rows // 2 + 2, 4), vmem(rows // 2 + 2, 4), vmem(rows // 2, 4)]


def level_2_scratch(rows):
    return [vmem(rows // 4 + 2, 2)] * 2 + [vmem(rows // 4, 2)] * 3


def per_device(right_side, terrain):
    gx, gy = lax.axis_size("gx"), lax.axis_size("gy")
    rows = TILE_ROWS * gx
    i, j = lax.axis_index("gx"), lax.axis_index("gy")
    mine, even = TILE_ROWS * i, 1 - lax.rem(j, 2)
    scalars = jnp.stack([
        jnp.clip(mine - 4, 0, rows - WINDOW), mine, lax.div(i, 2), lax.rem(i, 2),
        (j > 0).astype(jnp.int32), (j < gy - 1).astype(jnp.int32), even,
    ])

    def swaps(begin):
        pairs = [(k, k + 1) for k in range(begin, gy - 1, 2)]
        return pairs + [(b, a) for a, b in pairs]

    def exchange(first_out, second_out):
        first = lax.ppermute(first_out, "gy", swaps(1))
        second = lax.ppermute(second_out, "gy", swaps(0))
        return first, second

    smem, hbm = spec(pltpu.SMEM), spec(pl.ANY)
    flat = LAYERS * TILE_ROWS
    own, first_out, second_out = pl.pallas_call(
        pack_kernel,
        out_shape=(shape(2, 33), shape(33), shape(33)),
        in_specs=[smem] + [spec()] * 2, out_specs=(spec(),) * 3, name="pack",
    )(scalars, right_side.reshape(flat, LANES), terrain.reshape(flat, LANES))
    first, second = exchange(first_out, second_out)

    up = [(k, (k + 2) % gx) for k in range(gx)]
    down = [(k, (k - 2) % gx) for k in range(gx)]
    swap = [(k, k ^ 1) for k in range(gx)]

    def gather_near(tile):
        below = lax.ppermute(tile, "gx", up)
        above = lax.ppermute(tile, "gx", down)
        return below, above

    def swapped(*arrays):
        return tuple(lax.ppermute(x, "gx", swap) for x in arrays)

    own_near = gather_near(own)

    is_last = first_columns((1, 1, LANES)) != (even == 1)
    halo = jnp.stack([jnp.where(is_last, first, second), jnp.where(is_last, second, first)])
    halo_near = gather_near(halo)
    far = (
        lax.ppermute(jnp.stack([own_near[0][0], halo_near[0][0]]), "gx", up),
        lax.ppermute(jnp.stack([own_near[1][1], halo_near[1][1]]), "gx", down),
    )
    arrays = (own,) + own_near + (halo,) + halo_near + far
    tiles = arrays + swapped(*arrays)

    each = rows // 16
    level_0, level_1 = shape(2, rows, 8), shape(rows // 2, 4)
    fine_rows = [vmem(2, rows + 2, 8)] * 2
    u0, source, weight, height, u1, b1, sh1, packed = pl.pallas_call(
        lambda *refs: down_kernel(rows, *refs),
        out_shape=(level_0, level_0, level_0, shape(2, rows), level_1, level_1, level_1,
                   shape(2 * each, 2)),
        in_specs=[smem] + [spec()] * 16, out_specs=(hbm,) * 4 + (spec(),) * 4,
        scratch_shapes=[vmem(2, rows, 8), vmem(2, rows, 8), vmem(2, rows)]
        + fine_rows + level_1_scratch(rows) + [pltpu.SemaphoreType.DMA((4,))],
        compiler_params=params(DOWN_VMEM), name="down",
    )(scalars, *tiles)

    first, second = exchange(packed, packed)
    u0, u1, b1, packed_2 = pl.pallas_call(
        lambda *refs: middle_kernel(rows, *refs),
        out_shape=(level_0, level_1, level_1, shape(each, 2)),
        in_specs=[smem] + [hbm] * 4 + [spec()] * 6, out_specs=(hbm,) + (spec(),) * 3,
        scratch_shapes=[vmem(2, rows, 8), vmem(2, rows, 8), vmem(2, rows)]
        + fine_rows + level_1_scratch(rows) + level_2_scratch(rows)
        + [pltpu.SemaphoreType.DMA((4,))],
        compiler_params=params(OTHER_VMEM), name="middle",
    )(scalars, source, weight, height, u0, u1, b1, sh1, packed, second, first)

    first_2, second_2 = exchange(packed_2, packed_2)
    out = pl.pallas_call(
        lambda *refs: last_kernel(rows, *refs),
        out_shape=jax.ShapeDtypeStruct((flat, LANES), F32),
        in_specs=[smem] + [hbm] * 3 + [spec()] * 9, out_specs=spec(),
        scratch_shapes=[vmem(2, WINDOW, 8), vmem(2, WINDOW, 8)]
        + [vmem(2, WINDOW + 2, 8)] * 2 + level_1_scratch(rows) + level_2_scratch(rows)
        + [pltpu.SemaphoreType.DMA((3,))],
        compiler_params=params(OTHER_VMEM), name="last",
    )(scalars, source, weight, u0, u1, b1, sh1,
      packed_2, second_2, first_2, packed, second, first)
    return out.reshape(LAYERS, TILE_ROWS, LANES)


def solution(mesh):
    in_specs = (P(None, "gx", "gy"), P(None, "gx", "gy"))
    out_specs = P(None, "gx", "gy")
    return jax.shard_map(
        per_device, mesh=mesh, in_specs=in_specs, out_specs=out_specs, check_vma=False
    )
```

```python
import jax
import jax.numpy as jnp
from jax import lax
from jax.experimental import pallas as pl
from jax.experimental.pallas import tpu as pltpu
from jax.sharding import PartitionSpec as P

SWEEPS = 4
COARSE_SWEEPS = 8
RELAX_WEIGHT = 0.8
TERRAIN_PENALTY = 0.05

F32 = jnp.float32
LANES = 128
SUB = 8
LAYERS = 64
TILE_ROWS = 8
WINDOW = 16
VMEM_LIMIT = 28 * 1024 * 1024

D_AIR = 6.0
D_TERRAIN = 6.0 + TERRAIN_PENALTY


def lanes_iota(shape):
    return lax.broadcasted_iota(jnp.int32, shape, len(shape) - 1)


def edge_mask(level, has_left, has_right):
    lane = lanes_iota((1, LANES))
    zero = jnp.zeros((1, LANES), F32)
    left = zero + has_left.astype(F32)
    right = zero + has_right.astype(F32)
    if level < 2:
        return jnp.where(lane < 64, 1.0, jnp.where(lane < 96, right, left))
    if level == 2:
        return jnp.where(
            lane < 32, 1.0, jnp.where(lane < 64, right, jnp.where(lane < 96, 0.0, left))
        )
    return jnp.where(
        lane < 16, 1.0, jnp.where(lane < 32, right, jnp.where(lane < 112, 0.0, left))
    )


def dot(values, matrix):
    return lax.dot_general(
        values, matrix, (((1,), (0,)), ((), ())),
        precision=lax.Precision.HIGHEST, preferred_element_type=F32,
    )


def matrix_of(rule, value=1.0):
    row = lax.broadcasted_iota(jnp.int32, (LANES, LANES), 0)
    col = lax.broadcasted_iota(jnp.int32, (LANES, LANES), 1)
    return jnp.where(rule(row, col), value, 0.0).astype(F32)


def layer_sum(v):
    count = v.shape[0]
    sub = lax.broadcasted_iota(jnp.int32, (1, SUB, LANES), 1)
    below = jnp.where(sub == 0, 0.0, pltpu.roll(v[count - 1:], 1, axis=1))
    above = jnp.where(sub == SUB - 1, 0.0, pltpu.roll(v[:1], SUB - 1, axis=1))
    if count == 1:
        return below + above
    return jnp.concatenate([below, v[:-1]], axis=0) + jnp.concatenate([v[1:], above], axis=0)


def column_sum(parts):
    if len(parts) == 1:
        v = parts[0]
        return [pltpu.roll(v, 1, axis=2) + pltpu.roll(v, LANES - 1, axis=2)]
    even, odd = parts
    return [odd + pltpu.roll(odd, 1, axis=2), even + pltpu.roll(even, LANES - 1, axis=2)]


def stencil_group(load, first, count, emit):
    before, centre = load(first - 1), load(first)
    for k in range(count):
        after = load(first + k + 1)
        sides = column_sum(centre)
        pairs = []
        for h, v in enumerate(centre):
            total = before[h] + after[h]
            pairs.append((v, total + layer_sum(v) + sides[h]))
        emit(first + k, pairs)
        before, centre = centre, after


def over_rows(start, rows, group, body):
    if isinstance(rows, int) and rows <= group:
        body(start, rows)
        return

    def step(i, carry):
        body(start + i * group, group)
        return carry

    lax.fori_loop(0, rows // group, step, 0)


class Fine:
    def __init__(self, source, weight, height):
        self.source, self.weight, self.height = source, weight, height

    @staticmethod
    def loader(src):
        return lambda row: [src[h, row + 1] for h in range(2)]

    def ground(self, row, h):
        layer = (
            8 * lax.broadcasted_iota(jnp.int32, (8, SUB, LANES), 1)
            + lax.broadcasted_iota(jnp.int32, (8, SUB, LANES), 0)
        ).astype(F32)
        return layer < self.height[h, row][None]

    def relax(self, src, dst, start, rows, group):
        def emit(row, pairs):
            for h, (v, total) in enumerate(pairs):
                total = total + self.source[h, row]
                dst[h, row + 1] = (1.0 - RELAX_WEIGHT) * v + self.weight[h, row] * total

        over_rows(start, rows, group,
                  lambda first, count: stencil_group(self.loader(src), first, count, emit))

    def restricted_defect(self, src, rows, out):
        load = self.loader(src)

        def body(first, count):
            sums = []

            def emit(row, pairs):
                total = 0.0
                for h, (v, near) in enumerate(pairs):
                    diagonal = jnp.where(self.ground(row, h), D_TERRAIN, D_AIR)
                    total = total + (self.source[h, row] + near - diagonal * v)
                sums.append(total)

            stencil_group(load, first, count, emit)
            for k in range(count // 2):
                both = sums[2 * k] + sums[2 * k + 1]
                for z in range(4):
                    out[lax.div(first, 2) + k, z] = 0.5 * (both[2 * z] + both[2 * z + 1])

        over_rows(0, rows, 8, body)

    def coarse_shift(self, rows, out):
        base = (
            8 * lax.broadcasted_iota(jnp.int32, (4, SUB, LANES), 1)
            + 2 * lax.broadcasted_iota(jnp.int32, (4, SUB, LANES), 0)
        ).astype(F32)

        def body(first, count):
            for k in range(count):
                total = 0.0
                for h in range(2):
                    for m in range(2):
                        height = self.height[h, 2 * (first + k) + m][None]
                        total = total + jnp.clip(height - base, 0.0, 2.0)
                out[first + k] = (0.5 * TERRAIN_PENALTY) * total

        over_rows(0, rows // 2, 4, body)


class Coarse:
    def __init__(self, source, weight, shift_now, rows, group):
        self.source, self.weight, self.shift_now = source, weight, shift_now
        self.rows, self.group = rows, group

    def set_weight(self, edge):
        def body(first, count):
            for k in range(count):
                self.weight[first + k] = edge * (RELAX_WEIGHT / (6.0 + self.shift_now[first + k]))

        over_rows(0, self.rows, self.group, body)

    def first(self, dst):
        def body(first, count):
            for k in range(count):
                dst[first + k + 1] = self.weight[first + k] * self.source[first + k]

        over_rows(0, self.rows, self.group, body)

    def relax(self, src, dst):
        def emit(row, pairs):
            v, total = pairs[0]
            total = total + self.source[row]
            dst[row + 1] = (1.0 - RELAX_WEIGHT) * v + self.weight[row] * total

        load = lambda row: [src[row + 1]]
        over_rows(0, self.rows, self.group,
                  lambda first, count: stencil_group(load, first, count, emit))

    def defect_pairs(self, src):
        sums = []

        def emit(row, pairs):
            v, total = pairs[0]
            sums.append(self.source[row] + total - (6.0 + self.shift_now[row]) * v)

        stencil_group(lambda row: [src[row + 1]], 0, self.rows, emit)
        return pair_up(sums)

    def shift_pairs(self):
        return pair_up([self.shift_now[row] for row in range(self.rows)])


def pair_up(rows):
    out = []
    for k in range(len(rows) // 2):
        both = rows[2 * k] + rows[2 * k + 1]
        out.append(jnp.stack([both[2 * z] + both[2 * z + 1] for z in range(both.shape[0] // 2)]))
    return out


def pack_level_2(pairs, out, offset):
    into = matrix_of(lambda a, b: (a < 64) & (b == lax.div(a, 2)), 0.5)
    count = len(pairs) // 4
    flat = jnp.stack(pairs).reshape(len(pairs) * 2 * SUB, LANES)
    lanes = dot(flat, into).reshape(4, count, 2, SUB, LANES)
    total = lanes[0]
    for g in range(1, 4):
        total = total + pltpu.roll(lanes[g], 32 * g, axis=3)
    out[pl.ds(offset, count)] = total


def unpack_level_2(own, first, second, even, offset, each, out):
    lane = lanes_iota((each, 2, SUB, LANES))
    held = [ref[pl.ds(offset, each)] for ref in (own, first, second)]
    left = jnp.where(even, held[1], held[2])
    right = jnp.where(even, held[2], held[1])
    for g in range(4):
        parts = []
        for value, place in ((held[0], 0), (right, 32), (left, 96)):
            amount = (place - 32 * g) % LANES
            parts.append(pltpu.roll(value, amount, axis=3) if amount else value)
        out[pl.ds(g * each, each)] = jnp.where(
            lane < 32, parts[0],
            jnp.where(lane < 64, parts[1], jnp.where(lane < 96, 0.0, parts[2])),
        )


def coarsest(source, diagonal, edge, rows):
    weight = edge * (RELAX_WEIGHT / diagonal)
    zero = jnp.zeros((1, SUB, LANES), F32)

    def body(i, v):
        total = jnp.concatenate([zero, v[:-1]], axis=0) + jnp.concatenate([v[1:], zero], axis=0)
        sub = lax.broadcasted_iota(jnp.int32, (rows, SUB, LANES), 1)
        total = total + jnp.where(sub == 0, 0.0, pltpu.roll(v, 1, axis=1))
        total = total + jnp.where(sub == SUB - 1, 0.0, pltpu.roll(v, SUB - 1, axis=1))
        total = total + column_sum([v])[0]
        return (1.0 - RELAX_WEIGHT) * v + weight * (total + source)

    v = weight * source
    for i in range(COARSE_SWEEPS - 1):
        v = body(i, v)
    return v


def zero_rim(ref, rows, halves):
    if halves == 2:
        zero = jnp.zeros((2,) + ref.shape[2:], F32)
        ref[:, 0] = zero
        ref[:, rows + 1] = zero
    else:
        zero = jnp.zeros(ref.shape[1:], F32)
        ref[0] = zero
        ref[rows + 1] = zero


def level_1_down(level, va, vb, packed):
    level.first(va)
    level.relax(va, vb)
    level.relax(vb, va)
    level.relax(va, vb)
    pack_level_2(level.defect_pairs(vb), packed, 0)


def coarse_part(tiles, shift_tiles, at, rows2, refs):
    va, vb, b2, sh2, w2 = refs
    has_left, has_right, even = at.has_left, at.has_right, at.even
    each = rows2 // 4
    unpack_level_2(*tiles, even, 0, each, b2)
    unpack_level_2(*shift_tiles, even, each, each, sh2)
    for ref in (va, vb):
        zero_rim(ref, rows2, 1)
    level = Coarse(b2, w2, sh2, rows2, rows2)
    level.set_weight(edge_mask(2, has_left, has_right))
    level.first(va)
    level.relax(va, vb)
    level.relax(vb, va)
    level.relax(va, vb)

    into = matrix_of(
        lambda a, b: b == jnp.where(a < 64, lax.div(a, 2), 64 + lax.div(a, 2)), 0.5
    )
    rows3 = rows2 // 2

    def to_level_3(pairs):
        flat = jnp.stack(pairs).reshape(rows3 * SUB, LANES)
        return dot(flat, into).reshape(rows3, SUB, LANES)

    shift_3 = to_level_3(level.shift_pairs())
    source_3 = to_level_3(level.defect_pairs(vb))
    e3 = coarsest(source_3, 6.0 + shift_3, edge_mask(3, has_left, has_right), rows3)
    out_of = matrix_of(
        lambda a, b: a == jnp.where(b < 64, lax.div(b, 2), 64 + lax.div(b, 2))
    )
    spread = dot(e3.reshape(rows3 * SUB, LANES), out_of).reshape(rows3, SUB, LANES)
    for row in range(rows2):
        vb[row + 1] = vb[row + 1] + spread[row // 2][None]
    for _ in range(SWEEPS // 2):
        level.relax(vb, va)
        level.relax(va, vb)
    return vb


def level_1_up(level, e2, rows2, u1, va, vb):
    out_of = matrix_of(
        lambda a, b: a == jnp.where(b < 96, lax.div(b, 2), 64 + lax.div(b, 2))
    )
    flat = e2[pl.ds(1, rows2)].reshape(rows2 * 2 * SUB, LANES)
    spread = dot(flat, out_of).reshape(rows2, 2, SUB, LANES)
    for row in range(2 * rows2):
        e = spread[row // 2]
        for z in range(4):
            va[row + 1, z] = u1[row, z] + e[z // 2]
    for _ in range(SWEEPS // 2):
        level.relax(va, vb)
        level.relax(vb, va)


def add_to_fine(e1, target, first_pair, pairs):
    def body(first, count):
        for k in range(count):
            e = e1[first_pair + first + k + 1]
            twice = jnp.stack([e[z // 2] for z in range(8)])
            for h in range(2):
                for m in range(2):
                    row = 2 * (first + k) + m + 1
                    target[h, row] = target[h, row] + twice

    over_rows(0, pairs, 4, body)


def interior(ref, rows):
    return ref.at[:, pl.ds(1, rows)]


def first_columns(shape):
    return lax.rem(lax.div(lanes_iota(shape), 32), 2) == 0


def pack_kernel(s_ref, right_side, terrain, own, first_out, second_out):
    even = Place(s_ref).even
    apart = matrix_of(lambda a, b: b == lax.div(a, 2) + 64 * lax.rem(a, 2))
    heights = terrain[pl.ds(0, TILE_ROWS), :]
    for z in range(1, 32):
        heights = heights + terrain[pl.ds(TILE_ROWS * z, TILE_ROWS), :]
    heights = dot(heights.astype(F32), apart)
    own[0, 32] = heights
    own[1, 32] = heights
    heights = pltpu.roll(heights, 64, axis=1)
    first_out[32] = heights
    second_out[32] = heights
    first = first_columns((4, SUB, LANES))
    for r in range(TILE_ROWS):
        layers = [
            right_side[pl.ds(zz * TILE_ROWS + r, SUB, stride=8 * TILE_ROWS), :] for zz in range(8)
        ]
        value = dot(jnp.concatenate(layers, axis=0), apart).reshape(8, SUB, LANES)
        own[r // 4, pl.ds(8 * (r % 4), 8)] = value
        value = pltpu.roll(value, 64, axis=2)
        low, high = value[:4], value[4:]
        to_left = jnp.where(first, low, pltpu.roll(high, 32, axis=2))
        to_right = jnp.where(first, pltpu.roll(high, 96, axis=2), low)
        first_out[pl.ds(4 * r, 4)] = jnp.where(even, to_left, to_right)
        second_out[pl.ds(4 * r, 4)] = jnp.where(even, to_right, to_left)


def down_kernel(rows, s_ref, *refs):
    at = Place(s_ref)
    tiles, refs = refs[:16], refs[16:]
    (u0, source_out, weight_out, height_out, u1, b1, sh1, packed,
     source, weight, height, va0, vb0, va1, vb1, w1, sems) = refs
    has_left, has_right = at.has_left, at.has_right
    chips = rows // (2 * TILE_ROWS)
    z, core = at.chip, at.core

    def device(step, other):
        return 2 * lax.rem(z + step + chips, chips) + (1 - core if other else core)

    for ref in (va0, vb0):
        zero_rim(ref, rows, 2)
    for ref in (va1, vb1):
        zero_rim(ref, rows // 2, 1)

    edge = edge_mask(0, has_left, has_right)
    fine = Fine(source, weight, height)
    lane = lanes_iota((8, SUB, LANES))
    low = lane < 64

    def halves(own_value, beside_value, low):
        even = jnp.where(low, own_value, beside_value)
        odd = jnp.where(low, beside_value, own_value)
        return even, pltpu.roll(odd, 64, axis=odd.ndim - 1)

    first = first_columns((4, SUB, LANES))

    def assemble(dev, mine, side):
        tall = halves(mine(0)[32], side(0)[32], low[0])
        for r in range(TILE_ROWS):
            row = TILE_ROWS * dev + r
            upper = side(1)[pl.ds(4 * r, 4)]
            upper = jnp.where(first, pltpu.roll(upper, 96, axis=2), pltpu.roll(upper, 32, axis=2))
            beside = jnp.concatenate([side(0)[pl.ds(4 * r, 4)], upper], axis=0)
            both = halves(mine(r // 4)[pl.ds(8 * (r % 4), 8)], beside, low)
            for h in range(2):
                source[h, row] = both[h]
                height[h, row] = jnp.broadcast_to(tall[h][r:r + 1], (SUB, LANES))
                now = edge * jnp.where(
                    fine.ground(row, h), RELAX_WEIGHT / D_TERRAIN, RELAX_WEIGHT / D_AIR
                )
                weight[h, row] = now
                va0[h, row + 1] = now * both[h]

    for other in range(2):
        group = tiles[8 * other:8 * other + 8]
        for n, step in enumerate((0, -1, 1)):
            assemble(device(step, other), lambda part: group[n].at[part],
                     lambda part: group[3 + n].at[part])
        assemble(device(2, other), lambda part: group[6 + part].at[0],
                 lambda part: group[6 + part].at[1])
    saves = [
        pltpu.make_async_copy(source, source_out, sems.at[1]),
        pltpu.make_async_copy(weight, weight_out, sems.at[2]),
        pltpu.make_async_copy(height, height_out, sems.at[3]),
    ]
    for save in saves:
        save.start()
    fine.coarse_shift(rows, sh1)
    fine.relax(va0, vb0, 0, rows, 8)
    fine.relax(vb0, va0, 0, rows, 8)
    fine.relax(va0, vb0, 0, rows, 8)
    saves.append(pltpu.make_async_copy(interior(vb0, rows), u0, sems.at[0]))
    saves[-1].start()
    fine.restricted_defect(vb0, rows, b1)
    level = Coarse(b1, w1, sh1, rows // 2, 16)
    level.set_weight(edge_mask(1, has_left, has_right))
    level_1_down(level, va1, vb1, packed)
    pack_level_2(level.shift_pairs(), packed, rows // 16)
    u1[...] = vb1[pl.ds(1, rows // 2)]
    for save in saves:
        save.wait()


def middle_kernel(rows, s_ref, source_in, weight_in, height_in, u0, u1, b1, sh1, own, second, first,
                  u0_out, u1_out, b1_out, packed,
                  source, weight, height, va0, vb0, va1, vb1, w1, va2, vb2, b2, sh2, w2, sems):
    at = Place(s_ref)
    has_left, has_right = at.has_left, at.has_right
    copies = [
        pltpu.make_async_copy(u0, interior(va0, rows), sems.at[0]),
        pltpu.make_async_copy(source_in, source, sems.at[1]),
        pltpu.make_async_copy(weight_in, weight, sems.at[2]),
        pltpu.make_async_copy(height_in, height, sems.at[3]),
    ]
    for copy in copies:
        copy.start()
    for ref in (va1, vb1):
        zero_rim(ref, rows // 2, 1)
    e2 = coarse_part((own, first, second), (own, first, second), at, rows // 4,
                     (va2, vb2, b2, sh2, w2))
    level = Coarse(b1, w1, sh1, rows // 2, 16)
    level.set_weight(edge_mask(1, has_left, has_right))
    level_1_up(level, e2, rows // 4, u1, va1, vb1)
    for ref in (va0, vb0):
        zero_rim(ref, rows, 2)
    for copy in copies:
        copy.wait()
    fine = Fine(source, weight, height)
    add_to_fine(va1, va0, 0, rows // 2)
    for _ in range(SWEEPS):
        fine.relax(va0, vb0, 0, rows, 8)
        fine.relax(vb0, va0, 0, rows, 8)
    save = pltpu.make_async_copy(interior(va0, rows), u0_out, sems.at[0])
    save.start()
    fine.restricted_defect(va0, rows, b1_out)
    level = Coarse(b1_out, w1, sh1, rows // 2, 16)
    level_1_down(level, va1, vb1, packed)
    u1_out[...] = vb1[pl.ds(1, rows // 2)]
    save.wait()


def last_kernel(rows, s_ref, source_in, weight_in, u0, u1, b1, sh1,
                own, second, first, own_s, second_s, first_s,
                out, source, weight, va0, vb0, va1, vb1, w1, va2, vb2, b2, sh2, w2, sems):
    at = Place(s_ref)
    start, has_left, has_right, mine = at.start, at.has_left, at.has_right, at.mine
    window = pl.ds(start, WINDOW)
    copies = [
        pltpu.make_async_copy(u0.at[:, window], interior(va0, WINDOW), sems.at[0]),
        pltpu.make_async_copy(source_in.at[:, window], source, sems.at[1]),
        pltpu.make_async_copy(weight_in.at[:, window], weight, sems.at[2]),
    ]
    for copy in copies:
        copy.start()
    for ref in (va1, vb1):
        zero_rim(ref, rows // 2, 1)
    e2 = coarse_part((own, first, second), (own_s, first_s, second_s), at, rows // 4,
                     (va2, vb2, b2, sh2, w2))
    level = Coarse(b1, w1, sh1, rows // 2, 16)
    level.set_weight(edge_mask(1, has_left, has_right))
    level_1_up(level, e2, rows // 4, u1, va1, vb1)
    for ref in (va0, vb0):
        zero_rim(ref, WINDOW, 2)
    for copy in copies:
        copy.wait()
    fine = Fine(source, weight, None)
    add_to_fine(va1, va0, lax.div(start, 2), WINDOW // 2)
    src, dst = va0, vb0
    for k in range(SWEEPS):
        reach = SWEEPS - 1 - k
        count = TILE_ROWS + 2 * reach
        first = jnp.clip(mine - start - reach, 0, WINDOW - count)
        fine.relax(src, dst, first, count, count)
        src, dst = dst, src
    together = [
        matrix_of(lambda a, b, h=h: (a < 64) & (b == 2 * a + h)) for h in range(2)
    ]
    for r in range(TILE_ROWS):
        row = mine - start + r + 1
        value = 0.0
        for h in range(2):
            value = value + dot(src[h, row].reshape(8 * SUB, LANES), together[h])
        for zz in range(8):
            out[pl.ds(zz * TILE_ROWS + r, SUB, stride=8 * TILE_ROWS), :] = (
                value[SUB * zz:SUB * (zz + 1)]
            )


class Place:
    def __init__(self, s_ref):
        self.start, self.mine, self.chip, self.core = s_ref[0], s_ref[1], s_ref[2], s_ref[3]
        self.has_left, self.has_right, self.even = s_ref[4], s_ref[5], s_ref[6] == 1


def spec(space=pltpu.VMEM):
    return pl.BlockSpec(memory_space=space)


def params():
    return pltpu.CompilerParams(vmem_limit_bytes=VMEM_LIMIT)


def shape(*dims):
    return jax.ShapeDtypeStruct(dims + (SUB, LANES), F32)


def vmem(*dims):
    return pltpu.VMEM(dims + (SUB, LANES), F32)


def level_1_scratch(rows):
    return [vmem(rows // 2 + 2, 4), vmem(rows // 2 + 2, 4), vmem(rows // 2, 4)]


def level_2_scratch(rows):
    return [vmem(rows // 4 + 2, 2)] * 2 + [vmem(rows // 4, 2)] * 3


def per_device(right_side, terrain):
    gx, gy = lax.axis_size("gx"), lax.axis_size("gy")
    rows = TILE_ROWS * gx
    i, j = lax.axis_index("gx"), lax.axis_index("gy")
    mine, even = TILE_ROWS * i, 1 - lax.rem(j, 2)
    scalars = jnp.stack([
        jnp.clip(mine - 4, 0, rows - WINDOW), mine, lax.div(i, 2), lax.rem(i, 2),
        (j > 0).astype(jnp.int32), (j < gy - 1).astype(jnp.int32), even,
    ])

    def swaps(begin):
        pairs = [(k, k + 1) for k in range(begin, gy - 1, 2)]
        return pairs + [(b, a) for a, b in pairs]

    def exchange(first_out, second_out):
        first = lax.ppermute(first_out, "gy", swaps(1))
        second = lax.ppermute(second_out, "gy", swaps(0))
        return first, second

    smem, hbm = spec(pltpu.SMEM), spec(pl.ANY)
    flat = LAYERS * TILE_ROWS
    own, first_out, second_out = pl.pallas_call(
        pack_kernel,
        out_shape=(shape(2, 33), shape(33), shape(33)),
        in_specs=[smem] + [spec()] * 2, out_specs=(spec(),) * 3, name="pack",
    )(scalars, right_side.reshape(flat, LANES), terrain.reshape(flat, LANES))
    first, second = exchange(first_out, second_out)

    up = [(k, (k + 2) % gx) for k in range(gx)]
    down = [(k, (k - 2) % gx) for k in range(gx)]
    swap = [(k, k ^ 1) for k in range(gx)]

    def gather_near(tile):
        below = lax.ppermute(tile, "gx", up)
        above = lax.ppermute(tile, "gx", down)
        return below, above

    def swapped(*arrays):
        return tuple(lax.ppermute(x, "gx", swap) for x in arrays)

    own_near = gather_near(own)

    is_last = first_columns((1, 1, LANES)) != (even == 1)
    halo = jnp.stack([jnp.where(is_last, first, second), jnp.where(is_last, second, first)])
    halo_near = gather_near(halo)
    far = (
        lax.ppermute(jnp.stack([own_near[0][0], halo_near[0][0]]), "gx", up),
        lax.ppermute(jnp.stack([own_near[1][1], halo_near[1][1]]), "gx", down),
    )
    arrays = (own,) + own_near + (halo,) + halo_near + far
    tiles = arrays + swapped(*arrays)

    each = rows // 16
    level_0, level_1 = shape(2, rows, 8), shape(rows // 2, 4)
    fine_rows = [vmem(2, rows + 2, 8)] * 2
    u0, source, weight, height, u1, b1, sh1, packed = pl.pallas_call(
        lambda *refs: down_kernel(rows, *refs),
        out_shape=(level_0, level_0, level_0, shape(2, rows), level_1, level_1, level_1,
                   shape(2 * each, 2)),
        in_specs=[smem] + [spec()] * 16, out_specs=(hbm,) * 4 + (spec(),) * 4,
        scratch_shapes=[vmem(2, rows, 8), vmem(2, rows, 8), vmem(2, rows)]
        + fine_rows + level_1_scratch(rows) + [pltpu.SemaphoreType.DMA((4,))],
        compiler_params=params(), name="down",
    )(scalars, *tiles)

    first, second = exchange(packed, packed)
    u0, u1, b1, packed_2 = pl.pallas_call(
        lambda *refs: middle_kernel(rows, *refs),
        out_shape=(level_0, level_1, level_1, shape(each, 2)),
        in_specs=[smem] + [hbm] * 4 + [spec()] * 6, out_specs=(hbm,) + (spec(),) * 3,
        scratch_shapes=[vmem(2, rows, 8), vmem(2, rows, 8), vmem(2, rows)]
        + fine_rows + level_1_scratch(rows) + level_2_scratch(rows)
        + [pltpu.SemaphoreType.DMA((4,))],
        compiler_params=params(), name="middle",
    )(scalars, source, weight, height, u0, u1, b1, sh1, packed, second, first)

    first_2, second_2 = exchange(packed_2, packed_2)
    out = pl.pallas_call(
        lambda *refs: last_kernel(rows, *refs),
        out_shape=jax.ShapeDtypeStruct((flat, LANES), F32),
        in_specs=[smem] + [hbm] * 3 + [spec()] * 9, out_specs=spec(),
        scratch_shapes=[vmem(2, WINDOW, 8), vmem(2, WINDOW, 8)]
        + [vmem(2, WINDOW + 2, 8)] * 2 + level_1_scratch(rows) + level_2_scratch(rows)
        + [pltpu.SemaphoreType.DMA((3,))],
        compiler_params=params(), name="last",
    )(scalars, source, weight, u0, u1, b1, sh1,
      packed_2, second_2, first_2, packed, second, first)
    return out.reshape(LAYERS, TILE_ROWS, LANES)


def solution(mesh):
    in_specs = (P(None, "gx", "gy"), P(None, "gx", "gy"))
    out_specs = P(None, "gx", "gy")
    return jax.shard_map(
        per_device, mesh=mesh, in_specs=in_specs, out_specs=out_specs, check_vma=False
    )
```
